32 devices in a mesh: fsdp: 8 (over z, x), tp: 4 (over y, core).
Axes of the slice: x: 2, y: 2, z: 4, core: 2. Of those that a mesh axis runs over, the one named last changes fastest.
Arguments:
- residual_in: bfloat16 [16384, 1024], P(('fsdp', 'tp')), may hold values from -6 to 6
- out_cotangent: bfloat16 [16384, 1024], P(('fsdp', 'tp')), may hold values from -6 to 6
- expert_index: int32 [16384, 1], P(('fsdp', 'tp')), may hold values from 0 to 15; in each aligned block of 512 rows (0 to 511, 512 to 1023, ...) at most 64 rows name the same one
- document_index: int32 [8, 2048], P('fsdp', 'tp'), may hold values from 0 to 3, never falling along the last dimension, each value on 1 to 1024 neighbouring positions
- piece_starts: int32 [8, 2], P('fsdp'), may hold values from 0 to 1792, as said below
- first_norm_gain: float32 [1024], replicated, may hold values from 0.5 to 1.5
- first_norm_shift: float32 [1024], replicated, may hold values from -0.6 to 0.6
- input_weight: bfloat16 [1024, 3, 1024], P('fsdp', None, 'tp'), may hold values from -0.1875 to 0.1875
- input_bias: bfloat16 [2, 16, 64], P(None, 'tp', 'fsdp'), may hold values from -0.59765625 to 0.59765625
- output_weight: bfloat16 [1024, 1024], P('tp', 'fsdp'), may hold values from -0.5 to 0.5
- output_bias: float32 [1024], replicated, may hold values from -0.6 to 0.6
- second_norm_gain: float32 [1024], replicated, may hold values from 0.5 to 1.5
- second_norm_shift: float32 [1024], replicated, may hold values from -0.6 to 0.6
- expert_up: bfloat16 [16, 1024, 4096], P('fsdp', None, 'tp'), may hold values from -0.1875 to 0.1875
- expert_up_bias: float32 [16, 4096], P('fsdp', 'tp'), may hold values from -0.6 to 0.6
- expert_down: bfloat16 [16, 4096, 1024], P('fsdp', 'tp'), may hold values from -0.125 to 0.125
- expert_down_bias: float32 [16, 1024], P('fsdp'), may hold values from -2.4 to 2.4
Outputs:
- block_output: bfloat16 [16384, 1024], P(('fsdp', 'tp'))
- back_residual: float32 [16384, 1024], P(('fsdp', 'tp'))
- back_first_gain: float32 [1024], replicated
- back_first_shift: float32 [1024], replicated
- back_input_weight: float32 [1024, 3, 1024], P('fsdp', None, 'tp')
- back_input_bias: float32 [2, 16, 64], P(None, 'tp', 'fsdp')
- back_output_weight: float32 [1024, 1024], P('tp', 'fsdp')
- back_output_bias: float32 [1024], replicated
- back_second_gain: float32 [1024], replicated
- back_second_shift: float32 [1024], replicated
- back_expert_up: float32 [16, 1024, 4096], P('fsdp', None, 'tp')
- back_expert_up_bias: float32 [16, 4096], P('fsdp', 'tp')
- back_expert_down: float32 [16, 4096, 1024], P('fsdp', 'tp')
- back_expert_down_bias: float32 [16, 1024], P('fsdp')
The draws below stay inside these ranges and needn't reach their ends.
Inputs may be any that keep to these rules, and one draw needn't show every extreme that they name: `expert_index`: among the tokens of one device no expert is named by more than 64 tokens, a bound that some block reaches. `document_index`: document numbers never fall along a sequence; a document has 1 to 1024 positions. `piece_starts`: piece p of a sequence starts within positions p * (1024) to (p + 1) * 1024 - 256, so pieces never meet.
All inputs are finite; a program needn't handle non-finite values.
Results may differ from the reference program's by a relative error of at most 0.02.
Values may be sent and summed in bfloat16 or wider, within the bound.
No kernel may reach another device: no remote copies, remote signals or barrier semaphores. Data moves between devices by JAX's collectives and lax.ppermute only.
A program may use at most 256 MiB of HBM per device.

```python
import math
import jax
import jax.numpy as jnp
import numpy as np
from jax import lax

D = 1024
HEADS = 16
HEAD_DIM = 64
FF = 4096
TOK_DEV = 512
PIECE = 256
PIECES = 2
DOCS = 4
EXPERTS = 16
SEQ_LEN = 2048
SEQS = 8
TOKENS = 16384
CAP = 64
SLOTS = 2048


def draw_piece_starts(key, part):
    region = SEQ_LEN // PIECES
    offsets = jax.random.randint(jax.random.fold_in(key, 11), (SEQS, PIECES), 0, region - PIECE + 1)
    base = jnp.arange(PIECES, dtype=jnp.int32) * region
    starts = base[None, :] + offsets
    late_row = jax.random.randint(jax.random.fold_in(key, 12), (), 0, SEQS)
    early_row = jax.random.randint(jax.random.fold_in(key, 13), (), 0, SEQS)
    row_index = jnp.arange(SEQS, dtype=jnp.int32)[:, None]
    column_index = jnp.arange(PIECES, dtype=jnp.int32)[None, :]
    starts = jnp.where((row_index == late_row) & (column_index == PIECES - 1), SEQ_LEN - PIECE, starts)
    starts = jnp.where((row_index == early_row) & (column_index == 0), 0, starts)
    return starts.astype(jnp.int32)


def block_scale(key, extent, pieces, least, high):
    level = 1.0
    for position, parts in pieces:
        draws = jax.random.uniform(jax.random.fold_in(jax.random.fold_in(key, 6), position), (parts,), jnp.float32, least / len(pieces), high / len(pieces))
        level = level * jnp.repeat(jnp.exp(draws), extent[position] // parts).reshape((-1,) + (1,) * (len(extent) - 1 - position))
    return level


def profile(amount, total, bound, slope):
    weights = [(1 << 20) // math.isqrt(standing ** slope) + 1 for standing in range(2, amount + 1)]
    rest, given = total - bound - (amount - 1), [1] * (amount - 1)
    while rest > 0:
        candidates = [i for i in range(amount - 1) if given[i] < bound]
        mass, budget = sum([weights[i] for i in candidates]), rest
        for i in candidates:
            addition = min(bound - given[i], max(1, budget * weights[i] // mass), rest)
            given[i] = given[i] + addition
            rest = rest - addition
    return np.array([bound] + given)


def ragged_sizes(key, amount, total, most, lean):
    if amount == 2:
        one = jax.random.randint(key, (), max(1, total - most), min(most, total - 1) + 1)
        return jnp.stack([one, total - one])
    tallies = jnp.asarray(profile(amount, total, most, lean), jnp.int32)
    twos = (amount - 1) // 2
    donor, receiver = tallies[1:1 + 2 * twos:2], tallies[2:2 + 2 * twos:2]
    room = jnp.minimum(donor - 1, most - receiver)
    moved = jax.random.randint(jax.random.fold_in(key, 1), (twos,), 0, 1 << 20) % (room + 1)
    tallies = tallies.at[1:1 + 2 * twos:2].set(donor - moved).at[2:2 + 2 * twos:2].set(receiver + moved)
    return tallies[jax.random.permutation(jax.random.fold_in(key, 2), amount)]


def routed_block(rng, own, number, rows, count, top, bound, slope):
    order = jax.random.permutation(rng, count)
    crowded, ordinary = portions_of(count, rows * top, bound, slope, True), portions_of(count, rows * top, bound, slope, False)
    places = jnp.arange(count)

    def named(sizes, offset_by):
        used = int((sizes > 0).sum())
        fixed = max(1, used // 4)
        passed = fixed + (places - fixed + offset_by * (used - fixed)) % max(1, count - fixed)
        return jnp.zeros((count,), jnp.int32).at[order[jnp.where(places < fixed, places, passed)]].set(jnp.asarray(sizes, jnp.int32))

    sizes = jnp.where(number % 4 == 0, named(crowded, number // 4), named(ordinary, number - number // 4 - 1))
    mixed = jax.random.permutation(jax.random.fold_in(own, 3), count)
    donor, sink = mixed[0:count // 2 * 2:2], mixed[1:count // 2 * 2:2]
    slack = jnp.minimum(sizes[donor] - 1, bound - sizes[sink]) // 2
    slack = jnp.where((donor == order[0]) | (sink == order[0]) | (sizes[sink] == 0), 0, jnp.maximum(slack, 0))
    passed = jax.random.randint(jax.random.fold_in(own, 4), (count // 2,), 0, 1 << 20) % (slack + 1)
    sizes = sizes.at[donor].add(-passed).at[sink].add(passed)
    items = jnp.searchsorted(jnp.cumsum(sizes), jnp.arange(rows * top), side="right").astype(jnp.int32)
    grid = items.reshape(top, rows).T
    grid = grid[jax.random.permutation(jax.random.fold_in(own, 1), rows)]
    offset_by = jax.random.randint(jax.random.fold_in(own, 2), (rows, 1), 0, top)
    return jnp.take_along_axis(grid, (jnp.arange(top)[None, :] + offset_by) % top, axis=1)


def portions_of(amount, total, bound, lean, full):
    weights = [(1 << 20) // math.isqrt(rank ** lean) + 1 for rank in range(1, amount + 1)]
    largest = bound if full else min(bound, max(-(-total // amount), total * weights[0] // sum(weights)))
    least = 1 if total - largest >= amount - 1 else 0
    given, surplus = [largest] + [least] * (amount - 1), total - largest - least * (amount - 1)
    while surplus > 0:
        free = [i for i in range(1, amount) if given[i] < largest] or [i for i in range(1, amount) if given[i] < bound]
        whole, budget = sum([weights[i] for i in free]), surplus
        for i in free:
            addition = min(bound - given[i], max(1, budget * weights[i] // whole), surplus)
            given[i] = given[i] + addition
            surplus = surplus - addition
    return np.array(given)


def bell_draw(own_key, extent, width, limit, cuts=(), held_as=jnp.bfloat16):
    array = width * jax.random.normal(own_key, extent, jnp.float32)
    if cuts:
        array = array * block_scale(own_key, extent, cuts, -0.22, 0.18)
    return jnp.clip(array, -limit, limit).astype(held_as)


def setup_inputs(seed: int = 0) -> dict:
    seeds = jax.random.split(jax.random.key(seed), 18)
    residual_in = bell_draw(seeds[0], (TOKENS, D), 1.0, 6.0, ((0, 32),))
    out_cotangent = bell_draw(seeds[1], (TOKENS, D), 1.0, 6.0, ((0, 32),))
    expert_index_keys = jax.random.split(jax.random.fold_in(seeds[2], 1), TOKENS // TOK_DEV)
    expert_index_turns = jax.random.permutation(jax.random.fold_in(seeds[2], 3), TOKENS // TOK_DEV)
    expert_index = jax.vmap(lambda own, number: routed_block(jax.random.fold_in(seeds[2], 2), own, number, TOK_DEV, EXPERTS, 1, CAP, 2))(expert_index_keys, expert_index_turns).reshape((TOKENS, 1))
    document_index = jax.vmap(lambda own: jnp.searchsorted(jnp.cumsum(ragged_sizes(own, DOCS, SEQ_LEN, SEQ_LEN // 2, 2)), jnp.arange(SEQ_LEN), side="right"))(jax.random.split(seeds[3], SEQS)).reshape((SEQS, SEQ_LEN)).astype(jnp.int32)
    piece_starts = draw_piece_starts(jax.random.fold_in(seeds[17], 71), 0)
    first_norm_gain = jnp.clip(1.0 + 0.1 * jax.random.normal(seeds[5], (D,), jnp.float32), 0.5, 1.5)
    first_norm_shift = bell_draw(seeds[6], (D,), 0.1, 0.6, (), jnp.float32)
    input_weight = bell_draw(seeds[7], (D, 3, D), D ** -0.5, 0.1875, ((0, 8), (2, 4)))
    input_bias = bell_draw(seeds[8], (2, HEADS, HEAD_DIM), 0.1, 0.59765625, ((1, 4), (2, 8)))
    output_weight = bell_draw(seeds[9], (D, D), (D // 8) ** -0.5, 0.5, ((0, 4), (1, 8)))
    output_bias = bell_draw(seeds[10], (D,), 0.1, 0.6, (), jnp.float32)
    second_norm_gain = jnp.clip(1.0 + 0.1 * jax.random.normal(seeds[11], (D,), jnp.float32), 0.5, 1.5)
    second_norm_shift = bell_draw(seeds[12], (D,), 0.1, 0.6, (), jnp.float32)
    expert_up = bell_draw(seeds[13], (EXPERTS, D, FF), D ** -0.5, 0.1875, ((0, 8), (2, 4)))
    expert_up_bias = bell_draw(seeds[14], (EXPERTS, FF), 0.1, 0.6, ((0, 8), (1, 4)), jnp.float32)
    expert_down = bell_draw(seeds[15], (EXPERTS, FF, D), (FF // 2) ** -0.5, 0.125, ((0, 8), (1, 4)))
    expert_down_bias = bell_draw(seeds[16], (EXPERTS, D), 0.4, 2.4, ((0, 8),), jnp.float32)
    return {"residual_in": residual_in, "out_cotangent": out_cotangent, "expert_index": expert_index, "document_index": document_index, "piece_starts": piece_starts, "first_norm_gain": first_norm_gain, "first_norm_shift": first_norm_shift, "input_weight": input_weight, "input_bias": input_bias, "output_weight": output_weight, "output_bias": output_bias, "second_norm_gain": second_norm_gain, "second_norm_shift": second_norm_shift, "expert_up": expert_up, "expert_up_bias": expert_up_bias, "expert_down": expert_down, "expert_down_bias": expert_down_bias}


@jax.custom_vjp
def low(v):
    return lax.optimization_barrier(v.astype(jnp.bfloat16)).astype(jnp.float32)

@jax.custom_vjp
def low_back(v):
    return v

def low_keep(v):
    return (low(v), None)

def low_pass(kept, grad):
    return (grad,)

def back_keep(v):
    return (v, None)

def back_low(kept, grad):
    return (low(grad),)
low.defvjp(low_keep, low_pass)
low_back.defvjp(back_keep, back_low)
HIGH = lax.Precision.HIGHEST
EPSILON = 1e-05

def layer_norm(values, gain, shift):
    center = lax.optimization_barrier(jnp.mean(values, axis=-1, keepdims=True))
    centered = values - center
    inverse = lax.rsqrt(lax.optimization_barrier(jnp.mean(centered * centered, axis=-1, keepdims=True)) + EPSILON)
    return centered * inverse * gain + shift

def attend_sequence(queries, keys, values, docs, starts):
    places = jnp.arange(SEQ_LEN, dtype=jnp.int32)
    starts = starts.astype(jnp.int32)
    inside = (places[None, :] >= starts[:, None]) & (places[None, :] < starts[:, None] + PIECE)
    numbers = jnp.arange(1, PIECES + 1, dtype=jnp.int32)[:, None]
    labels = lax.optimization_barrier(jnp.max(jnp.where(inside, numbers, jnp.zeros_like(numbers)), axis=0)).astype(jnp.int32)
    same_doc = docs[:, None] == docs[None, :]
    causal = places[None, :] <= places[:, None]
    same_piece = (labels[:, None] == labels[None, :]) & (labels[:, None] > 0)
    allowed = same_doc & (causal | same_piece)
    scores = jnp.einsum('qhc,khc->hqk', queries, keys, precision=HIGH)
    scores = low_back(scores)
    scores = jnp.where(allowed[None], scores, -1e+30)
    probs = low(jax.nn.softmax(scores, axis=-1))
    return jnp.einsum('hqk,khc->qhc', probs, values, precision=HIGH)

def attend_item(item):
    return jax.checkpoint(attend_sequence)(item[0], item[1], item[2], item[3], item[4])

def expert_rows(rows_in, upper, upper_bias, lower, lower_bias):
    pre = low_back(jnp.dot(rows_in, upper, precision=HIGH) + upper_bias)
    act = low(jax.nn.gelu(pre, approximate=True))
    return low(jnp.dot(act, lower, precision=HIGH) + lower_bias)

def expert_item(item):
    return jax.checkpoint(expert_rows)(item[0], item[1], item[2], item[3], item[4])

def forward(residual, first_gain, first_shift, in_weight, in_bias, out_weight, out_bias, second_gain, second_shift, upper, upper_bias, lower, lower_bias, docs, starts, table, token_slot):
    first_normed = low(layer_norm(residual, first_gain, first_shift))
    projected = jnp.einsum('td,djc->tjc', first_normed, in_weight, precision=HIGH)
    bias_flat = in_bias.reshape(2, D)
    queries = low_back(low((projected[:, 0] + bias_flat[0]) * 0.125))
    keys = low_back(low(projected[:, 1]))
    values = low_back(low(projected[:, 2] + bias_flat[1]))
    shaped = (SEQS, SEQ_LEN, HEADS, HEAD_DIM)
    context = lax.map(attend_item, (queries.reshape(shaped), keys.reshape(shaped), values.reshape(shaped), docs, starts))
    context = low_back(low(context.reshape(TOKENS, D)))
    attention = low_back(jnp.dot(context, out_weight, precision=HIGH))
    mixed = residual + attention + out_bias
    second_normed = low(layer_norm(mixed, second_gain, second_shift))
    padded = jnp.concatenate([second_normed, jnp.zeros((1, D), second_normed.dtype)], axis=0)
    grouped = low_back(padded[table].reshape(EXPERTS, SLOTS, D))
    results = lax.map(expert_item, (grouped, upper, upper_bias, lower, lower_bias))
    chosen = results.reshape(EXPERTS * SLOTS, D)[token_slot]
    return mixed + chosen

def reference(residual_in, out_cotangent, expert_index, document_index, piece_starts, first_norm_gain, first_norm_shift, input_weight, input_bias, output_weight, output_bias, second_norm_gain, second_norm_shift, expert_up, expert_up_bias, expert_down, expert_down_bias):
    choice_ids = expert_index[:, 0].astype(jnp.int32)
    order = jnp.argsort(choice_ids, stable=True).astype(jnp.int32)
    matches = (choice_ids[:, None] == jnp.arange(EXPERTS, dtype=jnp.int32)[None, :]).astype(jnp.int32)
    counts = lax.optimization_barrier(jnp.sum(matches, axis=0)).astype(jnp.int32)
    begins = (jnp.cumsum(counts).astype(jnp.int32) - counts).astype(jnp.int32)
    sorted_ids = choice_ids[order]
    rank = (jnp.arange(TOKENS, dtype=jnp.int32) - begins[sorted_ids]).astype(jnp.int32)
    slots = (sorted_ids * SLOTS + rank).astype(jnp.int32)
    table = jnp.full((EXPERTS * SLOTS,), TOKENS, jnp.int32).at[slots].set(order)
    token_slot = jnp.zeros((TOKENS,), jnp.int32).at[order].set(slots)
    floats = (residual_in.astype(jnp.float32), first_norm_gain.astype(jnp.float32), first_norm_shift.astype(jnp.float32), input_weight.astype(jnp.float32), input_bias.astype(jnp.float32), output_weight.astype(jnp.float32), output_bias.astype(jnp.float32), second_norm_gain.astype(jnp.float32), second_norm_shift.astype(jnp.float32), expert_up.astype(jnp.float32), expert_up_bias.astype(jnp.float32), expert_down.astype(jnp.float32), expert_down_bias.astype(jnp.float32))
    docs = document_index.astype(jnp.int32)
    starts = piece_starts.astype(jnp.int32)

    def closed(*inputs):
        return forward(*inputs, docs, starts, table, token_slot)
    result, pullback = jax.vjp(closed, *floats)
    grads = pullback(out_cotangent.astype(jnp.float32))
    return (result.astype(jnp.bfloat16), grads[0], grads[1], grads[2], grads[3], grads[4], grads[5], grads[6], grads[7], grads[8], grads[9], grads[10], grads[11], grads[12])
```

```python
import functools

import jax
import jax.numpy as jnp
from jax import lax
from jax.experimental import pallas as pl
from jax.experimental.pallas import tpu as pltpu
from jax.sharding import PartitionSpec as P

f32 = jnp.float32
bf16 = jnp.bfloat16
HEAD_DIM = 64
EXP_DEV = 2
PIECE = 256
BLOCK_Q = 512
BLOCK_K = 256


EPSILON = 1e-05
MASKED = -1e30


def smooth_gelu(values):
    return jax.nn.gelu(values, approximate=True)


def layer_norm(values, gain, shift):
    center = jnp.mean(values, axis=-1, keepdims=True)
    centered = values - center
    inverse = lax.rsqrt(jnp.mean(centered * centered, axis=-1, keepdims=True) + EPSILON)
    unit = centered * inverse
    return (unit * gain + shift, unit, inverse)


def norm_back(incoming, unit, inverse, gain):
    scaled = incoming * gain
    return inverse * (
        scaled
        - jnp.mean(scaled, axis=-1, keepdims=True)
        - unit * jnp.mean(scaled * unit, axis=-1, keepdims=True)
    )


def half_rows(x, h):
    rows = lax.broadcasted_iota(jnp.int32, x.shape, 0)
    keep = (rows < 64) if h == 0 else (rows >= 64)
    return jnp.where(keep, x, jnp.zeros_like(x))

def half_lanes(x, h):
    lanes = lax.broadcasted_iota(jnp.int32, x.shape, 1)
    keep = (lanes < 64) if h == 0 else (lanes >= 64)
    return jnp.where(keep, x, jnp.zeros_like(x))

def attend_kernel(bk, lo_ref, hi_ref, q_ref, k_ref, v_ref, a_ref, b_ref, o_ref, lse_ref, vt, ):
    i = pl.program_id(1)
    bq = q_ref.shape[0]
    @pl.when(i == 0)
    def _():
        vt[...] = v_ref[...].T
    qt = q_ref[...].T
    qz = [half_rows(qt, h) for h in (0, 1)]
    a = a_ref[...]; b = b_ref[...]
    def body(kb, carry):
        base = pl.multiple_of(kb * bk, bk)
        kblk = k_ref[pl.ds(base, bk), :]
        j = base + lax.broadcasted_iota(jnp.int32, (bk, bq), 0)
        mask = (j >= a) & (j <= b)
        out = []
        for h in (0, 1):
            m, l, acc = carry[h]
            s = jnp.dot(kblk, qz[h], preferred_element_type=f32)
            s = jnp.where(mask, s, MASKED)
            mn = jnp.maximum(m, jnp.max(s, axis=0, keepdims=True))
            p = jnp.exp(s - mn)
            al = jnp.exp(m - mn)
            l = al * l + jnp.sum(p, axis=0, keepdims=True)
            acc = acc * al + jnp.dot(vt[pl.ds(64 * h, 64), pl.ds(base, bk)], p.astype(bf16), preferred_element_type=f32)
            out.append((mn, l, acc))
        return tuple(out)
    init = tuple((jnp.full((1, bq), MASKED, f32), jnp.zeros((1, bq), f32), jnp.zeros((64, bq), f32)) for _ in (0, 1))
    res = lax.fori_loop(lo_ref[i], hi_ref[i], body, init)
    ot = jnp.concatenate([acc / l for m, l, acc in res], axis=0)
    o_ref[...] = ot.T.astype(bf16)
    lse_ref[...] = jnp.concatenate([m + jnp.log(l) for m, l, acc in res] + [jnp.zeros((6, bq), f32)], axis=0)

def attention_fwd(q, k, v, a, b, lo, hi, bq, bk):
    S, W = q.shape
    n = S // bq
    return pl.pallas_call(
        functools.partial(attend_kernel, bk),
        grid_spec=pltpu.PrefetchScalarGridSpec(
            num_scalar_prefetch=2, grid=(W // 128, n),
            in_specs=[pl.BlockSpec((bq, 128), lambda p, i, *_: (i, p)),
                      pl.BlockSpec((S, 128), lambda p, i, *_: (0, p)),
                      pl.BlockSpec((S, 128), lambda p, i, *_: (0, p)),
                      pl.BlockSpec((1, bq), lambda p, i, *_: (0, i)),
                      pl.BlockSpec((1, bq), lambda p, i, *_: (0, i))],
            out_specs=[pl.BlockSpec((bq, 128), lambda p, i, *_: (i, p)),
                       pl.BlockSpec((8, bq), lambda p, i, *_: (p, i))],
            scratch_shapes=[pltpu.VMEM((128, S), bf16)]),
        out_shape=[jax.ShapeDtypeStruct((S, W), bf16), jax.ShapeDtypeStruct((W // 16, S), f32)],
        compiler_params=pltpu.CompilerParams(vmem_limit_bytes=40 << 20),
    )(lo, hi, q, k, v, a, b)

def attend_back_kernel(bk, lo_ref, hi_ref, q_ref, k_ref, v_ref, do_ref, o_ref, lse_ref, a_ref, b_ref, dq_ref, dk_ref, dv_ref, kt, dk_acc, dv_acc):
    i = pl.program_id(1)
    bq = q_ref.shape[0]
    @pl.when(i == 0)
    def _():
        kt[...] = k_ref[...].T
        dk_acc[...] = jnp.zeros_like(dk_acc)
        dv_acc[...] = jnp.zeros_like(dv_acc)
    q = q_ref[...]; do = do_ref[...]
    qt = q.T; dot_ = do.T
    qz = [half_rows(qt, h) for h in (0, 1)]
    dz = [half_rows(dot_, h) for h in (0, 1)]
    qcat = jnp.concatenate([half_lanes(q, 0), half_lanes(q, 1)], axis=0)
    dcat = jnp.concatenate([half_lanes(do, 0), half_lanes(do, 1)], axis=0)
    prod = (do.astype(f32) * o_ref[...].astype(f32)).T
    delta = [jnp.sum(prod[:64], axis=0, keepdims=True), jnp.sum(prod[64:], axis=0, keepdims=True)]
    lse = [lse_ref[0:1, :], lse_ref[1:2, :]]
    a = a_ref[...]; b = b_ref[...]
    def body(kb, carry):
        base = pl.multiple_of(kb * bk, bk)
        kblk = k_ref[pl.ds(base, bk), :]
        vblk = v_ref[pl.ds(base, bk), :]
        j = base + lax.broadcasted_iota(jnp.int32, (bk, bq), 0)
        mask = (j >= a) & (j <= b)
        ps, dss, out = [], [], []
        for h in (0, 1):
            s = jnp.dot(kblk, qz[h], preferred_element_type=f32)
            p = jnp.exp(jnp.where(mask, s - lse[h], MASKED))
            dp = jnp.dot(vblk, dz[h], preferred_element_type=f32)
            ds = (p * (dp - delta[h])).astype(bf16)
            ps.append(p.astype(bf16)); dss.append(ds)
            out.append(carry[h] + jnp.dot(kt[pl.ds(64 * h, 64), pl.ds(base, bk)], ds, preferred_element_type=f32))
        dv_acc[pl.ds(base, bk), :] += jnp.dot(jnp.concatenate(ps, axis=1), dcat, preferred_element_type=f32)
        dk_acc[pl.ds(base, bk), :] += jnp.dot(jnp.concatenate(dss, axis=1), qcat, preferred_element_type=f32)
        return tuple(out)
    init = tuple(jnp.zeros((64, bq), f32) for _ in (0, 1))
    dqt = lax.fori_loop(lo_ref[i], hi_ref[i], body, init)
    dq_ref[...] = (jnp.concatenate(dqt, axis=0).T * 0.125).astype(bf16)
    @pl.when(i == pl.num_programs(1) - 1)
    def _():
        dk_ref[...] = dk_acc[...].astype(bf16)
        dv_ref[...] = dv_acc[...].astype(bf16)

def attention_bwd(q, k, v, do, o, lse, a, b, lo, hi, bq, bk):
    S, W = q.shape
    n = S // bq
    qs = pl.BlockSpec((bq, 128), lambda p, i, *_: (i, p))
    ks = pl.BlockSpec((S, 128), lambda p, i, *_: (0, p))
    rs = pl.BlockSpec((1, bq), lambda p, i, *_: (0, i))
    return pl.pallas_call(
        functools.partial(attend_back_kernel, bk),
        grid_spec=pltpu.PrefetchScalarGridSpec(
            num_scalar_prefetch=2, grid=(W // 128, n),
            in_specs=[qs, ks, ks, qs, qs, pl.BlockSpec((8, bq), lambda p, i, *_: (p, i)), rs, rs],
            out_specs=[qs, ks, ks],
            scratch_shapes=[pltpu.VMEM((128, S), bf16), pltpu.VMEM((S, 128), f32), pltpu.VMEM((S, 128), f32)]),
        out_shape=[jax.ShapeDtypeStruct((S, W), bf16)] * 3,
        compiler_params=pltpu.CompilerParams(vmem_limit_bytes=40 << 20),
    )(lo, hi, q, k, v, do, o, lse, a, b)

def intervals(docs, starts, piece):
    S = docs.shape[0]
    pos = jnp.arange(S, dtype=jnp.int32)
    first = jnp.sum((docs[None, :] < docs[:, None]).astype(jnp.int32), axis=1)
    last = jnp.sum((docs[None, :] <= docs[:, None]).astype(jnp.int32), axis=1) - 1
    inside = (pos[None, :] >= starts[:, None]) & (pos[None, :] < starts[:, None] + piece)
    piece_last = jnp.max(jnp.where(inside, starts[:, None] + piece - 1, -1), axis=0)
    end = jnp.maximum(pos, jnp.minimum(piece_last, last))
    return first, end
def ranges(first, end, bq, bk):
    lo = first[::bq] // bk
    hi = jnp.max(end.reshape(-1, bq), axis=1) // bk + 1
    return lo, hi


def expert_forward(rows_in, upper, upper_bias, lower):
    pre = (
        jnp.einsum("secd,edf->secf", rows_in, upper, preferred_element_type=jnp.float32)
        + upper_bias[None, :, None, :]
    )
    act = smooth_gelu(pre).astype(jnp.bfloat16)
    partial_out = jnp.einsum("secf,efd->secd", act, lower, preferred_element_type=jnp.float32)
    return (pre, act, partial_out)


def expert_backward(rows_in, cotangent_rows, pre, act, upper, lower):
    lower_back = jnp.einsum(
        "secf,secd->efd", act, cotangent_rows, preferred_element_type=jnp.float32
    )
    lower_bias_back = jnp.sum(cotangent_rows, axis=(0, 2), dtype=jnp.float32)
    act_back = jnp.einsum(
        "secd,efd->secf", cotangent_rows, lower, preferred_element_type=jnp.float32
    )
    unused, gelu_pull = jax.vjp(smooth_gelu, pre)
    pre_back = gelu_pull(act_back)[0].astype(jnp.bfloat16)
    upper_back = jnp.einsum("secd,secf->edf", rows_in, pre_back, preferred_element_type=jnp.float32)
    upper_bias_back = jnp.sum(pre_back, axis=(0, 2), dtype=jnp.float32)
    rows_back_part = jnp.einsum(
        "secf,edf->secd", pre_back, upper, preferred_element_type=jnp.float32
    )
    return (upper_back, upper_bias_back, lower_back, lower_bias_back, rows_back_part)


def sum_shares(partial_out):
    return lax.psum_scatter(
        partial_out.astype(jnp.bfloat16), "tp", scatter_dimension=2, tiled=True
    ).astype(jnp.float32)


def send_home(block):
    return lax.all_to_all(block, "fsdp", split_axis=0, concat_axis=0, tiled=True)


def local(
    residual_in,
    out_cotangent,
    expert_index,
    document_index,
    piece_starts,
    first_norm_gain,
    first_norm_shift,
    input_weight,
    input_bias,
    output_weight,
    output_bias,
    second_norm_gain,
    second_norm_shift,
    expert_up,
    expert_up_bias,
    expert_down,
    expert_down_bias,
):
    width = residual_in.shape[1]
    fsdp_size = lax.axis_size("fsdp")
    residual = residual_in.astype(jnp.float32)
    first_normed, first_unit, first_inverse = layer_norm(
        residual, first_norm_gain, first_norm_shift
    )
    whole_normed, whole_docs = (
        lax.all_gather(first_normed.astype(jnp.bfloat16), "tp", axis=0, tiled=True),
        lax.all_gather(document_index, "tp", axis=1, tiled=True),
    )
    input_full, output_full, bias_full = (
        lax.all_gather(input_weight, "fsdp", axis=0, tiled=True),
        lax.all_gather(output_weight, "fsdp", axis=1, tiled=True),
        lax.all_gather(input_bias, "fsdp", axis=2, tiled=True),
    )
    docs = whole_docs[0]
    length = whole_normed.shape[0]
    local_width = input_full.shape[2]
    local_heads = local_width // HEAD_DIM
    projected = jnp.einsum(
        "sd,djc->sjc", whole_normed, input_full, preferred_element_type=jnp.float32
    )
    bias_flat = bias_full.reshape(2, local_width).astype(jnp.float32)
    queries = ((projected[:, 0] + bias_flat[0]) * 0.125).astype(bf16)
    keys = projected[:, 1].astype(bf16)
    values = (projected[:, 2] + bias_flat[1]).astype(bf16)
    first, end = intervals(docs, piece_starts[0], PIECE)
    lows, highs = ranges(first, end, BLOCK_Q, BLOCK_K)
    context, log_totals = attention_fwd(
        queries, keys, values, first[None], end[None], lows, highs, BLOCK_Q, BLOCK_K
    )
    attention_part = jnp.dot(context, output_full, preferred_element_type=jnp.float32)
    attention_rows = lax.psum_scatter(
        attention_part.astype(jnp.bfloat16), "tp", scatter_dimension=0, tiled=True
    ).astype(jnp.float32)
    mixed = residual + attention_rows + output_bias
    second_normed, second_unit, second_inverse = layer_norm(
        mixed, second_norm_gain, second_norm_shift
    )
    choice_ids = expert_index[:, 0]
    rows_here = choice_ids.shape[0]
    experts_all = EXP_DEV * fsdp_size
    capacity = 2 * rows_here // experts_all
    row_order = jnp.arange(rows_here, dtype=jnp.int32)
    earlier = (choice_ids[:, None] == choice_ids[None, :]) & (
        row_order[None, :] < row_order[:, None]
    )
    rank = jnp.sum(earlier.astype(jnp.int32), axis=1)
    flat_slot = choice_ids * capacity + rank
    slot_rows = (
        jnp.zeros((experts_all * capacity, width), jnp.bfloat16)
        .at[flat_slot]
        .set(second_normed.astype(jnp.bfloat16))
    )
    slot_cotangent = (
        jnp.zeros((experts_all * capacity, width), jnp.bfloat16).at[flat_slot].set(out_cotangent)
    )
    sent_rows = slot_rows.reshape(fsdp_size, EXP_DEV, capacity, width)
    sent_cotangent = slot_cotangent.reshape(fsdp_size, EXP_DEV, capacity, width)
    got_rows, got_cotangent = (
        lax.all_to_all(sent_rows, "fsdp", split_axis=0, concat_axis=0, tiled=True),
        lax.all_to_all(sent_cotangent, "fsdp", split_axis=0, concat_axis=0, tiled=True),
    )
    rows_in, cotangent_rows = (
        lax.all_gather(got_rows, "tp", axis=2, tiled=True),
        lax.all_gather(got_cotangent, "tp", axis=2, tiled=True),
    )
    pre, act, partial_out = expert_forward(rows_in, expert_up, expert_up_bias, expert_down)
    summed = sum_shares(partial_out)
    returned = send_home((summed + expert_down_bias[None, :, None, :]).astype(jnp.bfloat16))
    upper_back, upper_bias_back, lower_back, lower_bias_back, rows_back_part = expert_backward(
        rows_in, cotangent_rows, pre, act, expert_up, expert_down
    )
    rows_back = send_home(sum_shares(rows_back_part).astype(jnp.bfloat16))
    expert_result = returned.reshape(-1, width)[flat_slot].astype(jnp.float32)
    block_output = (mixed + expert_result).astype(jnp.bfloat16)
    second_back = rows_back.reshape(-1, width)[flat_slot].astype(jnp.float32)
    cotangent = out_cotangent.astype(jnp.float32)
    mixed_back = cotangent + norm_back(second_back, second_unit, second_inverse, second_norm_gain)
    second_gain_back = jnp.sum(second_back * second_unit, axis=0)
    second_shift_back = jnp.sum(second_back, axis=0)
    output_bias_back = jnp.sum(mixed_back, axis=0)
    whole_back = lax.all_gather(mixed_back.astype(jnp.bfloat16), "tp", axis=0, tiled=True)
    output_weight_back = jnp.einsum(
        "sc,sd->cd", context, whole_back, preferred_element_type=jnp.float32
    )
    context_back = jnp.einsum(
        "sd,cd->sc", whole_back, output_full, preferred_element_type=jnp.float32
    )
    query_low, key_low, value_low = attention_bwd(
        queries, keys, values, context_back.astype(bf16), context, log_totals,
        first[None], end[None], lows, highs, BLOCK_Q, BLOCK_K,
    )
    projected_back = jnp.stack([query_low, key_low, value_low], axis=1)
    input_weight_back = jnp.einsum(
        "sd,sjc->djc", whole_normed, projected_back, preferred_element_type=jnp.float32
    )
    input_bias_back = jnp.stack(
        [
            jnp.sum(projected_back[:, 0], axis=0, dtype=jnp.float32),
            jnp.sum(projected_back[:, 2], axis=0, dtype=jnp.float32),
        ]
    ).reshape(2, local_heads, HEAD_DIM)
    first_back_part = jnp.einsum(
        "sjc,djc->sd", projected_back, input_full, preferred_element_type=jnp.float32
    )
    first_back = lax.psum_scatter(
        first_back_part.astype(jnp.bfloat16), "tp", scatter_dimension=0, tiled=True
    ).astype(jnp.float32)
    residual_back = mixed_back + norm_back(first_back, first_unit, first_inverse, first_norm_gain)
    first_gain_back = jnp.sum(first_back * first_unit, axis=0)
    first_shift_back = jnp.sum(first_back, axis=0)
    weight_shard, bias_shard, output_shard = (
        lax.psum_scatter(
            input_weight_back.astype(jnp.bfloat16), "fsdp", scatter_dimension=0, tiled=True
        ).astype(jnp.float32),
        lax.psum_scatter(
            input_bias_back.astype(jnp.bfloat16), "fsdp", scatter_dimension=2, tiled=True
        ).astype(jnp.float32),
        lax.psum_scatter(
            output_weight_back.astype(jnp.bfloat16), "fsdp", scatter_dimension=1, tiled=True
        ).astype(jnp.float32),
    )
    (
        first_gain_total,
        first_shift_total,
        second_gain_total,
        second_shift_total,
        output_bias_total,
    ) = lax.psum(
        (first_gain_back, first_shift_back, second_gain_back, second_shift_back, output_bias_back),
        ("fsdp", "tp"),
    )
    return (
        block_output,
        residual_back,
        first_gain_total,
        first_shift_total,
        weight_shard,
        bias_shard,
        output_shard,
        output_bias_total,
        second_gain_total,
        second_shift_total,
        upper_back,
        upper_bias_back,
        lower_back,
        lower_bias_back,
    )


def solution(mesh):
    in_specs = (
        P(("fsdp", "tp"), None),
        P(("fsdp", "tp"), None),
        P(("fsdp", "tp"), None),
        P("fsdp", "tp"),
        P("fsdp", None),
        P(),
        P(),
        P("fsdp", None, "tp"),
        P(None, "tp", "fsdp"),
        P("tp", "fsdp"),
        P(),
        P(),
        P(),
        P("fsdp", None, "tp"),
        P("fsdp", "tp"),
        P("fsdp", "tp", None),
        P("fsdp", None),
    )
    out_specs = (
        P(("fsdp", "tp"), None),
        P(("fsdp", "tp"), None),
        P(),
        P(),
        P("fsdp", None, "tp"),
        P(None, "tp", "fsdp"),
        P("tp", "fsdp"),
        P(),
        P(),
        P(),
        P("fsdp", None, "tp"),
        P("fsdp", "tp"),
        P("fsdp", "tp", None),
        P("fsdp", None),
    )
    return jax.shard_map(local, mesh=mesh, in_specs=in_specs, out_specs=out_specs, check_vma=False)
```

```python
import functools

import jax
import jax.numpy as jnp
from jax import lax
from jax.experimental import pallas as pl
from jax.experimental.pallas import tpu as pltpu
from jax.sharding import PartitionSpec as P

f32 = jnp.float32
bf16 = jnp.bfloat16
i32 = jnp.int32

HEAD_DIM = 64
PIECE = 256
DOCS = 4
TP = 4
BLOCK_K = 256
EXTRA = 16
EPSILON = 1e-05
MASKED = -1e30
VMEM = 60 << 20

NN = (((1,), (0,)), ((), ()))
NT = (((1,), (1,)), ((), ()))
TN = (((0,), (0,)), ((), ()))


def mxu(a, b, dims=NN):
    return lax.dot_general(a, b, dims, preferred_element_type=f32)


def cost():
    return pl.CostEstimate(flops=1, bytes_accessed=1, transcendentals=0)


def whole_spec(x):
    return pl.BlockSpec(x.shape, lambda *_: (0,) * x.ndim)


def smem_spec():
    return pl.BlockSpec(memory_space=pltpu.SMEM)


def kernel_name(kernel):
    return getattr(kernel, "func", kernel).__name__


def plain_call(kernel, ins, outs, scratch=(), scalars=()):
    return pl.pallas_call(
        kernel,
        name=kernel_name(kernel),
        grid=(1,),
        in_specs=[smem_spec() for _ in scalars] + [whole_spec(x) for x in ins],
        out_specs=[whole_spec(x) for x in outs],
        out_shape=list(outs),
        scratch_shapes=list(scratch),
        compiler_params=pltpu.CompilerParams(vmem_limit_bytes=VMEM),
        cost_estimate=cost(),
    )(*scalars, *ins)


def struct(shape, dtype):
    return jax.ShapeDtypeStruct(shape, dtype)


def send_tp(x, turn):
    return lax.ppermute(x, "tp", [(i, i ^ turn) for i in range(TP)])


def send_fsdp(x, turn):
    n = lax.axis_size("fsdp")
    return lax.ppermute(x, "fsdp", [(i, i ^ turn) for i in range(n)])


def after(x, *firsts):
    return lax.optimization_barrier((x, firsts))[0]


def sum_kernel(*refs):
    total = refs[0][...].astype(f32)
    for ref in refs[1:-1]:
        total = total + ref[...].astype(f32)
    refs[-1][...] = total.astype(refs[-1].dtype)


def added(*parts, dtype=bf16):
    return plain_call(sum_kernel, parts, [struct(parts[0].shape, dtype)])[0]


def turned_sum_kernel(*refs):
    total = refs[0][...].astype(f32)
    for ref in refs[1:-1]:
        total = total + ref[...].astype(f32)
    refs[-1][...] = total.T


def two_parts(x):
    high = x.astype(bf16)
    return jnp.concatenate([high, (x - high.astype(f32)).astype(bf16)], axis=0)


def one_part(x):
    x = x.astype(f32)
    return x[: x.shape[0] // 2] + x[x.shape[0] // 2 :]


def first_fold_kernel(own, vector, got, kept, vectors, parts):
    rows = own.shape[0]
    kept[...] = own[...].astype(f32) + got[:rows, :].astype(f32)
    vectors[...] = vector[...] + one_part(got[rows:, :])
    parts[...] = two_parts(vectors[...])


def fold_kernel(own, got, parts, out):
    rows = own.shape[0]
    out[:rows, :] = (own[...].astype(f32) + got[...].astype(f32)).astype(bf16)
    out[rows:, :] = parts[...]


def last_fold_kernel(kept, vector, *refs):
    out, vectors = refs[-2:]
    rows, width = kept.shape[0], out.shape[2]
    total = kept[...]
    sums = vector[...]
    for ref in refs[:-2]:
        total = total + ref[:rows, :].astype(f32)
        sums = sums + one_part(ref[rows:, :])
    for j in range(out.shape[1]):
        out[:, j, :] = total[:, j * width : (j + 1) * width]
    vectors[...] = sums


def normed(values):
    centered = values - jnp.mean(values, axis=-1, keepdims=True)
    inverse = lax.rsqrt(jnp.mean(centered * centered, axis=-1, keepdims=True) + EPSILON)
    return centered * inverse, inverse


def norm_back(incoming, unit, inverse, gain):
    scaled = incoming * gain
    return inverse * (
        scaled
        - jnp.mean(scaled, axis=-1, keepdims=True)
        - unit * jnp.mean(scaled * unit, axis=-1, keepdims=True)
    )


def first_kernel(x, gain, shift, docs, w_in, w_out, bias, out, packed):
    rows = x.shape[0]
    unit, _ = normed(x[...].astype(f32))
    out[:rows, :] = (unit * gain[...] + shift[...]).astype(bf16)
    out[rows:, :] = jnp.zeros_like(out[rows:, :])
    out[rows : rows + EXTRA, :rows] = jnp.broadcast_to(
        docs[...].astype(f32), (EXTRA, rows)
    ).astype(bf16)
    shard, width = w_in.shape[0], w_in.shape[2]
    for j in range(3):
        packed[:shard, j * width : (j + 1) * width] = w_in[:, j, :]
    packed[:shard, 3 * width :] = w_out[...].T
    packed[shard:, :] = jnp.zeros_like(packed[shard:, :])
    packed[shard:, :width] = bias[...]


def slots_kernel(cap, place, ids, cot, slots, sent):
    rows = ids.shape[0]
    column = ids[...].astype(f32)
    across = jnp.broadcast_to(column, (rows, 128)).T[:1]
    before = lax.broadcasted_iota(i32, (rows, rows), 0) < lax.broadcasted_iota(i32, (rows, rows), 1)
    rank = jnp.sum(jnp.where(before & (column == across), 1.0, 0.0), axis=0, keepdims=True)
    rank = rank.astype(i32)
    expert = across.astype(i32)
    mine = (expert & 1) == (place[1] & 1)
    own = (expert >> 1) * cap + rank
    slots[...] = jnp.broadcast_to(jnp.where(mine, own, -1), slots.shape)
    sent[:rows, :] = cot[...]
    sent[rows:, :] = jnp.zeros_like(sent[rows:, :])
    meta = [jnp.where(mine, -1, v).astype(f32) for v in (expert >> 1, rank)]
    meta += [jnp.zeros((EXTRA - 2, rows), f32)]
    sent[rows:, :rows] = jnp.concatenate(meta, axis=0).astype(bf16)


def other_slots_kernel(cap, sent, slots, out):
    rows = slots.shape[1]
    meta = sent[rows:, :rows].astype(f32)
    group, rank = meta[0:1].astype(i32), meta[1:2].astype(i32)
    named = group >= 0
    own = jnp.where(named, group * cap + rank, -1)
    slots[...] = jnp.broadcast_to(own, slots.shape)
    spots = lax.broadcasted_iota(i32, (out.shape[0], rows), 0)
    out[...] = mxu(jnp.where(spots == own, 1.0, 0.0).astype(bf16), sent[:rows, :]).astype(bf16)


def project_kernel(n, rows, place, *refs):
    xs, ws = refs[:TP], refs[TP : TP + n]
    q, k, v, w_in, w_out = refs[TP + n :]
    width = q.shape[1]
    bias = jnp.zeros((8, width), f32)
    lane = lax.rem(lax.broadcasted_iota(i32, (8, width), 1), HEAD_DIM) // (HEAD_DIM // n)
    for turn in range(n):
        base = pl.multiple_of((place[0] ^ turn) * rows, rows)
        w_in[pl.ds(base, rows), :] = ws[turn][:rows, : 3 * width]
        w_out[pl.ds(base, rows), :] = ws[turn][:rows, 3 * width :]
        part = ws[turn][rows:, :width].astype(f32)[:8]
        bias = jnp.where(lane == (place[0] ^ turn), part, bias)
    block = q.shape[0] // TP
    for r in range(TP):
        x = xs[r][:block, :]
        here = pl.ds(r * block, block)
        q[here, :] = ((mxu(x, w_in[:, :width]) + bias[0:1, :]) * 0.125).astype(bf16)
        k[here, :] = mxu(x, w_in[:, width : 2 * width]).astype(bf16)
        v[here, :] = (mxu(x, w_in[:, 2 * width :]) + bias[1:2, :]).astype(bf16)


def middle_kernel(*refs):
    ctxs, ws = refs[:TP], refs[TP : 2 * TP]
    residual, bias, gain, shift, mixed, second = refs[-6:]
    total = residual[...].astype(f32) + bias[...]
    for r in range(TP):
        total = total + mxu(ctxs[r][...], ws[r][...], NT)
    mixed[...] = total
    unit, _ = normed(total)
    second[...] = (unit * gain[...] + shift[...]).astype(bf16)


def turn_kernel(*refs):
    ws = refs[:TP]
    own, other, mixed, cot, gain = refs[TP : TP + 5]
    back, low, sums = refs[TP + 5 : TP + 8]
    outs = refs[TP + 8 :]
    unit, inverse = normed(mixed[...])
    second_back = own[...].astype(f32) + other[...].astype(f32)
    total = cot[...].astype(f32) + norm_back(second_back, unit, inverse, gain[...])
    back[...] = total
    low[...] = total.astype(bf16)
    sums[...] = jnp.concatenate(
        [
            jnp.sum(second_back * unit, axis=0, keepdims=True),
            jnp.sum(second_back, axis=0, keepdims=True),
            jnp.sum(total, axis=0, keepdims=True),
            jnp.zeros((5, total.shape[1]), f32),
        ],
        axis=0,
    )
    for r in range(TP):
        outs[r][...] = mxu(low[...], ws[r][...]).astype(bf16)


def output_weight_kernel(n, rows, place, *refs):
    ctxs, low, kept, away, total = refs[:TP], refs[TP], refs[TP + 1], refs[TP + 2], refs[TP + 3]
    size = total.shape[0]
    for r in range(TP):
        total[...] = mxu(low[...], ctxs[r][...], TN)
        out = away if r & 1 else kept
        for at, turn in enumerate(list(range(0, n, 2)) + list(range(1, n, 2))):
            base = pl.multiple_of((place[0] ^ turn) * rows, rows)
            to = (r // 2) * size + at * rows
            out[to : to + rows, :] = total[pl.ds(base, rows), :].astype(bf16)


def pair_sum_kernel(a, b, here, there):
    size = here.shape[0]
    for at, out in enumerate((here, there)):
        rows = slice(at * size, (at + 1) * size)
        out[...] = (a[rows, :].astype(f32) + b[rows, :].astype(f32)).astype(bf16)


def input_back_kernel(count, turns, *refs):
    backs, w_in, outs = refs[:count], refs[count], refs[count + 1 :]
    pairs = count // 3
    width = w_in.shape[1] // 3
    block = outs[0].shape[0]
    for at, r in enumerate(turns):
        here = pl.ds(r * block, block)
        total = None
        for j in range(3):
            back = jnp.concatenate([backs[3 * p + j][here, :] for p in range(pairs)], axis=1)
            part = mxu(back, w_in[:, j * width : (j + 1) * width], NT)
            total = part if total is None else total + part
        outs[at][...] = total.astype(bf16)


def lane_sums(x):
    total = jnp.sum(x, axis=1, keepdims=True)
    return jnp.broadcast_to(total, (x.shape[0], 128)).T[:8]


def input_weight_kernel(n, rows, count, place, *refs):
    xs, backs, w_in, sums2 = refs[:TP], refs[TP : TP + count], refs[TP + count], refs[TP + count + 1]
    parts, vectors, small, total = refs[TP + count + 2 : -3], *refs[-3:]
    pairs = count // 3
    width = w_in.shape[1] // 3
    block = backs[0].shape[0] // TP
    ones = jnp.ones((8, block), bf16)
    for j in range(3):
        part = jnp.zeros((total.shape[0], width), f32)
        column = jnp.zeros((8, width), f32)
        for r in range(TP):
            here = pl.ds(r * block, block)
            back = jnp.concatenate([backs[3 * p + j][here, :] for p in range(pairs)], axis=1)
            part += mxu(xs[r][:block, :], back, TN)
            column += mxu(ones, back)
        total[:, j * width : (j + 1) * width] = part
        small[8 * j : 8 * j + 8, :] = column
    for turn in range(n):
        base = pl.multiple_of((place[0] ^ turn) * rows, rows)
        parts[turn][:rows, :] = total[pl.ds(base, rows), :].astype(bf16)
    w = w_in[...].astype(f32)
    column = jnp.concatenate([small[8 * j : 8 * j + 1, :] for j in range(3)], axis=1)
    lines = [lane_sums(total[...] * w)[:1], lane_sums(w * column)[:1]]
    lines += [sums2[r : r + 1, :] for r in range(3)]
    for r, line in enumerate(lines):
        vectors[r : r + 1, :] = line[:, : 3 * width]
    rests = [line[:, 3 * width :] for line in lines]
    rests += [small[0:1, :], small[16:17, :], jnp.zeros((1, 2 * width), f32)]
    rests = jnp.concatenate(rests, axis=1)
    for r in range(3):
        vectors[5 + r : 6 + r, :] = rests[:, 3 * width * r : 3 * width * (r + 1)]
    parts[1][rows:, :] = two_parts(vectors[...])


def last_kernel(residual, gain, own, other, mixed_back, out):
    unit, inverse = normed(residual[...].astype(f32))
    first_back = own[...].astype(f32) + other[...].astype(f32)
    out[...] = mixed_back[...] + norm_back(first_back, unit, inverse, gain[...])


def half_rows(x, h):
    rows = lax.broadcasted_iota(i32, x.shape, 0)
    keep = (rows < HEAD_DIM) if h == 0 else (rows >= HEAD_DIM)
    return jnp.where(keep, x, jnp.zeros_like(x))


def half_lanes(x, h):
    lanes = lax.broadcasted_iota(i32, x.shape, 1)
    keep = (lanes < HEAD_DIM) if h == 0 else (lanes >= HEAD_DIM)
    return jnp.where(keep, x, jnp.zeros_like(x))


def key_base(kb, block, t):
    per = block // BLOCK_K
    return pl.multiple_of(((kb // per) ^ t) * block + lax.rem(kb, per) * BLOCK_K, BLOCK_K)


def attend_kernel(t_ref, q_ref, k_ref, v_ref, a_ref, b_ref, *rest):
    outs, lse_ref, vt = rest[-TP - 2 : -2], rest[-2], rest[-1]
    i = pl.program_id(0)
    bq = q_ref.shape[0]
    bk = BLOCK_K

    @pl.when(i == 0)
    def _():
        vt[...] = v_ref[...].T

    qt = q_ref[...].T
    qz = [half_rows(qt, h) for h in (0, 1)]
    a = a_ref[...]
    b = b_ref[...]

    def body(kb, carry):
        base = key_base(kb, bq, t_ref[0])
        kblk = k_ref[pl.ds(base, bk), :]
        j = kb * bk + lax.broadcasted_iota(i32, (bk, bq), 0)
        mask = (j >= a) & (j <= b)
        out = []
        for h in (0, 1):
            m, l, acc = carry[h]
            s = jnp.where(mask, mxu(kblk, qz[h]), MASKED)
            mn = jnp.maximum(m, jnp.max(s, axis=0, keepdims=True))
            p = jnp.exp(s - mn)
            al = jnp.exp(m - mn)
            l = al * l + jnp.sum(p, axis=0, keepdims=True)
            acc = acc * al + mxu(
                vt[pl.ds(HEAD_DIM * h, HEAD_DIM), pl.ds(base, bk)], p.astype(bf16)
            )
            out.append((mn, l, acc))
        return tuple(out)

    init = tuple(
        (jnp.full((1, bq), MASKED, f32), jnp.zeros((1, bq), f32), jnp.zeros((HEAD_DIM, bq), f32))
        for _ in (0, 1)
    )
    res = lax.fori_loop(jnp.min(a) // bk, jnp.max(b) // bk + 1, body, init)
    ot = jnp.concatenate([acc / l for m, l, acc in res], axis=0)
    o = ot.T.astype(bf16)
    for r in range(TP):

        @pl.when(i == r)
        def _(r=r):
            outs[r][...] = o

    lse_ref[...] = jnp.concatenate(
        [m + jnp.log(l) for m, l, acc in res] + [jnp.zeros((6, bq), f32)], axis=0
    )


def attention_fwd(pair, q, k, v, a, b, t, before):
    S, W = q.shape
    bq = S // TP
    whole = pl.BlockSpec((S, 128), lambda i, *_: (0, pair))
    row = pl.BlockSpec((1, bq), lambda i, *_: (0, i))
    return pl.pallas_call(
        attend_kernel,
        name="attend",
        grid_spec=pltpu.PrefetchScalarGridSpec(
            num_scalar_prefetch=1,
            grid=(TP,),
            in_specs=[pl.BlockSpec((bq, 128), lambda i, *_: (i, pair)), whole, whole, row, row]
            + [pl.BlockSpec(memory_space=pl.ANY)] * len(before),
            out_specs=[pl.BlockSpec((bq, 128), lambda i, *_: (0, pair))] * TP
            + [pl.BlockSpec((8, bq), lambda i, *_: (0, i))],
            scratch_shapes=[pltpu.VMEM((128, S), bf16)],
        ),
        out_shape=[struct((bq, W), bf16)] * TP + [struct((8, S), f32)],
        input_output_aliases={6 + r: r for r in range(len(before))},
        compiler_params=pltpu.CompilerParams(vmem_limit_bytes=VMEM),
        cost_estimate=cost(),
    )(t, q, k, v, a, b, *before)


def attend_back_kernel(t_ref, q_ref, k_ref, v_ref, *rest):
    dos, os = rest[:TP], rest[TP : 2 * TP]
    lse_ref, a_ref, b_ref, dq_ref, dk_ref, dv_ref, kt, dk_acc, dv_acc, do_s, o_s = rest[2 * TP :]
    i = pl.program_id(0)
    bq = q_ref.shape[0]
    bk = BLOCK_K

    @pl.when(i == 0)
    def _():
        kt[...] = k_ref[...].T
        dk_acc[...] = jnp.zeros_like(dk_acc)
        dv_acc[...] = jnp.zeros_like(dv_acc)

    for r in range(TP):

        @pl.when(i == r)
        def _(r=r):
            do_s[...] = dos[r][...]
            o_s[...] = os[r][...]

    q = q_ref[...]
    do = do_s[...]
    qt = q.T
    dot_ = do.T
    qz = [half_rows(qt, h) for h in (0, 1)]
    dz = [half_rows(dot_, h) for h in (0, 1)]
    qcat = jnp.concatenate([half_lanes(q, 0), half_lanes(q, 1)], axis=0)
    dcat = jnp.concatenate([half_lanes(do, 0), half_lanes(do, 1)], axis=0)
    prod = (do.astype(f32) * o_s[...].astype(f32)).T
    delta = [
        jnp.sum(prod[:HEAD_DIM], axis=0, keepdims=True),
        jnp.sum(prod[HEAD_DIM:], axis=0, keepdims=True),
    ]
    lse = [lse_ref[0:1, :], lse_ref[1:2, :]]
    a = a_ref[...]
    b = b_ref[...]

    def body(kb, carry):
        base = key_base(kb, bq, t_ref[0])
        here = pl.ds(base, bk)
        kblk = k_ref[here, :]
        vblk = v_ref[here, :]
        j = kb * bk + lax.broadcasted_iota(i32, (bk, bq), 0)
        mask = (j >= a) & (j <= b)
        ps, dss, out = [], [], []
        for h in (0, 1):
            p = jnp.exp(jnp.where(mask, mxu(kblk, qz[h]) - lse[h], MASKED))
            ds = (p * (mxu(vblk, dz[h]) - delta[h])).astype(bf16)
            ps.append(p.astype(bf16))
            dss.append(ds)
            out.append(carry[h] + mxu(kt[pl.ds(HEAD_DIM * h, HEAD_DIM), here], ds))
        dv_acc[here, :] += mxu(jnp.concatenate(ps, axis=1), dcat)
        dk_acc[here, :] += mxu(jnp.concatenate(dss, axis=1), qcat)
        return tuple(out)

    init = tuple(jnp.zeros((HEAD_DIM, bq), f32) for _ in (0, 1))
    dqt = lax.fori_loop(jnp.min(a) // bk, jnp.max(b) // bk + 1, body, init)
    dq_ref[...] = (jnp.concatenate(dqt, axis=0).T * 0.125).astype(bf16)

    @pl.when(i == TP - 1)
    def _():
        dk_ref[...] = dk_acc[...].astype(bf16)
        dv_ref[...] = dv_acc[...].astype(bf16)


def attention_bwd(pair, q, k, v, dos, os, lse, a, b, t):
    S = q.shape[0]
    bq = S // TP
    context = pl.BlockSpec((bq, 128), lambda i, *_: (0, pair))
    whole = pl.BlockSpec((S, 128), lambda i, *_: (0, pair))
    out = pl.BlockSpec((S, 128), lambda i, *_: (0, 0))
    row = pl.BlockSpec((1, bq), lambda i, *_: (0, i))
    return pl.pallas_call(
        attend_back_kernel,
        name="attend_back",
        grid_spec=pltpu.PrefetchScalarGridSpec(
            num_scalar_prefetch=1,
            grid=(TP,),
            in_specs=[pl.BlockSpec((bq, 128), lambda i, *_: (i, pair)), whole, whole]
            + [context] * (2 * TP)
            + [pl.BlockSpec((8, bq), lambda i, *_: (0, i)), row, row],
            out_specs=[pl.BlockSpec((bq, 128), lambda i, *_: (i, 0)), out, out],
            scratch_shapes=[
                pltpu.VMEM((128, S), bf16),
                pltpu.VMEM((S, 128), f32),
                pltpu.VMEM((S, 128), f32),
                pltpu.VMEM((bq, 128), bf16),
                pltpu.VMEM((bq, 128), bf16),
            ],
        ),
        out_shape=[struct((S, 128), bf16)] * 3,
        compiler_params=pltpu.CompilerParams(vmem_limit_bytes=VMEM),
        cost_estimate=cost(),
    )(t, q, k, v, *dos, *os, lse, a, b)


def intervals_kernel(place, starts, *refs):
    first, end = refs[TP:]
    rows = first.shape[1] // TP
    docs = [ref[0:1, :rows].astype(f32) for ref in refs[:TP]]
    bounds = [jnp.zeros((1, 1), f32)]
    for number in range(DOCS):
        here = sum(jnp.sum(jnp.where(d == number, 1.0, 0.0), axis=1, keepdims=True) for d in docs)
        bounds.append(bounds[-1] + here)
    for r in range(TP):
        low = jnp.zeros((1, rows), f32)
        last = jnp.zeros((1, rows), f32)
        for number in range(DOCS):
            here = docs[r] == number
            low = jnp.where(here, bounds[number], low)
            last = jnp.where(here, bounds[number + 1] - 1.0, last)
        spot = (place[1] ^ r) * rows + lax.broadcasted_iota(i32, (1, rows), 1)
        piece_last = jnp.full((1, rows), -1, i32)
        for p in range(2):
            inside = (spot >= starts[0, p]) & (spot < starts[0, p] + PIECE)
            piece_last = jnp.where(inside, starts[0, p] + PIECE - 1, piece_last)
        first[:, r * rows : (r + 1) * rows] = low.astype(i32)
        end[:, r * rows : (r + 1) * rows] = jnp.maximum(
            spot, jnp.minimum(piece_last, last.astype(i32))
        )


def intervals(here, starts, xs, rows):
    tail = pl.BlockSpec((EXTRA, xs[0].shape[1]), lambda i: (rows // EXTRA, 0))
    out = struct((1, TP * rows), i32)
    return pl.pallas_call(
        intervals_kernel,
        name="intervals",
        grid=(1,),
        in_specs=[smem_spec(), smem_spec()] + [tail] * TP,
        out_specs=[whole_spec(out)] * 2,
        out_shape=[out] * 2,
        cost_estimate=cost(),
    )(here, starts, *xs)


def place_kernel(x, s, out):
    spots = lax.broadcasted_iota(i32, (out.shape[0], s.shape[1]), 0)
    pick = jnp.where(spots == s[0:1, :], 1.0, 0.0).astype(bf16)
    out[...] = mxu(pick, x[...]).astype(bf16)


def collect_kernel(s_own, s_other, own_rows, other_rows, own, other):
    slots = lax.broadcasted_iota(i32, (own_rows.shape[0], own.shape[0]), 0)
    for s, rows, out in ((s_own, own_rows, own), (s_other, other_rows, other)):
        pick = jnp.where(slots == s[0:1, :], 1.0, 0.0).astype(bf16)
        out[...] = mxu(pick, rows[...], TN).astype(bf16)


def collect(s_own, s_other, own_rows, other_rows):
    rows, width = s_own.shape[1], own_rows.shape[1]
    return plain_call(
        collect_kernel,
        [s_own, s_other, own_rows, other_rows],
        [struct((rows, width), bf16)] * 2,
    )


def act_back_kernel(lo, near, far, down_a, down_b, out_near, out_far, sums):
    hidden = down_a.shape[0]
    half = pl.num_programs(0) // 2
    for at, (x, out) in enumerate(((near, out_near), (far, out_far))):

        @pl.when(pl.program_id(0) // half == at)
        def _(x=x, out=out):
            act_back_tile(hidden, x, down_a, down_b, out, sums)


def act_back_tile(hidden, x, down_a, down_b, out, sums):
    for j, down in enumerate((down_a, down_b)):
        out[:, j * hidden : (j + 1) * hidden] = mxu(x[...], down[...], NT).astype(bf16)
    total = mxu(jnp.ones((8, x.shape[0]), bf16), x[...])

    @pl.when(pl.program_id(0) == 0)
    def _():
        sums[...] = jnp.zeros_like(sums)

    sums[...] += total


def expert_kernel(lo, x, act_back, up_a, up_b, bias_a, bias_b, act, pre_back, x_back):
    width = up_a.shape[1]
    total = None
    for j, (up, bias) in enumerate(((up_a, bias_a), (up_b, bias_b))):
        here = slice(j * width, (j + 1) * width)
        pre = mxu(x[...], up[...]) + bias[...]
        square = pre * pre
        tan = jnp.tanh(0.7978845608028654 * pre * (1.0 + 0.044715 * square))
        half = 0.5 + 0.5 * tan
        act[:, here] = (pre * half).astype(bf16)
        slope = half + (0.5 * pre) * (1.0 - tan * tan) * (
            0.7978845608028654 + 0.1070322243 * square
        )
        low = (act_back[:, here].astype(f32) * slope).astype(bf16)
        pre_back[:, here] = low
        part = mxu(low, up[...], NT)
        total = part if total is None else total + part
    x_back[...] = total.astype(bf16)


def expert_out_kernel(lo, act_0, act_1, down_a, down_b, out):
    hidden = down_a.shape[0]
    half = pl.num_programs(0) // 2
    for at, act in enumerate((act_0, act_1)):

        @pl.when(pl.program_id(0) // half == at)
        def _(act=act):
            total = mxu(act[:, :hidden], down_a[...]) + mxu(act[:, hidden:], down_b[...])
            out[...] = total.astype(bf16)


def out_sum_kernel(cap, near, far, bias, out):
    half = near.shape[0] // 2
    for at in range(half // cap):
        for core in range(2):
            here = slice(core * half + at * cap, core * half + (at + 1) * cap)
            to = (2 * at + core) * cap
            total = near[here, :].astype(f32) + far[here, :].astype(f32) + bias[...]
            out[to : to + cap, :] = total.astype(bf16)


def collect_both_kernel(cap, s_own, s_other, both, own, other):
    slots = lax.broadcasted_iota(i32, (both.shape[0] // 2, own.shape[0]), 0)
    for core, (s, out) in enumerate(((s_own, own), (s_other, other))):
        pick = jnp.where(slots == s[0:1, :], 1.0, 0.0).astype(bf16)
        rows = jnp.concatenate(
            [both[at : at + cap, :] for at in range(core * cap, both.shape[0], 2 * cap)], axis=0
        )
        out[...] = mxu(pick, rows, TN).astype(bf16)


def up_outer_kernel(count, lo, *refs):
    left = jnp.concatenate([r[...] for r in refs[:count]], axis=0)
    right = jnp.concatenate([r[...] for r in refs[count:-2]], axis=0)
    out, sums = refs[-2:]
    out[...] = mxu(left, right, TN).astype(out.dtype)
    sums[...] = mxu(jnp.ones((8, right.shape[0]), bf16), right)


def down_outer_kernel(count, lo, *refs):
    left = jnp.concatenate([r[...] for r in refs[:count]], axis=0)
    right = jnp.concatenate([r[...] for r in refs[count:-1]], axis=0)
    refs[-1][...] = mxu(left, right, TN).astype(refs[-1].dtype)


def halves_kernel(lo, up, down, out):
    out[0] = up[...]
    out[1] = down[...]


def fill_kernel(lo, kept, other, out):
    out[...] = other[...].astype(f32)


class Expert:
    def __init__(self, lo, width, hidden):
        self.lo = jnp.reshape(lo, (1,)).astype(i32)
        self.width, self.hidden = width, hidden
        self.tile = 256

    def hold(self, up, up_bias, up_bias_other, down, other):
        self.up, self.down, self.other = up, down, other
        self.up_bias, self.up_bias_other = up_bias[:, None, :], up_bias_other

    def call(self, kernel, grid, in_specs, out_specs, out_shape, args, alias=None, scratch=()):
        return pl.pallas_call(
            kernel,
            name=kernel_name(kernel),
            grid_spec=pltpu.PrefetchScalarGridSpec(
                num_scalar_prefetch=1,
                grid=grid,
                in_specs=in_specs,
                out_specs=out_specs,
                scratch_shapes=list(scratch),
            ),
            out_shape=out_shape,
            input_output_aliases=alias or {},
            compiler_params=pltpu.CompilerParams(vmem_limit_bytes=VMEM),
            cost_estimate=cost(),
        )(self.lo, *args)

    def away(self, at):
        return pl.BlockSpec((None,) + self.other.shape[1:], lambda i, lo: (at, 0, 0))

    def own(self, x):
        return pl.BlockSpec((None,) + x.shape[1:], lambda i, lo: (lo[0], 0, 0))

    def row(self, columns):
        return pl.BlockSpec((self.tile, columns), lambda i, lo: (i, 0))

    def two(self, columns, steps):
        return [
            pl.BlockSpec((self.tile, columns), lambda i, lo: (jnp.minimum(i, steps - 1), 0)),
            pl.BlockSpec((self.tile, columns), lambda i, lo: (jnp.maximum(i - steps, 0), 0)),
        ]

    def act_back(self, near, far):
        rows = near.shape[0]
        steps = rows // self.tile
        return self.call(
            act_back_kernel,
            (2 * steps,),
            self.two(self.width, steps) + [self.own(self.down), self.away(1)],
            self.two(2 * self.hidden, steps)
            + [pl.BlockSpec((8, self.width), lambda i, lo: (0, 0))],
            [struct((rows, 2 * self.hidden), bf16)] * 2 + [struct((8, self.width), f32)],
            [near, far, self.down, self.other],
        )

    def rows(self, x, act_back):
        rows = x.shape[0]
        wide = self.row(2 * self.hidden)
        return self.call(
            expert_kernel,
            (rows // self.tile,),
            [
                self.row(self.width),
                wide,
                self.own(self.up),
                self.away(0),
                self.own(self.up_bias),
                whole_spec(self.up_bias_other),
            ],
            [wide, wide, self.row(self.width)],
            [struct((rows, 2 * self.hidden), bf16)] * 2 + [struct((rows, self.width), bf16)],
            [x, act_back, self.up, self.other, self.up_bias, self.up_bias_other],
        )

    def out(self, act_0, act_1):
        rows = act_0.shape[0]
        steps = rows // self.tile
        return self.call(
            expert_out_kernel,
            (2 * steps,),
            self.two(2 * self.hidden, steps) + [self.own(self.down), self.away(1)],
            self.row(self.width),
            struct((2 * rows, self.width), bf16),
            [act_0, act_1, self.down, self.other],
        )

    def outer_specs(self, own):
        size, tile = self.width, 512
        if own:
            out = pl.BlockSpec((None, tile, size), lambda i, lo: (lo[0], i, 0))
            return out, struct((2, size, size), f32)
        return pl.BlockSpec((tile, size), lambda i, lo: (i, 0)), struct((size, size), bf16)

    def up_outer(self, xs, backs, at, own):
        size, count = self.width, len(xs)
        out, shape = self.outer_specs(own)
        return self.call(
            functools.partial(up_outer_kernel, count),
            (size // 512,),
            [pl.BlockSpec((xs[0].shape[0], 512), lambda i, lo: (0, i))] * count
            + [pl.BlockSpec((backs[0].shape[0], size), lambda i, lo: (0, at))] * len(backs),
            [out, pl.BlockSpec((8, size), lambda i, lo: (0, 0))],
            [shape, struct((8, size), f32)],
            list(xs) + list(backs),
        )

    def down_outer(self, acts, cots, at, own):
        rows, size, count = acts[0].shape[0], self.width, len(acts)
        out, shape = self.outer_specs(own)
        return self.call(
            functools.partial(down_outer_kernel, count),
            (size // 512,),
            [pl.BlockSpec((rows, 512), lambda i, lo: (0, at * (size // 512) + i))] * count
            + [whole_spec(c) for c in cots],
            out,
            shape,
            list(acts) + list(cots),
        )

    def halves(self, up, down):
        size = up.shape[1]
        part = pl.BlockSpec((None, size // 4, size), lambda i, lo: (1 - lo[0], i, 0))
        return self.call(
            halves_kernel,
            (4,),
            [part, part],
            pl.BlockSpec((2, size // 4, size), lambda i, lo: (0, i, 0)),
            struct((2, size, size), bf16),
            [up, down],
        )

    def fill(self, kept, other):
        size = other.shape[0]
        return self.call(
            fill_kernel,
            (4,),
            [
                pl.BlockSpec(memory_space=pl.ANY),
                pl.BlockSpec((size // 4, size), lambda i, lo: (i, 0)),
            ],
            pl.BlockSpec((None, size // 4, size), lambda i, lo: (1 - lo[0], i, 0)),
            struct(kept.shape, f32),
            [kept, other],
            alias={1: 0},
        )


def ordered(lo, own, other):
    return jnp.where(lo == 0, jnp.stack([own, other]), jnp.stack([other, own]))


def local(
    residual_in,
    out_cotangent,
    expert_index,
    document_index,
    piece_starts,
    first_norm_gain,
    first_norm_shift,
    input_weight,
    input_bias,
    output_weight,
    output_bias,
    second_norm_gain,
    second_norm_shift,
    expert_up,
    expert_up_bias,
    expert_down,
    expert_down_bias,
):
    rows, width = residual_in.shape
    n = lax.axis_size("fsdp")
    g = lax.axis_index("fsdp")
    t = lax.axis_index("tp")
    lo = t & 1
    place = jnp.reshape(g, (1,)).astype(i32)
    turn = jnp.reshape(t, (1,)).astype(i32)
    row = lambda v: v.reshape(1, -1)
    head_width = input_weight.shape[2]
    shard = input_weight.shape[0]
    cap = rows * 2 // (2 * n)
    evens = list(range(0, n, 2))

    expert = Expert(lo, width, expert_up.shape[2])

    share = jnp.pad(
        jnp.tile(input_bias, (1, 1, n)).reshape(2, head_width), ((0, EXTRA - 2), (0, 0))
    )
    x0, packed = plain_call(
        first_kernel,
        [
            residual_in,
            row(first_norm_gain),
            row(first_norm_shift),
            document_index,
            input_weight,
            output_weight,
            share,
        ],
        [struct((rows + EXTRA, width), bf16), struct((shard + EXTRA, 4 * head_width), bf16)],
    )
    x2 = send_tp(x0, 2)
    weights = {0: packed}
    for k in evens[1:]:
        weights[k] = send_fsdp(packed, k)
    weights[1] = send_fsdp(packed, 1)
    arrived = [weights[k] for k in evens[1:] + [1]]
    for k in evens[1:]:
        weights[k ^ 1] = send_fsdp(after(weights[k], arrived), 1)
    x1 = send_tp(after(x0, arrived), 1)
    x3 = send_tp(after(x2, arrived), 1)
    xs = [x0, x1, x2, x3]
    halves_sent = expert.halves(*after((expert_up, expert_down), x1))

    here = jnp.concatenate([place, turn])
    length = TP * rows
    first, end = intervals(here, piece_starts, xs, rows)
    s_own, cot_sent = plain_call(
        functools.partial(slots_kernel, cap),
        [after(expert_index, x1), out_cotangent],
        [struct((8, rows), i32), struct((rows + EXTRA, width), bf16)],
        scalars=[here],
    )

    def exchange(x):
        return lax.all_to_all(x, "fsdp", split_axis=0, concat_axis=0, tiled=True)

    slotted = struct((n * cap, width), bf16)
    cot_sent_own = plain_call(place_kernel, [out_cotangent, s_own], [slotted])[0]
    queries, keys, values, w_in, w_out0 = plain_call(
        functools.partial(project_kernel, n, shard),
        list(after(tuple(xs), cot_sent_own, halves_sent)) + [weights[k] for k in range(n)],
        [struct((length, head_width), bf16)] * 3
        + [struct((width, 3 * head_width), bf16), struct((width, head_width), bf16)],
        scalars=[place],
    )
    cot_other = send_tp(after(cot_sent, queries), 1)
    s_other, cot_sent_other = plain_call(
        functools.partial(other_slots_kernel, cap),
        [cot_other],
        [struct((8, rows), i32), slotted],
    )
    near_own = exchange(cot_sent_own)

    halves_other = send_tp(after(halves_sent, queries), 1)
    down_bias = lax.dynamic_index_in_dim(expert_down_bias, lo, keepdims=True)

    w_out2 = send_tp(w_out0, 2)
    w_out1 = send_tp(w_out0, 1)
    pairs = head_width // 128
    contexts, totals = [], []
    firsts = [queries, (cot_other, near_own)]
    cot_pieces = []
    for p in range(pairs):
        *contexts, total = attention_fwd(
            p,
            after(queries, firsts[min(p, 1)], totals),
            keys,
            values,
            first,
            end,
            turn,
            contexts,
        )
        if p == 0:
            near_other = exchange(after(cot_sent_other, near_own, total))
            far_own = send_tp(after(near_own, total, w_out1, w_out2, halves_other), 2)
            cot_pieces = [near_own, far_own, near_other, send_tp(near_other, 2)]
        totals.append(total)
    w_outs = [w_out0, w_out1, w_out2, send_tp(after(w_out2, total), 1)]
    ctxs = [contexts[0]] + [send_tp(contexts[r], r) for r in range(1, TP)]
    expert.hold(expert_up, expert_up_bias, None, expert_down, halves_other)
    act_backs, cot_sums = [None] * 4, [None] * 2
    act_backs[0], act_backs[1], cot_sums[0] = expert.act_back(*cot_pieces[:2])
    mixed, second = plain_call(
        middle_kernel,
        ctxs
        + w_outs
        + [
            after(residual_in, act_backs[0]),
            row(output_bias),
            row(second_norm_gain),
            row(second_norm_shift),
        ],
        [struct((rows, width), f32), struct((rows, width), bf16)],
    )

    bias_sent = lax.dynamic_index_in_dim(after(expert_up_bias, second), 1 - lo, keepdims=True)
    expert.hold(expert_up, expert_up_bias, send_tp(bias_sent, 1), expert_down, halves_other)
    act_backs[2], act_backs[3], cot_sums[1] = expert.act_back(*cot_pieces[2:])
    cot_sum = added(*cot_sums, dtype=f32)[:1]
    sent_own = plain_call(place_kernel, [second, s_own], [slotted])[0]
    second_other = send_tp(second, 1)
    sent_other = plain_call(
        place_kernel, [second_other, s_other], [slotted]
    )[0]
    rows_own = exchange(after(sent_own, near_other))
    rows_other = exchange(after(sent_other, rows_own, cot_pieces[3]))
    pieces = [rows_own, send_tp(rows_own, 2), rows_other]
    acts, pre_backs, x_backs = [], [], []
    for at in range(4):
        act, pre_back, x_back = expert.rows(after(pieces[at], x_backs, act_backs[3]), act_backs[at])
        if at == 0:
            pieces.append(send_tp(after(rows_other, x_back), 2))
        acts.append(act)
        pre_backs.append(pre_back)
        x_backs.append(x_back)

    got_own = send_tp(x_backs[1], 2)
    got_other = send_tp(x_backs[3], 2)
    back_sent_own = added(x_backs[0], after(got_own, x_backs[3]))
    back_home_own = exchange(back_sent_own)
    out_far = expert.out(*after((acts[1], acts[3]), back_sent_own))
    up_away, up_sum_away = expert.up_outer(pieces, after(tuple(pre_backs), out_far), 1, False)
    back_sent_other = added(x_backs[2], after(got_other, up_away))
    back_home_other = exchange(after(back_sent_other, back_home_own))
    out_got = send_tp(after(out_far, got_other), 2)
    late = after(tuple(acts), back_sent_other)
    down_away = expert.down_outer(late, cot_pieces, 1, False)
    out_near = expert.out(*after((acts[0], acts[2]), down_away))
    up_own, up_sum = expert.up_outer(pieces, after(tuple(pre_backs), out_near), 0, True)
    up_got, down_got = send_tp(up_away, 1), send_tp(down_away, 1)
    sent = send_tp(jnp.concatenate([up_sum_away[:1], cot_sum], axis=0), 1)
    back_own, back_away = collect(
        s_own, s_other, back_home_own, after(back_home_other, up_own, up_got, down_got, out_got, sent)
    )
    back_other = send_tp(back_away, 1)

    mixed_back, mixed_low, sums2, *ctx_backs = plain_call(
        turn_kernel,
        w_outs + [back_own, back_other, mixed, out_cotangent, row(second_norm_gain)],
        [
            struct((rows, width), f32),
            struct((rows, width), bf16),
            struct((8, width), f32),
        ]
        + [struct((rows, head_width), bf16)] * TP,
    )

    wo_kept, wo_away = plain_call(
        functools.partial(output_weight_kernel, n, shard),
        ctxs + [mixed_low],
        [struct((2 * width, head_width), bf16)] * 2,
        scratch=[pltpu.VMEM((width, head_width), f32)],
        scalars=[place],
    )
    up_bias_back = ordered(lo, up_sum[0], sent[0])
    down_bias_back = ordered(lo, cot_sum[0], sent[1])

    dos = [ctx_backs[0]] + [send_tp(ctx_backs[r], r) for r in range(1, TP)]
    wo_got = send_tp(wo_away, 1)
    out_sent = plain_call(
        functools.partial(out_sum_kernel, cap),
        [out_near, after(out_got, dos[0]), down_bias],
        [struct((2 * n * cap, width), bf16)],
    )[0]
    out_home = exchange(out_sent)
    projected_backs = []
    firsts = [(wo_away, out_sent), None]
    for p in range(pairs):
        back = attention_bwd(
            p,
            after(queries, firsts[min(p, 1)], projected_backs),
            keys,
            values,
            dos,
            contexts,
            totals[p],
            first,
            end,
            turn,
        )
        projected_backs += back
        if p == 0:
            wo_sum, wo_there = plain_call(
                pair_sum_kernel,
                [wo_kept, after(wo_got, back)],
                [struct((width, head_width), bf16)] * 2,
            )
            wo_got = send_tp(wo_there, 2)
            firsts[1] = wo_sum
    wo = added(wo_sum, after(wo_got, projected_backs))

    def input_back(turns, first):
        return plain_call(
            functools.partial(input_back_kernel, 3 * pairs, turns),
            projected_backs + [after(w_in, first)],
            [struct((rows, width), bf16)] * 2,
        )

    middle = n // 2 * shard
    wo_kept = added(wo[:middle], send_fsdp(wo[middle:], 1))
    wo_parts = [wo_kept[:shard]] + [
        send_fsdp(wo_kept[(at + 1) * shard : (at + 2) * shard], k)
        for at, k in enumerate(evens[1:])
    ]
    output_weight_back = plain_call(
        turned_sum_kernel, wo_parts, [struct((head_width, shard), f32)]
    )[0]

    *parts, vector = plain_call(
        functools.partial(input_weight_kernel, n, shard, 3 * pairs),
        xs + projected_backs + [w_in, sums2],
        [
            struct((shard + (EXTRA if k == 1 else 0), 3 * head_width), bf16)
            for k in range(n)
        ]
        + [struct((8, 3 * head_width), f32)],
        scratch=[
            pltpu.VMEM((24, head_width), f32),
            pltpu.VMEM((width, 3 * head_width), f32),
        ],
        scalars=[place],
    )
    part3, part2 = input_back((3, 2), (parts[0], wo))
    got3 = send_tp(part3, 1)
    part1, part0 = input_back((1, 0), part3)
    sum2 = added(part2, after(got3, part0))
    got2 = send_tp(sum2, 2)
    sum0 = added(part0, send_tp(part1, 1))
    got = {k: send_fsdp(parts[k + 1], 1) for k in evens}
    kept, vector, vector_parts = plain_call(
        first_fold_kernel,
        [parts[0], vector, got[0]],
        [
            struct((shard, 3 * head_width), f32),
            struct((8, 3 * head_width), f32),
            struct((EXTRA, 3 * head_width), bf16),
        ],
    )
    folds = [
        plain_call(
            fold_kernel,
            [parts[k], got[k], vector_parts],
            [struct((shard + EXTRA, 3 * head_width), bf16)],
        )[0]
        for k in evens[1:]
    ]
    wi_kept = (kept, folds)
    wi_total, vector = plain_call(
        last_fold_kernel,
        [kept, vector] + [send_fsdp(fold, k) for fold, k in zip(folds, evens[1:])],
        [struct((shard, 3, head_width), f32), struct((8, 3 * head_width), f32)],
    )

    out_own, out_away = plain_call(
        functools.partial(collect_both_kernel, cap),
        [s_own, s_other, after(out_home, wi_kept)],
        [struct((rows, width), bf16)] * 2,
    )
    out_other = send_tp(out_away, 1)
    block_output = added(mixed, out_own, out_other)

    down_own = expert.down_outer(after(tuple(acts), wi_kept), cot_pieces, 0, True)
    up_back = expert.fill(up_own, up_got)
    down_back = expert.fill(down_own, down_got)
    tails = vector[5:].reshape(-1)
    bias_sum = tails[5 * head_width : 7 * head_width]
    bias_sum = bias_sum.reshape(2, head_width // HEAD_DIM, n, HEAD_DIM // n)
    input_bias_back = lax.dynamic_index_in_dim(bias_sum, g, axis=2, keepdims=False)
    vector = after(vector, up_back, down_back, block_output, output_weight_back)
    vector = added(vector, send_tp(vector, 1), dtype=f32)
    vector = added(vector, send_tp(vector, 2), dtype=f32)
    tails = vector[5:].reshape(-1)[: 5 * head_width].reshape(5, head_width)
    vectors = jnp.concatenate([vector[:5], tails], axis=1)
    back_residual = plain_call(
        last_kernel,
        [residual_in, row(first_norm_gain), sum0, got2, after(mixed_back, vectors)],
        [struct((rows, width), f32)],
    )[0]

    first_gain_back = (vectors[0] - first_norm_shift * vectors[1]) / first_norm_gain
    return (
        block_output,
        back_residual,
        first_gain_back,
        vectors[1],
        wi_total,
        input_bias_back,
        output_weight_back,
        vectors[4],
        vectors[2],
        vectors[3],
        up_back,
        up_bias_back,
        down_back,
        down_bias_back,
    )


def solution(mesh):
    in_specs = (
        P(("fsdp", "tp"), None),
        P(("fsdp", "tp"), None),
        P(("fsdp", "tp"), None),
        P("fsdp", "tp"),
        P("fsdp", None),
        P(),
        P(),
        P("fsdp", None, "tp"),
        P(None, "tp", "fsdp"),
        P("tp", "fsdp"),
        P(),
        P(),
        P(),
        P("fsdp", None, "tp"),
        P("fsdp", "tp"),
        P("fsdp", "tp", None),
        P("fsdp", None),
    )
    out_specs = (
        P(("fsdp", "tp"), None),
        P(("fsdp", "tp"), None),
        P(),
        P(),
        P("fsdp", None, "tp"),
        P(None, "tp", "fsdp"),
        P("tp", "fsdp"),
        P(),
        P(),
        P(),
        P("fsdp", None, "tp"),
        P("fsdp", "tp"),
        P("fsdp", "tp", None),
        P("fsdp", None),
    )
    return jax.shard_map(local, mesh=mesh, in_specs=in_specs, out_specs=out_specs, check_vma=False)
```

```python
import functools

import jax
import jax.numpy as jnp
from jax import lax
from jax.experimental import pallas as pl
from jax.experimental.pallas import tpu as pltpu
from jax.sharding import PartitionSpec as P

f32 = jnp.float32
bf16 = jnp.bfloat16
i32 = jnp.int32

HEAD_DIM = 64
PIECE = 256
DOCS = 4
TP = 4
BLOCK_K = 256
EXTRA = 16
EPSILON = 1e-05
MASKED = -1e30
VMEM = 60 << 20

NN = (((1,), (0,)), ((), ()))
NT = (((1,), (1,)), ((), ()))
TN = (((0,), (0,)), ((), ()))


def mxu(a, b, dims=NN):
    return lax.dot_general(a, b, dims, preferred_element_type=f32)


TIMES = {
    "attend": 15,
    "middle_kernel": 5,
    "place_kernel": 3,
    "attend_back": 19,
    "project_kernel": 7,
    "halves_kernel": 5,
    "act_back_kernel": 9,
    "expert_kernel": 10,
    "expert_out_kernel": 9,
    "up_outer_kernel": 9,
    "down_outer_kernel": 9,
    "output_weight_kernel": 4,
    "out_sum_kernel": 4,
    "input_weight_kernel": 9,
    "input_back_kernel": 5,
}


def cost(name, part=1.0):
    flops = int(part * TIMES.get(name, 0) * 1.1e9) + 1
    return pl.CostEstimate(flops=flops, bytes_accessed=1, transcendentals=0)


def whole_spec(x):
    return pl.BlockSpec(x.shape, lambda *_: (0,) * x.ndim)


def smem_spec():
    return pl.BlockSpec(memory_space=pltpu.SMEM)


def kernel_name(kernel):
    return getattr(kernel, "func", kernel).__name__


def plain_call(kernel, ins, outs, scratch=(), scalars=()):
    return pl.pallas_call(
        kernel,
        name=kernel_name(kernel),
        grid=(1,),
        in_specs=[smem_spec() for _ in scalars] + [whole_spec(x) for x in ins],
        out_specs=[whole_spec(x) for x in outs],
        out_shape=list(outs),
        scratch_shapes=list(scratch),
        compiler_params=pltpu.CompilerParams(vmem_limit_bytes=VMEM),
        cost_estimate=cost(kernel_name(kernel)),
    )(*scalars, *ins)


def struct(shape, dtype):
    return jax.ShapeDtypeStruct(shape, dtype)


def send_tp(x, turn):
    return lax.ppermute(x, "tp", [(i, i ^ turn) for i in range(TP)])


def send_fsdp(x, turn):
    n = lax.axis_size("fsdp")
    return lax.ppermute(x, "fsdp", [(i, i ^ turn) for i in range(n)])


def after(x, *firsts):
    return lax.optimization_barrier((x, firsts))[0]


def sum_kernel(*refs):
    total = refs[0][...].astype(f32)
    for ref in refs[1:-1]:
        total = total + ref[...].astype(f32)
    refs[-1][...] = total.astype(refs[-1].dtype)


def added(*parts, dtype=bf16):
    return plain_call(sum_kernel, parts, [struct(parts[0].shape, dtype)])[0]


def turned_sum_kernel(blocks, out):
    rows = out.shape[1]
    total = blocks[:rows, :].astype(f32)
    for at in range(rows, blocks.shape[0], rows):
        total = total + blocks[at : at + rows, :].astype(f32)
    out[...] = total.T


def two_parts(x):
    high = x.astype(bf16)
    return jnp.concatenate([high, (x - high.astype(f32)).astype(bf16)], axis=0)


def one_part(x):
    x = x.astype(f32)
    return x[: x.shape[0] // 2] + x[x.shape[0] // 2 :]


def fold_kernel(own, vector, got, kept, vectors, *outs):
    rows = kept.shape[0]
    size = own.shape[0]
    kept[...] = own[:rows, :].astype(f32) + got[:rows, :].astype(f32)
    vectors[...] = vector[...] + one_part(got[size:, :])
    parts = two_parts(vectors[...])
    for at, out in enumerate(outs):
        here = slice((at + 1) * rows, (at + 2) * rows)
        out[:rows, :] = (own[here, :].astype(f32) + got[here, :].astype(f32)).astype(bf16)
        out[rows:, :] = parts


def last_fold_kernel(kept, vector, *refs):
    out, vectors = refs[-2:]
    rows, width = out.shape[1:]
    total = kept[...]
    sums = vector[...]
    for ref in refs[:-2]:
        total = total + ref[:rows, :].astype(f32)
        sums = sums + one_part(ref[rows:, :])
    for j in range(out.shape[0]):
        out[j] = total[:, j * width : (j + 1) * width]
    vectors[...] = sums


def normed(values):
    centered = values - jnp.mean(values, axis=-1, keepdims=True)
    inverse = lax.rsqrt(jnp.mean(centered * centered, axis=-1, keepdims=True) + EPSILON)
    return centered * inverse, inverse


def norm_back(incoming, unit, inverse, gain):
    scaled = incoming * gain
    return inverse * (
        scaled
        - jnp.mean(scaled, axis=-1, keepdims=True)
        - unit * jnp.mean(scaled * unit, axis=-1, keepdims=True)
    )


def first_kernel(x, gain, shift, docs, w_in, w_out, bias, out, packed, copies):
    rows = x.shape[0]
    unit, _ = normed(x[...].astype(f32))
    out[:rows, :] = (unit * gain[...] + shift[...]).astype(bf16)
    out[rows:, :] = jnp.zeros_like(out[rows:, :])
    out[rows : rows + EXTRA, :rows] = jnp.broadcast_to(
        docs[...].astype(f32), (EXTRA, rows)
    ).astype(bf16)
    shard, width = w_in.shape[1:]
    for j in range(3):
        packed[:shard, j * width : (j + 1) * width] = w_in[j]
    turned = w_out[...].T
    for at in range(0, copies.shape[0], shard):
        copies[at : at + shard, :] = turned
    packed[shard:, :] = jnp.zeros_like(packed[shard:, :])
    packed[shard:, :width] = bias[...]


def slots_kernel(cap, place, ids, cot, slots, sent):
    rows = ids.shape[0]
    column = ids[...].astype(f32)
    across = jnp.broadcast_to(column, (rows, 128)).T[:1]
    before = lax.broadcasted_iota(i32, (rows, rows), 0) < lax.broadcasted_iota(i32, (rows, rows), 1)
    rank = jnp.sum(jnp.where(before & (column == across), 1.0, 0.0), axis=0, keepdims=True)
    rank = rank.astype(i32)
    expert = across.astype(i32)
    mine = (expert & 1) == (place[1] & 1)
    own = (expert >> 1) * cap + rank
    slots[...] = jnp.broadcast_to(jnp.where(mine, own, -1), slots.shape)
    sent[:rows, :] = cot[...]
    sent[rows:, :] = jnp.zeros_like(sent[rows:, :])
    meta = [jnp.where(mine, -1, v).astype(f32) for v in (expert >> 1, rank)]
    meta += [jnp.zeros((EXTRA - 2, rows), f32)]
    sent[rows:, :rows] = jnp.concatenate(meta, axis=0).astype(bf16)


def other_slots_kernel(cap, sent, slots, out):
    rows = slots.shape[1]
    meta = sent[rows:, :rows].astype(f32)
    group, rank = meta[0:1].astype(i32), meta[1:2].astype(i32)
    named = group >= 0
    own = jnp.where(named, group * cap + rank, -1)
    slots[...] = jnp.broadcast_to(own, slots.shape)
    spots = lax.broadcasted_iota(i32, (out.shape[0], rows), 0)
    out[...] = mxu(jnp.where(spots == own, 1.0, 0.0).astype(bf16), sent[:rows, :]).astype(bf16)


def project_kernel(n, rows, place, *refs):
    xs, ws = refs[:TP], refs[TP : TP + n]
    q, k, v, w_in = refs[TP + n :]
    width = q.shape[1]
    bias = jnp.zeros((8, width), f32)
    lane = lax.rem(lax.broadcasted_iota(i32, (8, width), 1), HEAD_DIM) // (HEAD_DIM // n)
    for turn in range(n):
        base = pl.multiple_of((place[0] ^ turn) * rows, rows)
        w_in[pl.ds(base, rows), :] = ws[turn][:rows, :]
        part = ws[turn][rows:, :width].astype(f32)[:8]
        bias = jnp.where(lane == (place[0] ^ turn), part, bias)
    block = q.shape[0] // TP
    for r in range(TP):
        x = xs[r][:block, :]
        here = pl.ds(r * block, block)
        q[here, :] = ((mxu(x, w_in[:, :width]) + bias[0:1, :]) * 0.125).astype(bf16)
        k[here, :] = mxu(x, w_in[:, width : 2 * width]).astype(bf16)
        v[here, :] = (mxu(x, w_in[:, 2 * width :]) + bias[1:2, :]).astype(bf16)


def middle_kernel(*refs):
    ctxs, ws = refs[:TP], refs[TP : 2 * TP]
    residual, bias, gain, shift, mixed, second, upper, lower = refs[-8:]
    total = residual[...].astype(f32) + bias[...]
    for r in range(TP):
        total = total + mxu(ctxs[r][...], ws[r][...], NT)
    mixed[...] = total
    unit, _ = normed(total)
    second[...] = (unit * gain[...] + shift[...]).astype(bf16)
    half = upper.shape[0]
    upper[...] = second[:half, :]
    lower[...] = second[half:, :]


def turn_kernel(*refs):
    ws = refs[:TP]
    own, other, mixed, cot, gain = refs[TP : TP + 5]
    back, low, sums = refs[TP + 5 : TP + 8]
    outs = refs[TP + 8 :]
    unit, inverse = normed(mixed[...])
    second_back = own[...].astype(f32) + other[...].astype(f32)
    total = cot[...].astype(f32) + norm_back(second_back, unit, inverse, gain[...])
    back[...] = total
    low[...] = total.astype(bf16)
    sums[...] = jnp.concatenate(
        [
            jnp.sum(second_back * unit, axis=0, keepdims=True),
            jnp.sum(second_back, axis=0, keepdims=True),
            jnp.sum(total, axis=0, keepdims=True),
            jnp.zeros((5, total.shape[1]), f32),
        ],
        axis=0,
    )
    for r in range(TP):
        outs[r][...] = mxu(low[...], ws[r][...]).astype(bf16)


def output_weight_kernel(*refs):
    ctxs, low, kept, away = refs[:TP], refs[TP], refs[TP + 1], refs[TP + 2]
    size = low.shape[1]
    for r in range(TP):
        out = away if r & 1 else kept
        to = (r // 2) * size
        out[to : to + size, :] = mxu(low[...], ctxs[r][...], TN).astype(bf16)


def pair_sum_kernel(a, b, here, there):
    size = here.shape[0]
    for at, out in enumerate((here, there)):
        rows = slice(at * size, (at + 1) * size)
        out[...] = (a[rows, :].astype(f32) + b[rows, :].astype(f32)).astype(bf16)


def input_back_kernel(count, turns, *refs):
    backs, w_in, outs = refs[:count], refs[count], refs[count + 1 :]
    pairs = count // 3
    width = w_in.shape[1] // 3
    block = outs[0].shape[0]
    for at, r in enumerate(turns):
        here = pl.ds(r * block, block)
        total = None
        for j in range(3):
            back = jnp.concatenate([backs[3 * p + j][here, :] for p in range(pairs)], axis=1)
            part = mxu(back, w_in[:, j * width : (j + 1) * width], NT)
            total = part if total is None else total + part
        outs[at][...] = total.astype(bf16)


def lane_sums(x):
    total = jnp.sum(x, axis=1, keepdims=True)
    return jnp.broadcast_to(total, (x.shape[0], 128)).T[:8]


def input_weight_kernel(n, rows, count, place, *refs):
    xs, backs, w_in, sums2 = refs[:TP], refs[TP : TP + count], refs[TP + count], refs[TP + count + 1]
    keep, away, vectors, small, total = refs[TP + count + 2 :]
    pairs = count // 3
    width = w_in.shape[1] // 3
    block = backs[0].shape[0] // TP
    ones = jnp.ones((8, block), bf16)
    for j in range(3):
        part = jnp.zeros((total.shape[0], width), f32)
        column = jnp.zeros((8, width), f32)
        for r in range(TP):
            here = pl.ds(r * block, block)
            back = jnp.concatenate([backs[3 * p + j][here, :] for p in range(pairs)], axis=1)
            part += mxu(xs[r][:block, :], back, TN)
            column += mxu(ones, back)
        total[:, j * width : (j + 1) * width] = part
        small[8 * j : 8 * j + 8, :] = column
    for turn in range(n):
        base = pl.multiple_of((place[0] ^ turn) * rows, rows)
        dest = away if turn % 2 else keep
        to = turn // 2 * rows
        dest[to : to + rows, :] = total[pl.ds(base, rows), :].astype(bf16)
    w = w_in[...].astype(f32)
    column = jnp.concatenate([small[8 * j : 8 * j + 1, :] for j in range(3)], axis=1)
    lines = [lane_sums(total[...] * w)[:1], lane_sums(w * column)[:1]]
    lines += [sums2[r : r + 1, :] for r in range(3)]
    for r, line in enumerate(lines):
        vectors[r : r + 1, :] = line[:, : 3 * width]
    rests = [line[:, 3 * width :] for line in lines]
    rests += [small[0:1, :], small[16:17, :], jnp.zeros((1, 2 * width), f32)]
    rests = jnp.concatenate(rests, axis=1)
    for r in range(3):
        vectors[5 + r : 6 + r, :] = rests[:, 3 * width * r : 3 * width * (r + 1)]
    away[n // 2 * rows :, :] = two_parts(vectors[...])


def last_kernel(residual, gain, own, other, mixed_back, out):
    unit, inverse = normed(residual[...].astype(f32))
    first_back = own[...].astype(f32) + other[...].astype(f32)
    out[...] = mixed_back[...] + norm_back(first_back, unit, inverse, gain[...])


def half_rows(x, h):
    rows = lax.broadcasted_iota(i32, x.shape, 0)
    keep = (rows < HEAD_DIM) if h == 0 else (rows >= HEAD_DIM)
    return jnp.where(keep, x, jnp.zeros_like(x))


def half_lanes(x, h):
    lanes = lax.broadcasted_iota(i32, x.shape, 1)
    keep = (lanes < HEAD_DIM) if h == 0 else (lanes >= HEAD_DIM)
    return jnp.where(keep, x, jnp.zeros_like(x))


def key_base(kb, block, t):
    per = block // BLOCK_K
    return pl.multiple_of(((kb // per) ^ t) * block + lax.rem(kb, per) * BLOCK_K, BLOCK_K)


def attend_kernel(t_ref, q_ref, k_ref, v_ref, a_ref, b_ref, *rest):
    outs, lse_ref, vt = rest[-TP - 2 : -2], rest[-2], rest[-1]
    i = pl.program_id(0)
    bq = q_ref.shape[0]
    bk = BLOCK_K

    @pl.when(i == 0)
    def _():
        vt[...] = v_ref[...].T

    qt = q_ref[...].T
    qz = [half_rows(qt, h) for h in (0, 1)]
    a = a_ref[...]
    b = b_ref[...]

    def body(kb, carry):
        base = key_base(kb, bq, t_ref[0])
        kblk = k_ref[pl.ds(base, bk), :]
        j = kb * bk + lax.broadcasted_iota(i32, (bk, bq), 0)
        mask = (j >= a) & (j <= b)
        out = []
        for h in (0, 1):
            m, l, acc = carry[h]
            s = jnp.where(mask, mxu(kblk, qz[h]), MASKED)
            mn = jnp.maximum(m, jnp.max(s, axis=0, keepdims=True))
            p = jnp.exp(s - mn)
            al = jnp.exp(m - mn)
            l = al * l + jnp.sum(p, axis=0, keepdims=True)
            acc = acc * al + mxu(
                vt[pl.ds(HEAD_DIM * h, HEAD_DIM), pl.ds(base, bk)], p.astype(bf16)
            )
            out.append((mn, l, acc))
        return tuple(out)

    init = tuple(
        (jnp.full((1, bq), MASKED, f32), jnp.zeros((1, bq), f32), jnp.zeros((HEAD_DIM, bq), f32))
        for _ in (0, 1)
    )
    res = lax.fori_loop(jnp.min(a) // bk, jnp.max(b) // bk + 1, body, init)
    ot = jnp.concatenate([acc / l for m, l, acc in res], axis=0)
    o = ot.T.astype(bf16)
    for r in range(TP):

        @pl.when(i == r)
        def _(r=r):
            outs[r][...] = o

    lse_ref[...] = jnp.concatenate(
        [m + jnp.log(l) for m, l, acc in res] + [jnp.zeros((6, bq), f32)], axis=0
    )


def attention_fwd(pair, q, k, v, a, b, t, before):
    S, W = q.shape
    bq = S // TP
    whole = pl.BlockSpec((S, 128), lambda i, *_: (0, pair))
    row = pl.BlockSpec((1, bq), lambda i, *_: (0, i))
    return pl.pallas_call(
        attend_kernel,
        name="attend",
        grid_spec=pltpu.PrefetchScalarGridSpec(
            num_scalar_prefetch=1,
            grid=(TP,),
            in_specs=[pl.BlockSpec((bq, 128), lambda i, *_: (i, pair)), whole, whole, row, row]
            + [pl.BlockSpec(memory_space=pl.ANY)] * len(before),
            out_specs=[pl.BlockSpec((bq, 128), lambda i, *_: (0, pair))] * TP
            + [pl.BlockSpec((8, bq), lambda i, *_: (0, i))],
            scratch_shapes=[pltpu.VMEM((128, S), bf16)],
        ),
        out_shape=[struct((bq, W), bf16)] * TP + [struct((8, S), f32)],
        input_output_aliases={6 + r: r for r in range(len(before))},
        compiler_params=pltpu.CompilerParams(vmem_limit_bytes=VMEM),
        cost_estimate=cost("attend"),
    )(t, q, k, v, a, b, *before)


def attend_back_kernel(t_ref, q_ref, k_ref, v_ref, *rest):
    dos, os = rest[:TP], rest[TP : 2 * TP]
    lse_ref, a_ref, b_ref, dq_ref, dk_ref, dv_ref, kt, dk_acc, dv_acc, do_s, o_s = rest[2 * TP :]
    i = pl.program_id(0)
    bq = q_ref.shape[0]
    bk = BLOCK_K

    @pl.when(i == 0)
    def _():
        kt[...] = k_ref[...].T
        dk_acc[...] = jnp.zeros_like(dk_acc)
        dv_acc[...] = jnp.zeros_like(dv_acc)

    for r in range(TP):

        @pl.when(i == r)
        def _(r=r):
            do_s[...] = dos[r][...]
            o_s[...] = os[r][...]

    q = q_ref[...]
    do = do_s[...]
    qt = q.T
    dot_ = do.T
    qz = [half_rows(qt, h) for h in (0, 1)]
    dz = [half_rows(dot_, h) for h in (0, 1)]
    qcat = jnp.concatenate([half_lanes(q, 0), half_lanes(q, 1)], axis=0)
    dcat = jnp.concatenate([half_lanes(do, 0), half_lanes(do, 1)], axis=0)
    prod = (do.astype(f32) * o_s[...].astype(f32)).T
    delta = [
        jnp.sum(prod[:HEAD_DIM], axis=0, keepdims=True),
        jnp.sum(prod[HEAD_DIM:], axis=0, keepdims=True),
    ]
    lse = [lse_ref[0:1, :], lse_ref[1:2, :]]
    a = a_ref[...]
    b = b_ref[...]

    def body(kb, carry):
        base = key_base(kb, bq, t_ref[0])
        here = pl.ds(base, bk)
        kblk = k_ref[here, :]
        vblk = v_ref[here, :]
        j = kb * bk + lax.broadcasted_iota(i32, (bk, bq), 0)
        mask = (j >= a) & (j <= b)
        ps, dss, out = [], [], []
        for h in (0, 1):
            p = jnp.exp(jnp.where(mask, mxu(kblk, qz[h]) - lse[h], MASKED))
            ds = (p * (mxu(vblk, dz[h]) - delta[h])).astype(bf16)
            ps.append(p.astype(bf16))
            dss.append(ds)
            out.append(carry[h] + mxu(kt[pl.ds(HEAD_DIM * h, HEAD_DIM), here], ds))
        dv_acc[here, :] += mxu(jnp.concatenate(ps, axis=1), dcat)
        dk_acc[here, :] += mxu(jnp.concatenate(dss, axis=1), qcat)
        return tuple(out)

    init = tuple(jnp.zeros((HEAD_DIM, bq), f32) for _ in (0, 1))
    dqt = lax.fori_loop(jnp.min(a) // bk, jnp.max(b) // bk + 1, body, init)
    dq_ref[...] = (jnp.concatenate(dqt, axis=0).T * 0.125).astype(bf16)

    @pl.when(i == TP - 1)
    def _():
        dk_ref[...] = dk_acc[...].astype(bf16)
        dv_ref[...] = dv_acc[...].astype(bf16)


def attention_bwd(pair, q, k, v, dos, os, lse, a, b, t):
    S = q.shape[0]
    bq = S // TP
    context = pl.BlockSpec((bq, 128), lambda i, *_: (0, pair))
    whole = pl.BlockSpec((S, 128), lambda i, *_: (0, pair))
    out = pl.BlockSpec((S, 128), lambda i, *_: (0, 0))
    row = pl.BlockSpec((1, bq), lambda i, *_: (0, i))
    return pl.pallas_call(
        attend_back_kernel,
        name="attend_back",
        grid_spec=pltpu.PrefetchScalarGridSpec(
            num_scalar_prefetch=1,
            grid=(TP,),
            in_specs=[pl.BlockSpec((bq, 128), lambda i, *_: (i, pair)), whole, whole]
            + [context] * (2 * TP)
            + [pl.BlockSpec((8, bq), lambda i, *_: (0, i)), row, row],
            out_specs=[pl.BlockSpec((bq, 128), lambda i, *_: (i, 0)), out, out],
            scratch_shapes=[
                pltpu.VMEM((128, S), bf16),
                pltpu.VMEM((S, 128), f32),
                pltpu.VMEM((S, 128), f32),
                pltpu.VMEM((bq, 128), bf16),
                pltpu.VMEM((bq, 128), bf16),
            ],
        ),
        out_shape=[struct((S, 128), bf16)] * 3,
        compiler_params=pltpu.CompilerParams(vmem_limit_bytes=VMEM),
        cost_estimate=cost("attend_back"),
    )(t, q, k, v, *dos, *os, lse, a, b)


def intervals_kernel(place, starts, *refs):
    first, end = refs[TP:]
    rows = first.shape[1] // TP
    docs = [ref[0:1, :rows].astype(f32) for ref in refs[:TP]]
    bounds = [jnp.zeros((1, 1), f32)]
    for number in range(DOCS):
        here = sum(jnp.sum(jnp.where(d == number, 1.0, 0.0), axis=1, keepdims=True) for d in docs)
        bounds.append(bounds[-1] + here)
    for r in range(TP):
        low = jnp.zeros((1, rows), f32)
        last = jnp.zeros((1, rows), f32)
        for number in range(DOCS):
            here = docs[r] == number
            low = jnp.where(here, bounds[number], low)
            last = jnp.where(here, bounds[number + 1] - 1.0, last)
        spot = (place[1] ^ r) * rows + lax.broadcasted_iota(i32, (1, rows), 1)
        piece_last = jnp.full((1, rows), -1, i32)
        for p in range(2):
            inside = (spot >= starts[0, p]) & (spot < starts[0, p] + PIECE)
            piece_last = jnp.where(inside, starts[0, p] + PIECE - 1, piece_last)
        first[:, r * rows : (r + 1) * rows] = low.astype(i32)
        end[:, r * rows : (r + 1) * rows] = jnp.maximum(
            spot, jnp.minimum(piece_last, last.astype(i32))
        )


def intervals(here, starts, xs, rows):
    tail = pl.BlockSpec((EXTRA, xs[0].shape[1]), lambda i: (rows // EXTRA, 0))
    out = struct((1, TP * rows), i32)
    return pl.pallas_call(
        intervals_kernel,
        name="intervals",
        grid=(1,),
        in_specs=[smem_spec(), smem_spec()] + [tail] * TP,
        out_specs=[whole_spec(out)] * 2,
        out_shape=[out] * 2,
        cost_estimate=cost("intervals"),
    )(here, starts, *xs)


def place_halves_kernel(upper, lower, s, out):
    spots = lax.broadcasted_iota(i32, (out.shape[0], s.shape[1]), 0)
    pick = jnp.where(spots == s[0:1, :], 1.0, 0.0).astype(bf16)
    half = upper.shape[0]
    total = mxu(pick[:, :half], upper[...]) + mxu(pick[:, half:], lower[...])
    out[...] = total.astype(bf16)


def place_kernel(x, s, out):
    spots = lax.broadcasted_iota(i32, (out.shape[0], s.shape[1]), 0)
    pick = jnp.where(spots == s[0:1, :], 1.0, 0.0).astype(bf16)
    out[...] = mxu(pick, x[...]).astype(bf16)


def collect_kernel(s_own, s_other, own_rows, other_rows, own, other):
    slots = lax.broadcasted_iota(i32, (own_rows.shape[0], own.shape[0]), 0)
    for s, rows, out in ((s_own, own_rows, own), (s_other, other_rows, other)):
        pick = jnp.where(slots == s[0:1, :], 1.0, 0.0).astype(bf16)
        out[...] = mxu(pick, rows[...], TN).astype(bf16)


def collect(s_own, s_other, own_rows, other_rows):
    rows, width = s_own.shape[1], own_rows.shape[1]
    return plain_call(
        collect_kernel,
        [s_own, s_other, own_rows, other_rows],
        [struct((rows, width), bf16)] * 2,
    )


def act_back_kernel(lo, near, far, down_a, down_b, out_near, out_far, sums):
    hidden = down_a.shape[0]
    half = pl.num_programs(0) // 2
    for at, (x, out) in enumerate(((near, out_near), (far, out_far))):

        @pl.when(pl.program_id(0) // half == at)
        def _(x=x, out=out):
            act_back_tile(hidden, x, down_a, down_b, out, sums)


def act_back_tile(hidden, x, down_a, down_b, out, sums):
    for j, down in enumerate((down_a, down_b)):
        out[:, j * hidden : (j + 1) * hidden] = mxu(x[...], down[...], NT).astype(bf16)
    total = mxu(jnp.ones((8, x.shape[0]), bf16), x[...])

    @pl.when(pl.program_id(0) == 0)
    def _():
        sums[...] = jnp.zeros_like(sums)

    sums[...] += total


def expert_kernel(lo, x, act_back, up_a, up_b, bias_a, bias_b, act, pre_back, x_back):
    width = up_a.shape[1]
    total = None
    for j, (up, bias) in enumerate(((up_a, bias_a), (up_b, bias_b))):
        here = slice(j * width, (j + 1) * width)
        pre = mxu(x[...], up[...]) + bias[...]
        square = pre * pre
        tan = jnp.tanh(0.7978845608028654 * pre * (1.0 + 0.044715 * square))
        half = 0.5 + 0.5 * tan
        act[:, here] = (pre * half).astype(bf16)
        slope = half + (0.5 * pre) * (1.0 - tan * tan) * (
            0.7978845608028654 + 0.1070322243 * square
        )
        low = (act_back[:, here].astype(f32) * slope).astype(bf16)
        pre_back[:, here] = low
        part = mxu(low, up[...], NT)
        total = part if total is None else total + part
    x_back[...] = total.astype(bf16)


def expert_out_kernel(lo, act_0, act_1, down_a, down_b, out):
    hidden = down_a.shape[0]
    half = pl.num_programs(0) // 2
    for at, act in enumerate((act_0, act_1)):

        @pl.when(pl.program_id(0) // half == at)
        def _(act=act):
            total = mxu(act[:, :hidden], down_a[...]) + mxu(act[:, hidden:], down_b[...])
            out[...] = total.astype(bf16)


def out_sum_kernel(cap, near, far, bias, out):
    half = near.shape[0] // 2
    for at in range(half // cap):
        for core in range(2):
            here = slice(core * half + at * cap, core * half + (at + 1) * cap)
            to = (2 * at + core) * cap
            total = near[here, :].astype(f32) + far[here, :].astype(f32) + bias[...]
            out[to : to + cap, :] = total.astype(bf16)


def collect_both_kernel(cap, s_own, s_other, both, own, other):
    slots = lax.broadcasted_iota(i32, (both.shape[0] // 2, own.shape[0]), 0)
    for core, (s, out) in enumerate(((s_own, own), (s_other, other))):
        pick = jnp.where(slots == s[0:1, :], 1.0, 0.0).astype(bf16)
        rows = jnp.concatenate(
            [both[at : at + cap, :] for at in range(core * cap, both.shape[0], 2 * cap)], axis=0
        )
        out[...] = mxu(pick, rows, TN).astype(bf16)


def up_outer_kernel(count, lo, *refs):
    left = jnp.concatenate([r[...] for r in refs[:count]], axis=0)
    right = jnp.concatenate([r[...] for r in refs[count:-2]], axis=0)
    out, sums = refs[-2:]
    out[...] = mxu(left, right, TN).astype(out.dtype)
    sums[...] = mxu(jnp.ones((8, right.shape[0]), bf16), right)


def down_outer_kernel(count, lo, *refs):
    left = jnp.concatenate([r[...] for r in refs[:count]], axis=0)
    right = jnp.concatenate([r[...] for r in refs[count:-1]], axis=0)
    refs[-1][...] = mxu(left, right, TN).astype(refs[-1].dtype)


def halves_kernel(lo, up, down, out):
    out[0] = up[...]
    out[1] = down[...]


def fill_kernel(lo, up, down, up_other, down_other, up_out, down_out):
    up_out[...] = up_other[...].astype(f32)
    down_out[...] = down_other[...].astype(f32)


class Expert:
    def __init__(self, lo, width, hidden):
        self.lo = jnp.reshape(lo, (1,)).astype(i32)
        self.width, self.hidden = width, hidden
        self.tile = 256

    def hold(self, up, up_bias, up_bias_other, down, other):
        self.up, self.down, self.other = up, down, other
        self.up_bias, self.up_bias_other = up_bias[:, None, :], up_bias_other

    def call(self, kernel, grid, in_specs, out_specs, out_shape, args, alias=None, scratch=(), part=1.0):
        return pl.pallas_call(
            kernel,
            name=kernel_name(kernel),
            grid_spec=pltpu.PrefetchScalarGridSpec(
                num_scalar_prefetch=1,
                grid=grid,
                in_specs=in_specs,
                out_specs=out_specs,
                scratch_shapes=list(scratch),
            ),
            out_shape=out_shape,
            input_output_aliases=alias or {},
            compiler_params=pltpu.CompilerParams(vmem_limit_bytes=VMEM),
            cost_estimate=cost(kernel_name(kernel), part),
        )(self.lo, *args)

    def away(self, at):
        return pl.BlockSpec((None,) + self.other.shape[1:], lambda i, lo: (at, 0, 0))

    def own(self, x):
        return pl.BlockSpec((None,) + x.shape[1:], lambda i, lo: (lo[0], 0, 0))

    def row(self, columns):
        return pl.BlockSpec((self.tile, columns), lambda i, lo: (i, 0))

    def two(self, columns, steps):
        return [
            pl.BlockSpec((self.tile, columns), lambda i, lo: (jnp.minimum(i, steps - 1), 0)),
            pl.BlockSpec((self.tile, columns), lambda i, lo: (jnp.maximum(i - steps, 0), 0)),
        ]

    def act_back(self, near, far):
        rows = near.shape[0]
        steps = rows // self.tile
        return self.call(
            act_back_kernel,
            (2 * steps,),
            self.two(self.width, steps) + [self.own(self.down), self.away(1)],
            self.two(2 * self.hidden, steps)
            + [pl.BlockSpec((8, self.width), lambda i, lo: (0, 0))],
            [struct((rows, 2 * self.hidden), bf16)] * 2 + [struct((8, self.width), f32)],
            [near, far, self.down, self.other],
        )

    def rows(self, x, act_back):
        rows = x.shape[0]
        wide = self.row(2 * self.hidden)
        return self.call(
            expert_kernel,
            (rows // self.tile,),
            [
                self.row(self.width),
                wide,
                self.own(self.up),
                self.away(0),
                self.own(self.up_bias),
                whole_spec(self.up_bias_other),
            ],
            [wide, wide, self.row(self.width)],
            [struct((rows, 2 * self.hidden), bf16)] * 2 + [struct((rows, self.width), bf16)],
            [x, act_back, self.up, self.other, self.up_bias, self.up_bias_other],
        )

    def out(self, act_0, act_1, part=1.0):
        rows = act_0.shape[0]
        steps = rows // self.tile
        return self.call(
            expert_out_kernel,
            (2 * steps,),
            self.two(2 * self.hidden, steps) + [self.own(self.down), self.away(1)],
            self.row(self.width),
            struct((2 * rows, self.width), bf16),
            [act_0, act_1, self.down, self.other],
            part=part,
        )

    def outer_specs(self, own):
        size, tile = self.width, 512
        if own:
            out = pl.BlockSpec((None, tile, size), lambda i, lo: (lo[0], i, 0))
            return out, struct((2, size, size), f32)
        return pl.BlockSpec((tile, size), lambda i, lo: (i, 0)), struct((size, size), bf16)

    def up_outer(self, xs, backs, at, own, part=1.0):
        size, count = self.width, len(xs)
        out, shape = self.outer_specs(own)
        return self.call(
            functools.partial(up_outer_kernel, count),
            (size // 512,),
            [pl.BlockSpec((xs[0].shape[0], 512), lambda i, lo: (0, i))] * count
            + [pl.BlockSpec((backs[0].shape[0], size), lambda i, lo: (0, at))] * len(backs),
            [out, pl.BlockSpec((8, size), lambda i, lo: (0, 0))],
            [shape, struct((8, size), f32)],
            list(xs) + list(backs),
            part=part,
        )

    def down_outer(self, acts, cots, at, own, part=1.0):
        rows, size, count = acts[0].shape[0], self.width, len(acts)
        out, shape = self.outer_specs(own)
        return self.call(
            functools.partial(down_outer_kernel, count),
            (size // 512,),
            [pl.BlockSpec((rows, 512), lambda i, lo: (0, at * (size // 512) + i))] * count
            + [whole_spec(c) for c in cots],
            out,
            shape,
            list(acts) + list(cots),
            part=part,
        )

    def halves(self, up, down):
        size = up.shape[1]
        part = pl.BlockSpec((None, size // 4, size), lambda i, lo: (1 - lo[0], i, 0))
        return self.call(
            halves_kernel,
            (4,),
            [part, part],
            pl.BlockSpec((2, size // 4, size), lambda i, lo: (0, i, 0)),
            struct((2, size, size), bf16),
            [up, down],
        )

    def fill(self, up, down, up_other, down_other):
        size = up_other.shape[0]
        part = pl.BlockSpec((size // 4, size), lambda i, lo: (i, 0))
        out = pl.BlockSpec((None, size // 4, size), lambda i, lo: (1 - lo[0], i, 0))
        return self.call(
            fill_kernel,
            (4,),
            [pl.BlockSpec(memory_space=pl.ANY)] * 2 + [part, part],
            [out, out],
            [struct(up.shape, f32), struct(down.shape, f32)],
            [up, down, up_other, down_other],
            alias={1: 0, 2: 1},
        )


def ordered(lo, own, other):
    return jnp.where(lo == 0, jnp.stack([own, other]), jnp.stack([other, own]))


def local(
    residual_in,
    out_cotangent,
    expert_index,
    document_index,
    piece_starts,
    first_norm_gain,
    first_norm_shift,
    input_weight,
    input_bias,
    output_weight,
    output_bias,
    second_norm_gain,
    second_norm_shift,
    expert_up,
    expert_up_bias,
    expert_down,
    expert_down_bias,
):
    rows, width = residual_in.shape
    n = lax.axis_size("fsdp")
    g = lax.axis_index("fsdp")
    t = lax.axis_index("tp")
    lo = t & 1
    place = jnp.reshape(g, (1,)).astype(i32)
    turn = jnp.reshape(t, (1,)).astype(i32)
    row = lambda v: v.reshape(1, -1)
    head_width = input_weight.shape[2]
    shard = input_weight.shape[0]
    cap = rows * 2 // (2 * n)
    evens = list(range(0, n, 2))

    expert = Expert(lo, width, expert_up.shape[2])

    def exchange(x):
        return lax.all_to_all(x, "fsdp", split_axis=0, concat_axis=0, tiled=True)

    share = jnp.pad(
        jnp.tile(input_bias, (1, 1, n)).reshape(2, head_width), ((0, EXTRA - 2), (0, 0))
    )
    x0, packed, copies = plain_call(
        first_kernel,
        [
            residual_in,
            row(first_norm_gain),
            row(first_norm_shift),
            document_index,
            jnp.transpose(input_weight, (1, 0, 2)),
            output_weight,
            share,
        ],
        [
            struct((rows + EXTRA, width), bf16),
            struct((shard + EXTRA, 3 * head_width), bf16),
            struct((n * shard, head_width), bf16),
        ],
    )
    x2 = send_tp(x0, 2)
    weights = {0: packed}
    for k in evens[1:]:
        weights[k] = send_fsdp(packed, k)
    weights[1] = send_fsdp(packed, 1)
    arrived = [weights[k] for k in evens[1:] + [1]]
    for k in evens[1:]:
        weights[k ^ 1] = send_fsdp(after(weights[k], arrived), 1)
    x1 = send_tp(after(x0, arrived), 1)
    x3 = send_tp(after(x2, arrived), 1)
    xs = [x0, x1, x2, x3]

    here = jnp.concatenate([place, turn])
    length = TP * rows
    first, end = intervals(here, piece_starts, xs, rows)
    s_own, cot_sent = plain_call(
        functools.partial(slots_kernel, cap),
        [after(expert_index, x1), out_cotangent],
        [struct((8, rows), i32), struct((rows + EXTRA, width), bf16)],
        scalars=[here],
    )

    slotted = struct((n * cap, width), bf16)
    cot_sent_own = plain_call(place_kernel, [out_cotangent, s_own], [slotted])[0]
    queries, keys, values, w_in = plain_call(
        functools.partial(project_kernel, n, shard),
        list(after(tuple(xs), cot_sent_own)) + [weights[k] for k in range(n)],
        [struct((length, head_width), bf16)] * 3 + [struct((width, 3 * head_width), bf16)],
        scalars=[place],
    )
    cot_other = send_tp(after(cot_sent, queries), 1)
    s_other, cot_sent_other = plain_call(
        functools.partial(other_slots_kernel, cap),
        [cot_other],
        [struct((8, rows), i32), slotted],
    )
    near_own = exchange(cot_sent_own)
    halves_sent = expert.halves(*after((expert_up, expert_down), queries))
    w_out0 = exchange(after(copies, near_own))

    halves_other = send_tp(after(halves_sent, queries), 1)
    down_bias = lax.dynamic_index_in_dim(expert_down_bias, lo, keepdims=True)

    w_out2 = send_tp(w_out0, 2)
    w_out1 = send_tp(w_out0, 1)
    pairs = head_width // 128
    contexts, totals = [], []
    firsts = [(near_own, halves_sent), (cot_other, w_out0)]
    cot_pieces = []
    for p in range(pairs):
        *contexts, total = attention_fwd(
            p,
            after(queries, firsts[min(p, 1)], totals),
            keys,
            values,
            first,
            end,
            turn,
            contexts,
        )
        if p == 0:
            near_other = exchange(after(cot_sent_other, w_out0, total))
            far_own = send_tp(near_own, 2)
            cot_pieces = [near_own, far_own, near_other, send_tp(near_other, 2)]
        totals.append(total)
    w_outs = [w_out0, w_out1, w_out2, send_tp(after(w_out2, total), 1)]
    ctxs = [contexts[0]] + [send_tp(contexts[r], r) for r in range(1, TP)]
    expert.hold(expert_up, expert_up_bias, None, expert_down, halves_other)
    act_backs, cot_sums = [None] * 4, [None] * 2
    act_backs[0], act_backs[1], cot_sums[0] = expert.act_back(*cot_pieces[:2])
    mixed, second, upper, lower = plain_call(
        middle_kernel,
        ctxs
        + w_outs
        + [
            after(residual_in, act_backs[0]),
            row(output_bias),
            row(second_norm_gain),
            row(second_norm_shift),
        ],
        [struct((rows, width), f32), struct((rows, width), bf16)]
        + [struct((rows // 2, width), bf16)] * 2,
    )

    bias_sent = lax.dynamic_index_in_dim(after(expert_up_bias, second), 1 - lo, keepdims=True)
    expert.hold(expert_up, expert_up_bias, send_tp(bias_sent, 1), expert_down, halves_other)
    act_backs[2], act_backs[3], cot_sums[1] = expert.act_back(*cot_pieces[2:])
    cot_sum = added(*cot_sums, dtype=f32)[:1]
    sent_own = plain_call(place_kernel, [second, s_own], [slotted])[0]
    sent_other = plain_call(
        place_halves_kernel, [send_tp(upper, 1), send_tp(lower, 1), s_other], [slotted]
    )[0]
    rows_own = exchange(after(sent_own, near_other))
    rows_other = exchange(after(sent_other, rows_own, cot_pieces[3]))
    pieces = [rows_own, send_tp(rows_own, 2), rows_other]
    acts, pre_backs, x_backs = [], [], []
    for at in range(4):
        act, pre_back, x_back = expert.rows(after(pieces[at], x_backs, act_backs[3]), act_backs[at])
        if at == 0:
            pieces.append(send_tp(after(rows_other, x_back), 2))
        acts.append(act)
        pre_backs.append(pre_back)
        x_backs.append(x_back)

    got_own = send_tp(x_backs[1], 2)
    got_other = send_tp(x_backs[3], 2)
    down_own = expert.down_outer(after(tuple(acts), x_backs[3]), cot_pieces, 0, True)
    back_sent_own = added(x_backs[0], after(got_own, down_own))
    back_home_own = exchange(back_sent_own)
    out_far = expert.out(*after((acts[1], acts[3]), back_sent_own))
    up_away, up_sum_away = expert.up_outer(pieces, after(tuple(pre_backs), out_far), 1, False)
    back_sent_other = added(x_backs[2], after(got_other, up_away))
    back_home_other = exchange(after(back_sent_other, back_home_own))
    out_got = send_tp(after(out_far, got_other), 2)
    late = after(tuple(acts), back_sent_other)
    down_away = expert.down_outer(late, cot_pieces, 1, False)
    out_near = expert.out(*after((acts[0], acts[2]), down_away), part=0.3)
    up_own, up_sum = expert.up_outer(pieces, after(tuple(pre_backs), out_near), 0, True, part=0.3)
    up_got, down_got = send_tp(up_away, 1), send_tp(down_away, 1)
    sent = send_tp(jnp.concatenate([up_sum_away[:1], cot_sum], axis=0), 1)
    back_own, back_away = collect(
        s_own, s_other, back_home_own, after(back_home_other, up_own, out_got, sent)
    )
    back_other = send_tp(back_away, 1)

    mixed_back, mixed_low, sums2, *ctx_backs = plain_call(
        turn_kernel,
        w_outs + [back_own, back_other, mixed, out_cotangent, row(second_norm_gain)],
        [
            struct((rows, width), f32),
            struct((rows, width), bf16),
            struct((8, width), f32),
        ]
        + [struct((rows, head_width), bf16)] * TP,
    )

    wo_kept, wo_away = plain_call(
        output_weight_kernel,
        ctxs + [mixed_low],
        [struct((2 * width, head_width), bf16)] * 2,
    )
    up_bias_back = ordered(lo, up_sum[0], sent[0])
    down_bias_back = ordered(lo, cot_sum[0], sent[1])

    dos = [ctx_backs[0]] + [send_tp(ctx_backs[r], r) for r in range(1, TP)]
    wo_sum, wo_there = plain_call(
        pair_sum_kernel,
        [wo_kept, send_tp(wo_away, 1)],
        [struct((width, head_width), bf16)] * 2,
    )
    wo_got = send_tp(wo_there, 2)
    out_sent = plain_call(
        functools.partial(out_sum_kernel, cap),
        [out_near, after(out_got, dos[0]), down_bias],
        [struct((2 * n * cap, width), bf16)],
    )[0]
    out_home = exchange(out_sent)
    projected_backs = []
    firsts = [(wo_sum, out_sent), None]
    for p in range(pairs):
        back = attention_bwd(
            p,
            after(queries, firsts[min(p, 1)], projected_backs),
            keys,
            values,
            dos,
            contexts,
            totals[p],
            first,
            end,
            turn,
        )
        projected_backs += back
        if p == 0:
            wo = added(wo_sum, after(wo_got, back))
            firsts[1] = (wo, up_got, down_got)

    def input_back(turns, first):
        return plain_call(
            functools.partial(input_back_kernel, 3 * pairs, turns),
            projected_backs + [after(w_in, first)],
            [struct((rows, width), bf16)] * 2,
        )

    part3, part2 = input_back((3, 2), projected_backs[0])
    got3 = send_tp(part3, 1)
    keep, away, vector = plain_call(
        functools.partial(input_weight_kernel, n, shard, 3 * pairs),
        xs + projected_backs + [after(w_in, part3), sums2],
        [
            struct((n // 2 * shard, 3 * head_width), bf16),
            struct((n // 2 * shard + EXTRA, 3 * head_width), bf16),
        ]
        + [struct((8, 3 * head_width), f32)],
        scratch=[
            pltpu.VMEM((24, head_width), f32),
            pltpu.VMEM((width, 3 * head_width), f32),
        ],
        scalars=[place],
    )
    got = send_fsdp(away, 1)
    part1, part0 = input_back((1, 0), keep)
    sum2 = added(part2, after(got3, keep))
    got2 = send_tp(sum2, 2)
    sum0 = added(part0, send_tp(part1, 1))
    out_own, out_away = plain_call(
        functools.partial(collect_both_kernel, cap),
        [s_own, s_other, after(out_home, part0)],
        [struct((rows, width), bf16)] * 2,
    )
    out_other = send_tp(out_away, 1)

    kept, vector, *folds = plain_call(
        fold_kernel,
        [keep, vector, after(got, out_own, sum2)],
        [struct((shard, 3 * head_width), f32), struct((8, 3 * head_width), f32)]
        + [struct((shard + EXTRA, 3 * head_width), bf16)] * (n // 2 - 1),
    )
    wi_kept = (kept, folds)
    wo_home = exchange(after(wo, out_own))
    output_weight_back = plain_call(
        turned_sum_kernel, [wo_home], [struct((head_width, shard), f32)]
    )[0]
    wi_total, vector = plain_call(
        last_fold_kernel,
        [kept, vector] + [send_fsdp(fold, k) for fold, k in zip(folds, evens[1:])],
        [struct((3, shard, head_width), f32), struct((8, 3 * head_width), f32)],
    )

    up_back, down_back = expert.fill(after(up_own, wi_kept), down_own, up_got, down_got)
    block_output = added(mixed, after(out_own, up_back), out_other)

    back_residual = plain_call(
        last_kernel,
        [residual_in, row(first_norm_gain), sum0, got2, mixed_back],
        [struct((rows, width), f32)],
    )[0]

    tails = vector[5:].reshape(-1)
    bias_sum = tails[5 * head_width : 7 * head_width]
    bias_sum = bias_sum.reshape(2, head_width // HEAD_DIM, n, HEAD_DIM // n)
    input_bias_back = lax.dynamic_index_in_dim(bias_sum, g, axis=2, keepdims=False)
    vector = after(vector, up_back, back_residual)
    vector = added(after(vector, block_output), send_tp(vector, 1), dtype=f32)
    vector = added(after(vector, output_weight_back), send_tp(vector, 2), dtype=f32)
    tails = vector[5:].reshape(-1)[: 5 * head_width].reshape(5, head_width)
    vectors = jnp.concatenate([vector[:5], tails], axis=1)
    first_gain_back = (vectors[0] - first_norm_shift * vectors[1]) / first_norm_gain
    return (
        block_output,
        back_residual,
        first_gain_back,
        vectors[1],
        jnp.transpose(wi_total, (1, 0, 2)),
        input_bias_back,
        output_weight_back,
        vectors[4],
        vectors[2],
        vectors[3],
        up_back,
        up_bias_back,
        down_back,
        down_bias_back,
    )


def solution(mesh):
    in_specs = (
        P(("fsdp", "tp"), None),
        P(("fsdp", "tp"), None),
        P(("fsdp", "tp"), None),
        P("fsdp", "tp"),
        P("fsdp", None),
        P(),
        P(),
        P("fsdp", None, "tp"),
        P(None, "tp", "fsdp"),
        P("tp", "fsdp"),
        P(),
        P(),
        P(),
        P("fsdp", None, "tp"),
        P("fsdp", "tp"),
        P("fsdp", "tp", None),
        P("fsdp", None),
    )
    out_specs = (
        P(("fsdp", "tp"), None),
        P(("fsdp", "tp"), None),
        P(),
        P(),
        P("fsdp", None, "tp"),
        P(None, "tp", "fsdp"),
        P("tp", "fsdp"),
        P(),
        P(),
        P(),
        P("fsdp", None, "tp"),
        P("fsdp", "tp"),
        P("fsdp", "tp", None),
        P("fsdp", None),
    )
    return jax.shard_map(local, mesh=mesh, in_specs=in_specs, out_specs=out_specs, check_vma=False)
```

```python
import functools

import jax
import jax.numpy as jnp
from jax import lax
from jax.experimental import pallas as pl
from jax.experimental.pallas import tpu as pltpu
from jax.sharding import PartitionSpec as P

f32 = jnp.float32
bf16 = jnp.bfloat16
i32 = jnp.int32

HEAD_DIM = 64
PIECE = 256
DOCS = 4
TP = 4
BLOCK_K = 256
EXTRA = 16
EPSILON = 1e-05
MASKED = -1e30
VMEM = 60 << 20

NN = (((1,), (0,)), ((), ()))
NT = (((1,), (1,)), ((), ()))
TN = (((0,), (0,)), ((), ()))


def mxu(a, b, dims=NN):
    return lax.dot_general(a, b, dims, preferred_element_type=f32)


TIMES = {
    "attend": 22,
    "middle_kernel": 5,
    "place_kernel": 3,
    "attend_back": 30,
    "act_back_kernel": 9,
    "expert_kernel": 10,
    "expert_out_kernel": 9,
    "up_outer_kernel": 9,
    "down_outer_kernel": 9,
    "output_weight_kernel": 4,
    "out_sum_kernel": 4,
    "projection_back_kernel": 13,
}


def cost(name, part=1.0):
    flops = int(part * TIMES.get(name, 0) * 1.1e9) + 1
    return pl.CostEstimate(flops=flops, bytes_accessed=1, transcendentals=0)


def whole_spec(x):
    return pl.BlockSpec(x.shape, lambda *_: (0,) * x.ndim)


def smem_spec():
    return pl.BlockSpec(memory_space=pltpu.SMEM)


def kernel_name(kernel):
    return getattr(kernel, "func", kernel).__name__


def plain_call(kernel, ins, outs, scratch=(), scalars=()):
    return pl.pallas_call(
        kernel,
        name=kernel_name(kernel),
        grid=(1,),
        in_specs=[smem_spec() for _ in scalars] + [whole_spec(x) for x in ins],
        out_specs=[whole_spec(x) for x in outs],
        out_shape=list(outs),
        scratch_shapes=list(scratch),
        compiler_params=pltpu.CompilerParams(vmem_limit_bytes=VMEM),
        cost_estimate=cost(kernel_name(kernel)),
    )(*scalars, *ins)


def struct(shape, dtype):
    return jax.ShapeDtypeStruct(shape, dtype)


def send_tp(x, turn):
    return lax.ppermute(x, "tp", [(i, i ^ turn) for i in range(TP)])


def send_fsdp(x, turn):
    n = lax.axis_size("fsdp")
    return lax.ppermute(x, "fsdp", [(i, i ^ turn) for i in range(n)])


def after(x, *firsts):
    return lax.optimization_barrier((x, firsts))[0]


def sum_kernel(*refs):
    total = refs[0][...].astype(f32)
    for ref in refs[1:-1]:
        total = total + ref[...].astype(f32)
    refs[-1][...] = total.astype(refs[-1].dtype)


def added(*parts, dtype=bf16):
    return plain_call(sum_kernel, parts, [struct(parts[0].shape, dtype)])[0]


def pairs_sum_kernel(a, b, c, d, out):
    out[...] = (a[...] + b[...]) + (c[...] + d[...])


def turned_sum_kernel(blocks, out):
    rows = out.shape[1]
    total = blocks[:rows, :].astype(f32)
    for at in range(rows, blocks.shape[0], rows):
        total = total + blocks[at : at + rows, :].astype(f32)
    out[...] = total.T


def two_parts(x):
    high = x.astype(bf16)
    return jnp.concatenate([high, (x - high.astype(f32)).astype(bf16)], axis=0)


def one_part(x):
    x = x.astype(f32)
    return x[: x.shape[0] // 2] + x[x.shape[0] // 2 :]


def fold_kernel(own, vector, got, kept, vectors, *outs):
    rows = kept.shape[0]
    size = own.shape[0]
    kept[...] = own[:rows, :].astype(f32) + got[:rows, :].astype(f32)
    vectors[...] = one_part(two_parts(vector[...])) + one_part(got[size:, :])
    parts = two_parts(vectors[...])
    for at, out in enumerate(outs):
        here = slice((at + 1) * rows, (at + 2) * rows)
        out[:rows, :] = (own[here, :].astype(f32) + got[here, :].astype(f32)).astype(bf16)
        out[rows:, :] = parts


def last_fold_kernel(kept, vector, *refs):
    out, vectors = refs[-2:]
    rows, width = out.shape[1:]
    total = kept[...]
    sums = [one_part(two_parts(vector[...]))]
    for ref in refs[:-2]:
        total = total + ref[:rows, :].astype(f32)
        sums.append(one_part(ref[rows:, :]))
    while len(sums) > 1:
        sums = [a + b for a, b in zip(sums[0::2], sums[1::2])]
    for j in range(out.shape[0]):
        out[j] = total[:, j * width : (j + 1) * width]
    vectors[...] = sums[0]


def normed(values):
    centered = values - jnp.mean(values, axis=-1, keepdims=True)
    inverse = lax.rsqrt(jnp.mean(centered * centered, axis=-1, keepdims=True) + EPSILON)
    return centered * inverse, inverse


def norm_back(incoming, unit, inverse, gain):
    scaled = incoming * gain
    return inverse * (
        scaled
        - jnp.mean(scaled, axis=-1, keepdims=True)
        - unit * jnp.mean(scaled * unit, axis=-1, keepdims=True)
    )


def first_kernel(x, gain, shift, docs, w_in, w_out, bias, out, packed, copies):
    rows = x.shape[0]
    unit, _ = normed(x[...].astype(f32))
    out[:rows, :] = (unit * gain[...] + shift[...]).astype(bf16)
    out[rows:, :] = jnp.zeros_like(out[rows:, :])
    out[rows : rows + EXTRA, :rows] = jnp.broadcast_to(
        docs[...].astype(f32), (EXTRA, rows)
    ).astype(bf16)
    shard, width = w_in.shape[1:]
    for j in range(3):
        packed[:shard, j * width : (j + 1) * width] = w_in[j]
    turned = w_out[...].T
    for at in range(0, copies.shape[0], shard):
        copies[at : at + shard, :] = turned
    packed[shard:, :] = jnp.zeros_like(packed[shard:, :])
    packed[shard:, :width] = bias[...]


def slots_kernel(cap, place, ids, cot, slots, sent):
    rows = ids.shape[0]
    column = ids[...].astype(f32)
    across = jnp.broadcast_to(column, (rows, 128)).T[:1]
    before = lax.broadcasted_iota(i32, (rows, rows), 0) < lax.broadcasted_iota(i32, (rows, rows), 1)
    rank = jnp.sum(jnp.where(before & (column == across), 1.0, 0.0), axis=0, keepdims=True)
    rank = rank.astype(i32)
    expert = across.astype(i32)
    mine = (expert & 1) == (place[1] & 1)
    own = (expert >> 1) * cap + rank
    slots[...] = jnp.broadcast_to(jnp.where(mine, own, -1), slots.shape)
    sent[:rows, :] = cot[...]
    sent[rows:, :] = jnp.zeros_like(sent[rows:, :])
    meta = [jnp.where(mine, -1, v).astype(f32) for v in (expert >> 1, rank)]
    meta += [jnp.zeros((EXTRA - 2, rows), f32)]
    sent[rows:, :rows] = jnp.concatenate(meta, axis=0).astype(bf16)


def other_slots_kernel(cap, sent, slots, out):
    rows = slots.shape[1]
    meta = sent[rows:, :rows].astype(f32)
    group, rank = meta[0:1].astype(i32), meta[1:2].astype(i32)
    named = group >= 0
    own = jnp.where(named, group * cap + rank, -1)
    slots[...] = jnp.broadcast_to(own, slots.shape)
    spots = lax.broadcasted_iota(i32, (out.shape[0], rows), 0)
    out[...] = mxu(jnp.where(spots == own, 1.0, 0.0).astype(bf16), sent[:rows, :]).astype(bf16)


def project_kernel(n, rows, place, *refs):
    xs, ws = refs[:TP], refs[TP : TP + n]
    q, k, v, w_in = refs[TP + n :]
    width = q.shape[1]
    bias = jnp.zeros((8, width), f32)
    lane = lax.rem(lax.broadcasted_iota(i32, (8, width), 1), HEAD_DIM) // (HEAD_DIM // n)
    for turn in range(n):
        base = pl.multiple_of((place[0] ^ turn) * rows, rows)
        w_in[pl.ds(base, rows), :] = ws[turn][:rows, :]
        part = ws[turn][rows:, :width].astype(f32)[:8]
        bias = jnp.where(lane == (place[0] ^ turn), part, bias)
    block = q.shape[0] // TP
    for r in range(TP):
        x = xs[r][:block, :]
        here = pl.ds(r * block, block)
        q[here, :] = ((mxu(x, w_in[:, :width]) + bias[0:1, :]) * 0.125).astype(bf16)
        k[here, :] = mxu(x, w_in[:, width : 2 * width]).astype(bf16)
        v[here, :] = (mxu(x, w_in[:, 2 * width :]) + bias[1:2, :]).astype(bf16)


def middle_kernel(*refs):
    ctxs, ws = refs[:TP], refs[TP : 2 * TP]
    residual, bias, gain, shift, mixed, second, upper, lower = refs[-8:]
    total = residual[...].astype(f32) + bias[...]
    for r in range(TP):
        total = total + mxu(ctxs[r][...], ws[r][...], NT)
    mixed[...] = total
    unit, _ = normed(total)
    second[...] = (unit * gain[...] + shift[...]).astype(bf16)
    half = upper.shape[0]
    upper[...] = second[:half, :]
    lower[...] = second[half:, :]


def turn_kernel(*refs):
    ws = refs[:TP]
    own, other, mixed, cot, gain = refs[TP : TP + 5]
    back, low, sums = refs[TP + 5 : TP + 8]
    outs = refs[TP + 8 :]
    unit, inverse = normed(mixed[...])
    second_back = own[...].astype(f32) + other[...].astype(f32)
    total = cot[...].astype(f32) + norm_back(second_back, unit, inverse, gain[...])
    back[...] = total
    low[...] = total.astype(bf16)
    sums[...] = jnp.concatenate(
        [
            jnp.sum(second_back * unit, axis=0, keepdims=True),
            jnp.sum(second_back, axis=0, keepdims=True),
            jnp.sum(total, axis=0, keepdims=True),
            jnp.zeros((5, total.shape[1]), f32),
        ],
        axis=0,
    )
    for r in range(TP):
        outs[r][...] = mxu(low[...], ws[r][...]).astype(bf16)


def output_weight_kernel(*refs):
    ctxs, low, kept, away = refs[:TP], refs[TP], refs[TP + 1], refs[TP + 2]
    size = low.shape[1]
    for r in range(TP):
        out = away if r & 1 else kept
        to = (r // 2) * size
        out[to : to + size, :] = mxu(low[...], ctxs[r][...], TN).astype(bf16)


def pair_sum_kernel(a, b, here, there):
    size = here.shape[0]
    for at, out in enumerate((here, there)):
        rows = slice(at * size, (at + 1) * size)
        out[...] = (a[rows, :].astype(f32) + b[rows, :].astype(f32)).astype(bf16)


def lane_sums(x):
    total = jnp.sum(x, axis=1, keepdims=True)
    return jnp.broadcast_to(total, (x.shape[0], 128)).T[:8]


def projection_back_kernel(n, rows, place, *refs):
    xs, backs, w_in, sums2 = refs[:TP], refs[TP : TP + 3], refs[TP + 3], refs[TP + 4]
    outs, keep, away, vectors, small, total = refs[TP + 5 : -5], *refs[-5:]
    width = w_in.shape[1] // 3
    block = backs[0].shape[0] // TP
    ones = jnp.ones((8, block), bf16)
    for j in range(3):
        part, column = None, None
        for r in range(TP):
            here = pl.ds(r * block, block)
            back = backs[j][here, :]
            term, ends = mxu(xs[r][:block, :], back, TN), mxu(ones, back)
            part = term if part is None else part + term
            column = ends if column is None else column + ends
        total[:, j * width : (j + 1) * width] = part
        small[8 * j : 8 * j + 8, :] = column
    for r in range(TP):
        here = pl.ds(r * block, block)
        term = None
        for j in range(3):
            product = mxu(backs[j][here, :], w_in[:, j * width : (j + 1) * width], NT)
            term = product if term is None else term + product
        outs[r][...] = term.astype(bf16)
    for turn in range(n):
        base = pl.multiple_of((place[0] ^ turn) * rows, rows)
        dest = away if turn % 2 else keep
        to = turn // 2 * rows
        dest[to : to + rows, :] = total[pl.ds(base, rows), :].astype(bf16)
    w = w_in[...].astype(f32)
    column = jnp.concatenate([small[8 * j : 8 * j + 1, :] for j in range(3)], axis=1)
    lines = [lane_sums(total[...] * w)[:1], lane_sums(w * column)[:1]]
    lines += [sums2[r : r + 1, :] for r in range(3)]
    for r, line in enumerate(lines):
        vectors[r : r + 1, :] = line[:, : 3 * width]
    rests = [line[:, 3 * width :] for line in lines]
    rests += [small[0:1, :], small[16:17, :], jnp.zeros((1, 2 * width), f32)]
    rests = jnp.concatenate(rests, axis=1)
    for r in range(3):
        vectors[5 + r : 6 + r, :] = rests[:, 3 * width * r : 3 * width * (r + 1)]
    away[n // 2 * rows :, :] = two_parts(vectors[...])


def last_kernel(residual, gain, own, other, mixed_back, out):
    unit, inverse = normed(residual[...].astype(f32))
    first_back = own[...].astype(f32) + other[...].astype(f32)
    out[...] = mixed_back[...] + norm_back(first_back, unit, inverse, gain[...])


def half_rows(x, h):
    rows = lax.broadcasted_iota(i32, x.shape, 0)
    keep = (rows < HEAD_DIM) if h == 0 else (rows >= HEAD_DIM)
    return jnp.where(keep, x, jnp.zeros_like(x))


def half_lanes(x, h):
    lanes = lax.broadcasted_iota(i32, x.shape, 1)
    keep = (lanes < HEAD_DIM) if h == 0 else (lanes >= HEAD_DIM)
    return jnp.where(keep, x, jnp.zeros_like(x))


def key_base(kb, block, t):
    per = block // BLOCK_K
    return pl.multiple_of(((kb // per) ^ t) * block + lax.rem(kb, per) * BLOCK_K, BLOCK_K)


def lanes(p):
    return slice(128 * p, 128 * (p + 1))


def attend_kernel(t_ref, q_ref, k_ref, v_ref, a_ref, b_ref, *rest):
    outs, lse_ref, vt = rest[:TP], rest[TP], rest[TP + 1]
    i = pl.program_id(0)
    bq, width = q_ref.shape
    bk = BLOCK_K
    pairs = range(width // 128)
    heads = [(p, h) for p in pairs for h in (0, 1)]

    @pl.when(i == 0)
    def _():
        vt[...] = v_ref[...].T

    qts = [q_ref[:, lanes(p)].T for p in pairs]
    qz = [half_rows(qts[p], h) for p, h in heads]
    a = a_ref[...]
    b = b_ref[...]

    def body(kb, carry):
        base = key_base(kb, bq, t_ref[0])
        here = pl.ds(base, bk)
        j = kb * bk + lax.broadcasted_iota(i32, (bk, bq), 0)
        mask = (j >= a) & (j <= b)
        products = [mxu(k_ref[here, lanes(p)], z) for (p, h), z in zip(heads, qz)]
        ss = [jnp.where(mask, s, MASKED) for s in products]
        tops = [
            jnp.maximum(c[0], jnp.max(s, axis=0, keepdims=True)) for c, s in zip(carry, ss)
        ]
        ps = [jnp.exp(s - top) for s, top in zip(ss, tops)]
        out = []
        for at, (m, l, acc) in enumerate(carry):
            al = jnp.exp(m - tops[at])
            l = al * l + jnp.sum(ps[at], axis=0, keepdims=True)
            part = mxu(vt[pl.ds(HEAD_DIM * at, HEAD_DIM), here], ps[at].astype(bf16))
            out.append((tops[at], l, acc * al + part))
        return tuple(out)

    init = tuple(
        (jnp.full((1, bq), MASKED, f32), jnp.zeros((1, bq), f32), jnp.zeros((HEAD_DIM, bq), f32))
        for _ in heads
    )
    res = lax.fori_loop(jnp.min(a) // bk, jnp.max(b) // bk + 1, body, init)
    o = jnp.concatenate([acc / l for m, l, acc in res], axis=0).T.astype(bf16)
    for r in range(TP):

        @pl.when(i == r)
        def _(r=r):
            outs[r][...] = o

    lse_ref[...] = jnp.concatenate(
        [m + jnp.log(l) for m, l, acc in res] + [jnp.zeros((8 - len(heads), bq), f32)], axis=0
    )


def attention_fwd(q, k, v, a, b, t):
    S, W = q.shape
    bq = S // TP
    whole = pl.BlockSpec((S, W), lambda i, *_: (0, 0))
    row = pl.BlockSpec((1, bq), lambda i, *_: (0, i))
    return pl.pallas_call(
        attend_kernel,
        name="attend",
        grid_spec=pltpu.PrefetchScalarGridSpec(
            num_scalar_prefetch=1,
            grid=(TP,),
            in_specs=[pl.BlockSpec((bq, W), lambda i, *_: (i, 0)), whole, whole, row, row],
            out_specs=[pl.BlockSpec((bq, W), lambda i, *_: (0, 0))] * TP
            + [pl.BlockSpec((8, bq), lambda i, *_: (0, i))],
            scratch_shapes=[pltpu.VMEM((W, S), bf16)],
        ),
        out_shape=[struct((bq, W), bf16)] * TP + [struct((8, S), f32)],
        compiler_params=pltpu.CompilerParams(vmem_limit_bytes=VMEM),
        cost_estimate=cost("attend"),
    )(t, q, k, v, a, b)


def attend_back_kernel(t_ref, q_ref, k_ref, v_ref, *rest):
    dos, os = rest[:TP], rest[TP : 2 * TP]
    lse_ref, a_ref, b_ref, dq_ref, dk_ref, dv_ref, kt, dk_acc, dv_acc, do_s, o_s = rest[2 * TP :]
    i = pl.program_id(0)
    bq, width = q_ref.shape
    bk = BLOCK_K
    pairs = range(width // 128)
    heads = [(p, h) for p in pairs for h in (0, 1)]

    @pl.when(i == 0)
    def _():
        kt[...] = k_ref[...].T
        dk_acc[...] = jnp.zeros_like(dk_acc)
        dv_acc[...] = jnp.zeros_like(dv_acc)

    for r in range(TP):

        @pl.when(i == r)
        def _(r=r):
            do_s[...] = dos[r][...]
            o_s[...] = os[r][...]

    def split(x):
        turned = [x[:, lanes(p)].T for p in pairs]
        rows = [half_rows(turned[p], h) for p, h in heads]
        both = [
            jnp.concatenate([half_lanes(x[:, lanes(p)], h) for h in (0, 1)], axis=0) for p in pairs
        ]
        return rows, both

    qz, qcat = split(q_ref[...])
    dz, dcat = split(do_s[...])
    prod = (do_s[...].astype(f32) * o_s[...].astype(f32)).T
    delta = [
        jnp.sum(prod[HEAD_DIM * at : HEAD_DIM * (at + 1)], axis=0, keepdims=True)
        for at in range(len(heads))
    ]
    lse = [lse_ref[at : at + 1, :] for at in range(len(heads))]
    a = a_ref[...]
    b = b_ref[...]

    def body(kb, carry):
        base = key_base(kb, bq, t_ref[0])
        here = pl.ds(base, bk)
        j = kb * bk + lax.broadcasted_iota(i32, (bk, bq), 0)
        mask = (j >= a) & (j <= b)
        ss = [mxu(k_ref[here, lanes(p)], z) for (p, h), z in zip(heads, qz)]
        dps = [mxu(v_ref[here, lanes(p)], z) for (p, h), z in zip(heads, dz)]
        ps, dss = [], []
        for at in range(len(heads)):
            p = jnp.exp(jnp.where(mask, ss[at] - lse[at], MASKED))
            dss.append((p * (dps[at] - delta[at])).astype(bf16))
            ps.append(p.astype(bf16))
        for p in pairs:
            both = slice(2 * p, 2 * p + 2)
            dv_acc[here, lanes(p)] += mxu(jnp.concatenate(ps[both], axis=1), dcat[p])
            dk_acc[here, lanes(p)] += mxu(jnp.concatenate(dss[both], axis=1), qcat[p])
        return tuple(
            c + mxu(kt[pl.ds(HEAD_DIM * at, HEAD_DIM), here], dss[at])
            for at, c in enumerate(carry)
        )

    init = tuple(jnp.zeros((HEAD_DIM, bq), f32) for _ in heads)
    dqt = lax.fori_loop(jnp.min(a) // bk, jnp.max(b) // bk + 1, body, init)
    dq_ref[...] = (jnp.concatenate(dqt, axis=0).T * 0.125).astype(bf16)

    @pl.when(i == TP - 1)
    def _():
        dk_ref[...] = dk_acc[...].astype(bf16)
        dv_ref[...] = dv_acc[...].astype(bf16)


def attention_bwd(q, k, v, dos, os, lse, a, b, t):
    S, W = q.shape
    bq = S // TP
    block = pl.BlockSpec((bq, W), lambda i, *_: (0, 0))
    rows = pl.BlockSpec((bq, W), lambda i, *_: (i, 0))
    whole = pl.BlockSpec((S, W), lambda i, *_: (0, 0))
    row = pl.BlockSpec((1, bq), lambda i, *_: (0, i))
    return pl.pallas_call(
        attend_back_kernel,
        name="attend_back",
        grid_spec=pltpu.PrefetchScalarGridSpec(
            num_scalar_prefetch=1,
            grid=(TP,),
            in_specs=[rows, whole, whole]
            + [block] * (2 * TP)
            + [pl.BlockSpec((8, bq), lambda i, *_: (0, i)), row, row],
            out_specs=[rows, whole, whole],
            scratch_shapes=[
                pltpu.VMEM((W, S), bf16),
                pltpu.VMEM((S, W), f32),
                pltpu.VMEM((S, W), f32),
                pltpu.VMEM((bq, W), bf16),
                pltpu.VMEM((bq, W), bf16),
            ],
        ),
        out_shape=[struct((S, W), bf16)] * 3,
        compiler_params=pltpu.CompilerParams(vmem_limit_bytes=VMEM),
        cost_estimate=cost("attend_back"),
    )(t, q, k, v, *dos, *os, lse, a, b)


def intervals_kernel(place, starts, *refs):
    first, end = refs[TP:]
    rows = first.shape[1] // TP
    docs = [ref[0:1, :rows].astype(f32) for ref in refs[:TP]]
    bounds = [jnp.zeros((1, 1), f32)]
    for number in range(DOCS):
        here = sum(jnp.sum(jnp.where(d == number, 1.0, 0.0), axis=1, keepdims=True) for d in docs)
        bounds.append(bounds[-1] + here)
    for r in range(TP):
        low = jnp.zeros((1, rows), f32)
        last = jnp.zeros((1, rows), f32)
        for number in range(DOCS):
            here = docs[r] == number
            low = jnp.where(here, bounds[number], low)
            last = jnp.where(here, bounds[number + 1] - 1.0, last)
        spot = (place[1] ^ r) * rows + lax.broadcasted_iota(i32, (1, rows), 1)
        piece_last = jnp.full((1, rows), -1, i32)
        for p in range(2):
            inside = (spot >= starts[0, p]) & (spot < starts[0, p] + PIECE)
            piece_last = jnp.where(inside, starts[0, p] + PIECE - 1, piece_last)
        first[:, r * rows : (r + 1) * rows] = low.astype(i32)
        end[:, r * rows : (r + 1) * rows] = jnp.maximum(
            spot, jnp.minimum(piece_last, last.astype(i32))
        )


def intervals(here, starts, xs, rows):
    tail = pl.BlockSpec((EXTRA, xs[0].shape[1]), lambda i: (rows // EXTRA, 0))
    out = struct((1, TP * rows), i32)
    return pl.pallas_call(
        intervals_kernel,
        name="intervals",
        grid=(1,),
        in_specs=[smem_spec(), smem_spec()] + [tail] * TP,
        out_specs=[whole_spec(out)] * 2,
        out_shape=[out] * 2,
        cost_estimate=cost("intervals"),
    )(here, starts, *xs)


def place_halves_kernel(upper, lower, s, out):
    spots = lax.broadcasted_iota(i32, (out.shape[0], s.shape[1]), 0)
    pick = jnp.where(spots == s[0:1, :], 1.0, 0.0).astype(bf16)
    half = upper.shape[0]
    total = mxu(pick[:, :half], upper[...]) + mxu(pick[:, half:], lower[...])
    out[...] = total.astype(bf16)


def place_kernel(x, s, out):
    spots = lax.broadcasted_iota(i32, (out.shape[0], s.shape[1]), 0)
    pick = jnp.where(spots == s[0:1, :], 1.0, 0.0).astype(bf16)
    out[...] = mxu(pick, x[...]).astype(bf16)


def collect_kernel(s_own, s_other, own_rows, other_rows, own, other):
    slots = lax.broadcasted_iota(i32, (own_rows.shape[0], own.shape[0]), 0)
    for s, rows, out in ((s_own, own_rows, own), (s_other, other_rows, other)):
        pick = jnp.where(slots == s[0:1, :], 1.0, 0.0).astype(bf16)
        out[...] = mxu(pick, rows[...], TN).astype(bf16)


def collect(s_own, s_other, own_rows, other_rows):
    rows, width = s_own.shape[1], own_rows.shape[1]
    return plain_call(
        collect_kernel,
        [s_own, s_other, own_rows, other_rows],
        [struct((rows, width), bf16)] * 2,
    )


def act_back_kernel(lo, near, far, down_a, down_b, out_near, out_far, sums):
    hidden = down_a.shape[0]
    half = pl.num_programs(0) // 2
    for at, (x, out) in enumerate(((near, out_near), (far, out_far))):

        @pl.when(pl.program_id(0) // half == at)
        def _(x=x, out=out):
            act_back_tile(hidden, x, down_a, down_b, out, sums)


def act_back_tile(hidden, x, down_a, down_b, out, sums):
    for j, down in enumerate((down_a, down_b)):
        out[:, j * hidden : (j + 1) * hidden] = mxu(x[...], down[...], NT).astype(bf16)
    total = mxu(jnp.ones((8, x.shape[0]), bf16), x[...])

    @pl.when(pl.program_id(0) == 0)
    def _():
        sums[...] = jnp.zeros_like(sums)

    sums[...] += total


def expert_kernel(lo, x, act_back, up_a, up_b, bias_a, bias_b, act, pre_back, x_back):
    width = up_a.shape[1]
    total = None
    for j, (up, bias) in enumerate(((up_a, bias_a), (up_b, bias_b))):
        here = slice(j * width, (j + 1) * width)
        pre = mxu(x[...], up[...]) + bias[...]
        square = pre * pre
        tan = jnp.tanh(0.7978845608028654 * pre * (1.0 + 0.044715 * square))
        half = 0.5 + 0.5 * tan
        act[:, here] = (pre * half).astype(bf16)
        slope = half + (0.5 * pre) * (1.0 - tan * tan) * (
            0.7978845608028654 + 0.1070322243 * square
        )
        low = (act_back[:, here].astype(f32) * slope).astype(bf16)
        pre_back[:, here] = low
        part = mxu(low, up[...], NT)
        total = part if total is None else total + part
    x_back[...] = total.astype(bf16)


def expert_out_kernel(lo, act_0, act_1, down_a, down_b, out):
    hidden = down_a.shape[0]
    half = pl.num_programs(0) // 2
    for at, act in enumerate((act_0, act_1)):

        @pl.when(pl.program_id(0) // half == at)
        def _(act=act):
            total = mxu(act[:, :hidden], down_a[...]) + mxu(act[:, hidden:], down_b[...])
            out[...] = total.astype(bf16)


def out_sum_kernel(cap, near, far, bias, out):
    half = near.shape[0] // 2
    for at in range(half // cap):
        for core in range(2):
            here = slice(core * half + at * cap, core * half + (at + 1) * cap)
            to = (2 * at + core) * cap
            total = near[here, :].astype(f32) + far[here, :].astype(f32) + bias[...]
            out[to : to + cap, :] = total.astype(bf16)


def collect_both_kernel(cap, s_own, s_other, both, own, other):
    slots = lax.broadcasted_iota(i32, (both.shape[0] // 2, own.shape[0]), 0)
    for core, (s, out) in enumerate(((s_own, own), (s_other, other))):
        pick = jnp.where(slots == s[0:1, :], 1.0, 0.0).astype(bf16)
        rows = jnp.concatenate(
            [both[at : at + cap, :] for at in range(core * cap, both.shape[0], 2 * cap)], axis=0
        )
        out[...] = mxu(pick, rows, TN).astype(bf16)


def up_outer_kernel(count, lo, *refs):
    left = jnp.concatenate([r[...] for r in refs[:count]], axis=0)
    right = jnp.concatenate([r[...] for r in refs[count:-2]], axis=0)
    out, sums = refs[-2:]
    out[...] = mxu(left, right, TN).astype(out.dtype)
    sums[...] = mxu(jnp.ones((8, right.shape[0]), bf16), right)


def down_outer_kernel(count, lo, *refs):
    left = jnp.concatenate([r[...] for r in refs[:count]], axis=0)
    right = jnp.concatenate([r[...] for r in refs[count:-1]], axis=0)
    refs[-1][...] = mxu(left, right, TN).astype(refs[-1].dtype)


def halves_kernel(lo, up, down, out):
    out[0] = up[...]
    out[1] = down[...]


def fill_kernel(lo, up, down, up_other, down_other, up_out, down_out):
    up_out[...] = up_other[...].astype(f32)
    down_out[...] = down_other[...].astype(f32)


class Expert:
    def __init__(self, lo, width, hidden):
        self.lo = jnp.reshape(lo, (1,)).astype(i32)
        self.width, self.hidden = width, hidden
        self.tile = 256

    def hold(self, up, up_bias, up_bias_other, down, other):
        self.up, self.down, self.other = up, down, other
        self.up_bias, self.up_bias_other = up_bias[:, None, :], up_bias_other

    def call(self, kernel, grid, in_specs, out_specs, out_shape, args, alias=None, scratch=(), part=1.0):
        return pl.pallas_call(
            kernel,
            name=kernel_name(kernel),
            grid_spec=pltpu.PrefetchScalarGridSpec(
                num_scalar_prefetch=1,
                grid=grid,
                in_specs=in_specs,
                out_specs=out_specs,
                scratch_shapes=list(scratch),
            ),
            out_shape=out_shape,
            input_output_aliases=alias or {},
            compiler_params=pltpu.CompilerParams(vmem_limit_bytes=VMEM),
            cost_estimate=cost(kernel_name(kernel), part),
        )(self.lo, *args)

    def away(self, at):
        return pl.BlockSpec((None,) + self.other.shape[1:], lambda i, lo: (at, 0, 0))

    def own(self, x):
        return pl.BlockSpec((None,) + x.shape[1:], lambda i, lo: (lo[0], 0, 0))

    def row(self, columns):
        return pl.BlockSpec((self.tile, columns), lambda i, lo: (i, 0))

    def two(self, columns, steps):
        return [
            pl.BlockSpec((self.tile, columns), lambda i, lo: (jnp.minimum(i, steps - 1), 0)),
            pl.BlockSpec((self.tile, columns), lambda i, lo: (jnp.maximum(i - steps, 0), 0)),
        ]

    def act_back(self, near, far):
        rows = near.shape[0]
        steps = rows // self.tile
        return self.call(
            act_back_kernel,
            (2 * steps,),
            self.two(self.width, steps) + [self.own(self.down), self.away(1)],
            self.two(2 * self.hidden, steps)
            + [pl.BlockSpec((8, self.width), lambda i, lo: (0, 0))],
            [struct((rows, 2 * self.hidden), bf16)] * 2 + [struct((8, self.width), f32)],
            [near, far, self.down, self.other],
        )

    def rows(self, x, act_back):
        rows = x.shape[0]
        wide = self.row(2 * self.hidden)
        return self.call(
            expert_kernel,
            (rows // self.tile,),
            [
                self.row(self.width),
                wide,
                self.own(self.up),
                self.away(0),
                self.own(self.up_bias),
                whole_spec(self.up_bias_other),
            ],
            [wide, wide, self.row(self.width)],
            [struct((rows, 2 * self.hidden), bf16)] * 2 + [struct((rows, self.width), bf16)],
            [x, act_back, self.up, self.other, self.up_bias, self.up_bias_other],
        )

    def out(self, act_0, act_1, part=1.0):
        rows = act_0.shape[0]
        steps = rows // self.tile
        return self.call(
            expert_out_kernel,
            (2 * steps,),
            self.two(2 * self.hidden, steps) + [self.own(self.down), self.away(1)],
            self.row(self.width),
            struct((2 * rows, self.width), bf16),
            [act_0, act_1, self.down, self.other],
            part=part,
        )

    def outer_specs(self, own):
        size, tile = self.width, 512
        if own:
            out = pl.BlockSpec((None, tile, size), lambda i, lo: (lo[0], i, 0))
            return out, struct((2, size, size), f32)
        return pl.BlockSpec((tile, size), lambda i, lo: (i, 0)), struct((size, size), bf16)

    def up_outer(self, xs, backs, at, own, part=1.0):
        size, count = self.width, len(xs)
        out, shape = self.outer_specs(own)
        return self.call(
            functools.partial(up_outer_kernel, count),
            (size // 512,),
            [pl.BlockSpec((xs[0].shape[0], 512), lambda i, lo: (0, i))] * count
            + [pl.BlockSpec((backs[0].shape[0], size), lambda i, lo: (0, at))] * len(backs),
            [out, pl.BlockSpec((8, size), lambda i, lo: (0, 0))],
            [shape, struct((8, size), f32)],
            list(xs) + list(backs),
            part=part,
        )

    def down_outer(self, acts, cots, at, own, part=1.0):
        rows, size, count = acts[0].shape[0], self.width, len(acts)
        out, shape = self.outer_specs(own)
        return self.call(
            functools.partial(down_outer_kernel, count),
            (size // 512,),
            [pl.BlockSpec((rows, 512), lambda i, lo: (0, at * (size // 512) + i))] * count
            + [whole_spec(c) for c in cots],
            out,
            shape,
            list(acts) + list(cots),
            part=part,
        )

    def halves(self, up, down):
        size = up.shape[1]
        part = pl.BlockSpec((None, size // 4, size), lambda i, lo: (1 - lo[0], i, 0))
        return self.call(
            halves_kernel,
            (4,),
            [part, part],
            pl.BlockSpec((2, size // 4, size), lambda i, lo: (0, i, 0)),
            struct((2, size, size), bf16),
            [up, down],
        )

    def fill(self, up, down, up_other, down_other):
        size = up_other.shape[0]
        part = pl.BlockSpec((size // 4, size), lambda i, lo: (i, 0))
        out = pl.BlockSpec((None, size // 4, size), lambda i, lo: (1 - lo[0], i, 0))
        return self.call(
            fill_kernel,
            (4,),
            [pl.BlockSpec(memory_space=pl.ANY)] * 2 + [part, part],
            [out, out],
            [struct(up.shape, f32), struct(down.shape, f32)],
            [up, down, up_other, down_other],
            alias={1: 0, 2: 1},
        )


def ordered(lo, own, other):
    return jnp.where(lo == 0, jnp.stack([own, other]), jnp.stack([other, own]))


def local(
    residual_in,
    out_cotangent,
    expert_index,
    document_index,
    piece_starts,
    first_norm_gain,
    first_norm_shift,
    input_weight,
    input_bias,
    output_weight,
    output_bias,
    second_norm_gain,
    second_norm_shift,
    expert_up,
    expert_up_bias,
    expert_down,
    expert_down_bias,
):
    rows, width = residual_in.shape
    n = lax.axis_size("fsdp")
    g = lax.axis_index("fsdp")
    t = lax.axis_index("tp")
    lo = t & 1
    place = jnp.reshape(g, (1,)).astype(i32)
    turn = jnp.reshape(t, (1,)).astype(i32)
    row = lambda v: v.reshape(1, -1)
    head_width = input_weight.shape[2]
    shard = input_weight.shape[0]
    cap = rows * 2 // (2 * n)
    evens = list(range(0, n, 2))

    expert = Expert(lo, width, expert_up.shape[2])

    def exchange(x):
        return lax.all_to_all(x, "fsdp", split_axis=0, concat_axis=0, tiled=True)

    share = jnp.pad(
        jnp.tile(input_bias, (1, 1, n)).reshape(2, head_width), ((0, EXTRA - 2), (0, 0))
    )
    x0, packed, copies = plain_call(
        first_kernel,
        [
            residual_in,
            row(first_norm_gain),
            row(first_norm_shift),
            document_index,
            jnp.transpose(input_weight, (1, 0, 2)),
            output_weight,
            share,
        ],
        [
            struct((rows + EXTRA, width), bf16),
            struct((shard + EXTRA, 3 * head_width), bf16),
            struct((n * shard, head_width), bf16),
        ],
    )
    x2 = send_tp(x0, 2)
    weights = {0: packed}
    for k in evens[1:]:
        weights[k] = send_fsdp(packed, k)
    weights[1] = send_fsdp(packed, 1)
    arrived = [weights[k] for k in evens[1:] + [1]]
    for k in evens[1:]:
        weights[k ^ 1] = send_fsdp(after(weights[k], arrived), 1)
    x1 = send_tp(after(x0, arrived), 1)
    x3 = send_tp(after(x2, arrived), 1)
    xs = [x0, x1, x2, x3]

    w_out0 = exchange(after(copies, x1))

    here = jnp.concatenate([place, turn])
    length = TP * rows
    first, end = intervals(here, piece_starts, xs, rows)
    s_own, cot_sent = plain_call(
        functools.partial(slots_kernel, cap),
        [after(expert_index, x1), out_cotangent],
        [struct((8, rows), i32), struct((rows + EXTRA, width), bf16)],
        scalars=[here],
    )

    slotted = struct((n * cap, width), bf16)
    cot_sent_own = plain_call(place_kernel, [out_cotangent, s_own], [slotted])[0]
    queries, keys, values, w_in = plain_call(
        functools.partial(project_kernel, n, shard),
        list(after(tuple(xs), cot_sent_own)) + [weights[k] for k in range(n)],
        [struct((length, head_width), bf16)] * 3 + [struct((width, 3 * head_width), bf16)],
        scalars=[place],
    )
    cot_other = send_tp(after(cot_sent, queries), 1)
    s_other, cot_sent_other = plain_call(
        functools.partial(other_slots_kernel, cap),
        [cot_other],
        [struct((8, rows), i32), slotted],
    )
    halves_sent = expert.halves(*after((expert_up, expert_down), queries))
    halves_other = send_tp(halves_sent, 1)
    near_own = exchange(after(cot_sent_own, w_out0))
    down_bias = lax.dynamic_index_in_dim(expert_down_bias, lo, keepdims=True)

    w_out2 = send_tp(w_out0, 2)
    w_out1 = send_tp(w_out0, 1)
    *contexts, totals = attention_fwd(
        after(queries, w_out0, halves_sent), keys, values, first, end, turn
    )
    ctxs = [contexts[0]] + [send_tp(contexts[r], r) for r in range(1, TP)]
    w_outs = [w_out0, w_out1, w_out2, send_tp(after(w_out2, ctxs[1]), 1)]
    near_other = exchange(after(cot_sent_other, near_own, totals))
    far_own = send_tp(after(near_own, ctxs[3]), 2)
    cot_pieces = [near_own, far_own, near_other, send_tp(near_other, 2)]
    expert.hold(expert_up, expert_up_bias, None, expert_down, halves_other)
    act_backs, cot_sums = [None] * 4, [None] * 2
    mixed, second, upper, lower = plain_call(
        middle_kernel,
        ctxs
        + w_outs
        + [
            after(residual_in, near_own, halves_other),
            row(output_bias),
            row(second_norm_gain),
            row(second_norm_shift),
        ],
        [struct((rows, width), f32), struct((rows, width), bf16)]
        + [struct((rows // 2, width), bf16)] * 2,
    )

    bias_sent = lax.dynamic_index_in_dim(after(expert_up_bias, second), 1 - lo, keepdims=True)
    expert.hold(expert_up, expert_up_bias, send_tp(bias_sent, 1), expert_down, halves_other)
    act_backs[0], act_backs[1], cot_sums[0] = expert.act_back(*cot_pieces[:2])
    act_backs[2], act_backs[3], cot_sums[1] = expert.act_back(*cot_pieces[2:])
    cot_sum = added(*cot_sums, dtype=f32)[:1]
    sent_own = plain_call(place_kernel, [second, s_own], [slotted])[0]
    sent_other = plain_call(
        place_halves_kernel, [send_tp(upper, 1), send_tp(lower, 1), after(s_other, act_backs[0])], [slotted]
    )[0]
    rows_own = exchange(after(sent_own, near_other))
    rows_other = exchange(after(sent_other, rows_own, cot_pieces[3]))
    pieces = [rows_own, send_tp(rows_own, 2), rows_other]
    acts, pre_backs, x_backs = [], [], []
    for at in range(4):
        act, pre_back, x_back = expert.rows(after(pieces[at], x_backs, act_backs[3]), act_backs[at])
        if at == 0:
            pieces.append(send_tp(after(rows_other, x_back), 2))
        acts.append(act)
        pre_backs.append(pre_back)
        x_backs.append(x_back)

    got_own = send_tp(x_backs[1], 2)
    got_other = send_tp(x_backs[3], 2)
    down_own = expert.down_outer(after(tuple(acts), x_backs[3]), cot_pieces, 0, True)
    back_sent_own = added(x_backs[0], after(got_own, down_own))
    back_home_own = exchange(back_sent_own)
    out_far = expert.out(*after((acts[1], acts[3]), back_sent_own))
    up_away, up_sum_away = expert.up_outer(pieces, after(tuple(pre_backs), out_far), 1, False)
    back_sent_other = added(x_backs[2], after(got_other, up_away))
    back_home_other = exchange(after(back_sent_other, back_home_own))
    out_got = send_tp(after(out_far, got_other), 2)
    late = after(tuple(acts), back_sent_other)
    down_away = expert.down_outer(late, cot_pieces, 1, False)
    out_near = expert.out(*after((acts[0], acts[2]), down_away), part=0.3)
    up_own, up_sum = expert.up_outer(pieces, after(tuple(pre_backs), out_near), 0, True, part=0.3)
    up_got, down_got = send_tp(up_away, 1), send_tp(down_away, 1)
    sent = send_tp(jnp.concatenate([up_sum_away[:1], cot_sum], axis=0), 1)
    back_own, back_away = collect(
        s_own, s_other, back_home_own, after(back_home_other, up_own, out_got, sent)
    )
    back_other = send_tp(back_away, 1)

    mixed_back, mixed_low, sums2, *ctx_backs = plain_call(
        turn_kernel,
        w_outs + [back_own, back_other, mixed, out_cotangent, row(second_norm_gain)],
        [
            struct((rows, width), f32),
            struct((rows, width), bf16),
            struct((8, width), f32),
        ]
        + [struct((rows, head_width), bf16)] * TP,
    )

    wo_kept, wo_away = plain_call(
        output_weight_kernel,
        ctxs + [mixed_low],
        [struct((2 * width, head_width), bf16)] * 2,
    )

    dos = [ctx_backs[0]] + [send_tp(ctx_backs[r], r) for r in range(1, TP)]
    wo_sum, wo_there = plain_call(
        pair_sum_kernel,
        [wo_kept, send_tp(wo_away, 1)],
        [struct((width, head_width), bf16)] * 2,
    )
    wo_got = send_tp(wo_there, 2)
    out_sent = plain_call(
        functools.partial(out_sum_kernel, cap),
        [out_near, after(out_got, dos[0]), down_bias],
        [struct((2 * n * cap, width), bf16)],
    )[0]
    out_home = exchange(out_sent)
    projected_backs = attention_bwd(
        after(queries, wo_sum, out_sent), keys, values, dos, contexts, totals, first, end, turn
    )
    wo = added(wo_sum, after(wo_got, projected_backs))

    part0, part1, part2, part3, keep, away, vector = plain_call(
        functools.partial(projection_back_kernel, n, shard),
        xs + list(projected_backs) + [after(w_in, up_got, down_got, wo), sums2],
        [struct((rows, width), bf16)] * TP
        + [
            struct((n // 2 * shard, 3 * head_width), bf16),
            struct((n // 2 * shard + EXTRA, 3 * head_width), bf16),
            struct((8, 3 * head_width), f32),
        ],
        scratch=[
            pltpu.VMEM((24, head_width), f32),
            pltpu.VMEM((width, 3 * head_width), f32),
        ],
        scalars=[place],
    )
    got = send_fsdp(away, 1)
    sum2 = added(part2, send_tp(part3, 1))
    got2 = send_tp(sum2, 2)
    sum0 = added(part0, send_tp(part1, 1))
    out_own, out_away = plain_call(
        functools.partial(collect_both_kernel, cap),
        [s_own, s_other, after(out_home, sum2)],
        [struct((rows, width), bf16)] * 2,
    )
    out_other = send_tp(out_away, 1)

    kept, vector, *folds = plain_call(
        fold_kernel,
        [keep, vector, after(got, out_own, sum2)],
        [struct((shard, 3 * head_width), f32), struct((8, 3 * head_width), f32)]
        + [struct((shard + EXTRA, 3 * head_width), bf16)] * (n // 2 - 1),
    )
    wi_kept = (kept, folds)
    sent = after(sent, folds)
    up_bias_back = ordered(lo, up_sum[0], sent[0])
    down_bias_back = ordered(lo, cot_sum[0], sent[1])
    wo_home = exchange(after(wo, out_own))
    output_weight_back = plain_call(
        turned_sum_kernel, [wo_home], [struct((head_width, shard), f32)]
    )[0]
    wi_total, vector = plain_call(
        last_fold_kernel,
        [kept, vector] + [send_fsdp(fold, k) for fold, k in zip(folds, evens[1:])],
        [struct((3, shard, head_width), f32), struct((8, 3 * head_width), f32)],
    )

    up_back, down_back = expert.fill(after(up_own, wi_kept), down_own, up_got, down_got)
    block_output = added(mixed, after(out_own, up_back), out_other)

    back_residual = plain_call(
        last_kernel,
        [residual_in, row(first_norm_gain), sum0, got2, after(mixed_back, folds)],
        [struct((rows, width), f32)],
    )[0]

    tails = vector[5:].reshape(-1)
    bias_sum = tails[5 * head_width : 7 * head_width]
    bias_sum = bias_sum.reshape(2, head_width // HEAD_DIM, n, HEAD_DIM // n)
    input_bias_back = lax.dynamic_index_in_dim(bias_sum, g, axis=2, keepdims=False)
    vector = after(vector, up_back, back_residual)
    turned = [send_tp(vector, r) for r in (1, 2, 3)]
    vector = plain_call(
        pairs_sum_kernel,
        [after(vector, block_output, output_weight_back)] + turned,
        [struct(vector.shape, f32)],
    )[0]
    tails = vector[5:].reshape(-1)[: 5 * head_width].reshape(5, head_width)
    vectors = jnp.concatenate([vector[:5], tails], axis=1)
    first_gain_back = (vectors[0] - first_norm_shift * vectors[1]) / first_norm_gain
    return (
        block_output,
        back_residual,
        first_gain_back,
        vectors[1],
        jnp.transpose(wi_total, (1, 0, 2)),
        input_bias_back,
        output_weight_back,
        vectors[4],
        vectors[2],
        vectors[3],
        up_back,
        up_bias_back,
        down_back,
        down_bias_back,
    )


def solution(mesh):
    in_specs = (
        P(("fsdp", "tp"), None),
        P(("fsdp", "tp"), None),
        P(("fsdp", "tp"), None),
        P("fsdp", "tp"),
        P("fsdp", None),
        P(),
        P(),
        P("fsdp", None, "tp"),
        P(None, "tp", "fsdp"),
        P("tp", "fsdp"),
        P(),
        P(),
        P(),
        P("fsdp", None, "tp"),
        P("fsdp", "tp"),
        P("fsdp", "tp", None),
        P("fsdp", None),
    )
    out_specs = (
        P(("fsdp", "tp"), None),
        P(("fsdp", "tp"), None),
        P(),
        P(),
        P("fsdp", None, "tp"),
        P(None, "tp", "fsdp"),
        P("tp", "fsdp"),
        P(),
        P(),
        P(),
        P("fsdp", None, "tp"),
        P("fsdp", "tp"),
        P("fsdp", "tp", None),
        P("fsdp", None),
    )
    return jax.shard_map(local, mesh=mesh, in_specs=in_specs, out_specs=out_specs, check_vma=False)
```

```python
import functools

import jax
import jax.numpy as jnp
from jax import lax
from jax.experimental import pallas as pl
from jax.experimental.pallas import tpu as pltpu
from jax.sharding import PartitionSpec as P

f32 = jnp.float32
bf16 = jnp.bfloat16
i32 = jnp.int32

HEAD_DIM = 64
PIECE = 256
DOCS = 4
TP = 4
BLOCK_K = 256
EXTRA = 16
EPSILON = 1e-05
MASKED = -1e30
VMEM = 60 << 20

NN = (((1,), (0,)), ((), ()))
NT = (((1,), (1,)), ((), ()))
TN = (((0,), (0,)), ((), ()))


def mxu(a, b, dims=NN):
    return lax.dot_general(a, b, dims, preferred_element_type=f32)


TIMES = {
    "attend": 22,
    "middle_kernel": 8,
    "project_kernel": 7,
    "halves_kernel": 5,
    "attend_back": 30,
    "act_back_kernel": 9,
    "expert_kernel": 10,
    "expert_out_kernel": 9,
    "up_outer_kernel": 9,
    "down_outer_kernel": 9,
    "output_weight_kernel": 4,
    "out_sum_kernel": 4,
    "projection_back_kernel": 13,
}


def cost(name, part=1.0):
    flops = int(part * TIMES.get(name, 0) * 1.1e9) + 1
    return pl.CostEstimate(flops=flops, bytes_accessed=1, transcendentals=0)


def whole_spec(x):
    return pl.BlockSpec(x.shape, lambda *_: (0,) * x.ndim)


def smem_spec():
    return pl.BlockSpec(memory_space=pltpu.SMEM)


def kernel_name(kernel):
    return getattr(kernel, "func", kernel).__name__


def plain_call(kernel, ins, outs, scratch=(), scalars=()):
    return pl.pallas_call(
        kernel,
        name=kernel_name(kernel),
        grid=(1,),
        in_specs=[smem_spec() for _ in scalars] + [whole_spec(x) for x in ins],
        out_specs=[whole_spec(x) for x in outs],
        out_shape=list(outs),
        scratch_shapes=list(scratch),
        compiler_params=pltpu.CompilerParams(vmem_limit_bytes=VMEM),
        cost_estimate=cost(kernel_name(kernel)),
    )(*scalars, *ins)


def row_call(kernel, ins, outs, rows, tile=128):
    spec = lambda x: (
        pl.BlockSpec((tile,) + x.shape[1:], lambda i: (i, 0))
        if x.shape[0] == rows
        else whole_spec(x)
    )
    return pl.pallas_call(
        kernel,
        name=kernel_name(kernel),
        grid=(rows // tile,),
        in_specs=[spec(x) for x in ins],
        out_specs=[spec(x) for x in outs],
        out_shape=list(outs),
        compiler_params=pltpu.CompilerParams(vmem_limit_bytes=VMEM),
        cost_estimate=cost(kernel_name(kernel)),
    )(*ins)


def struct(shape, dtype):
    return jax.ShapeDtypeStruct(shape, dtype)


def send_tp(x, turn):
    return lax.ppermute(x, "tp", [(i, i ^ turn) for i in range(TP)])


def send_fsdp(x, turn):
    n = lax.axis_size("fsdp")
    return lax.ppermute(x, "fsdp", [(i, i ^ turn) for i in range(n)])


def after(x, *firsts):
    return lax.optimization_barrier((x, firsts))[0]


def sum_kernel(*refs):
    total = refs[0][...].astype(f32)
    for ref in refs[1:-1]:
        total = total + ref[...].astype(f32)
    refs[-1][...] = total.astype(refs[-1].dtype)


def added(*parts, dtype=bf16):
    return plain_call(sum_kernel, parts, [struct(parts[0].shape, dtype)])[0]


def pairs_sum_kernel(a, b, c, d, out):
    out[...] = (a[...] + b[...]) + (c[...] + d[...])


def turned_sum_kernel(blocks, out):
    rows = out.shape[1]
    total = blocks[:rows, :].astype(f32)
    for at in range(rows, blocks.shape[0], rows):
        total = total + blocks[at : at + rows, :].astype(f32)
    out[...] = total.T


def two_parts(x):
    high = x.astype(bf16)
    return jnp.concatenate([high, (x - high.astype(f32)).astype(bf16)], axis=0)


def one_part(x):
    x = x.astype(f32)
    return x[: x.shape[0] // 2] + x[x.shape[0] // 2 :]


def fold_kernel(own, vector, got, kept, vectors, *outs):
    rows = kept.shape[0]
    size = own.shape[0]
    kept[...] = own[:rows, :].astype(f32) + got[:rows, :].astype(f32)
    vectors[...] = one_part(two_parts(vector[...])) + one_part(got[size:, :])
    parts = two_parts(vectors[...])
    for at, out in enumerate(outs):
        here = slice((at + 1) * rows, (at + 2) * rows)
        out[:rows, :] = (own[here, :].astype(f32) + got[here, :].astype(f32)).astype(bf16)
        out[rows:, :] = parts


def last_fold_kernel(kept, vector, *refs):
    out, vectors = refs[-2:]
    rows, width = out.shape[1:]
    total = kept[...]
    sums = [one_part(two_parts(vector[...]))]
    for ref in refs[:-2]:
        total = total + ref[:rows, :].astype(f32)
        sums.append(one_part(ref[rows:, :]))
    while len(sums) > 1:
        sums = [a + b for a, b in zip(sums[0::2], sums[1::2])]
    for j in range(out.shape[0]):
        out[j] = total[:, j * width : (j + 1) * width]
    vectors[...] = sums[0]


def normed(values):
    centered = values - jnp.mean(values, axis=-1, keepdims=True)
    inverse = lax.rsqrt(jnp.mean(centered * centered, axis=-1, keepdims=True) + EPSILON)
    return centered * inverse, inverse


def norm_back(incoming, unit, inverse, gain):
    scaled = incoming * gain
    return inverse * (
        scaled
        - jnp.mean(scaled, axis=-1, keepdims=True)
        - unit * jnp.mean(scaled * unit, axis=-1, keepdims=True)
    )


def first_kernel(x, gain, shift, docs, w_in, w_out, bias, out, packed, copies):
    rows = x.shape[0]
    unit, _ = normed(x[...].astype(f32))
    out[:rows, :] = (unit * gain[...] + shift[...]).astype(bf16)
    out[rows:, :] = jnp.zeros_like(out[rows:, :])
    out[rows : rows + EXTRA, :rows] = jnp.broadcast_to(
        docs[...].astype(f32), (EXTRA, rows)
    ).astype(bf16)
    shard, width = w_in.shape[1:]
    for j in range(3):
        packed[:shard, j * width : (j + 1) * width] = w_in[j]
    turned = w_out[...].T
    for at in range(0, copies.shape[0], shard):
        copies[at : at + shard, :] = turned
    packed[shard:, :] = jnp.zeros_like(packed[shard:, :])
    packed[shard:, :width] = bias[...]


def slots_kernel(cap, place, ids, cot, slots, sent):
    rows = ids.shape[0]
    column = ids[...].astype(f32)
    across = jnp.broadcast_to(column, (rows, 128)).T[:1]
    before = lax.broadcasted_iota(i32, (rows, rows), 0) < lax.broadcasted_iota(i32, (rows, rows), 1)
    rank = jnp.sum(jnp.where(before & (column == across), 1.0, 0.0), axis=0, keepdims=True)
    rank = rank.astype(i32)
    expert = across.astype(i32)
    mine = (expert & 1) == (place[1] & 1)
    own = (expert >> 1) * cap + rank
    slots[...] = jnp.broadcast_to(jnp.where(mine, own, -1), slots.shape)
    sent[:rows, :] = cot[...]
    sent[rows:, :] = jnp.zeros_like(sent[rows:, :])
    meta = [jnp.where(mine, -1, v).astype(f32) for v in (expert >> 1, rank)]
    meta += [jnp.zeros((EXTRA - 2, rows), f32)]
    sent[rows:, :rows] = jnp.concatenate(meta, axis=0).astype(bf16)


def other_slots_kernel(cap, sent, slots, out):
    rows = slots.shape[1]
    meta = sent[rows:, :rows].astype(f32)
    group, rank = meta[0:1].astype(i32), meta[1:2].astype(i32)
    named = group >= 0
    own = jnp.where(named, group * cap + rank, -1)
    slots[...] = jnp.broadcast_to(own, slots.shape)
    spots = lax.broadcasted_iota(i32, (out.shape[0], rows), 0)
    out[...] = mxu(jnp.where(spots == own, 1.0, 0.0).astype(bf16), sent[:rows, :]).astype(bf16)


def project_kernel(n, rows, place, *refs):
    xs, ws = refs[:TP], refs[TP : TP + n]
    q, k, v, w_in = refs[TP + n :]
    width = q.shape[1]
    bias = jnp.zeros((8, width), f32)
    lane = lax.rem(lax.broadcasted_iota(i32, (8, width), 1), HEAD_DIM) // (HEAD_DIM // n)
    for turn in range(n):
        base = pl.multiple_of((place[0] ^ turn) * rows, rows)
        w_in[pl.ds(base, rows), :] = ws[turn][:rows, :]
        part = ws[turn][rows:, :width].astype(f32)[:8]
        bias = jnp.where(lane == (place[0] ^ turn), part, bias)
    block = q.shape[0] // TP
    for r in range(TP):
        x = xs[r][:block, :]
        here = pl.ds(r * block, block)
        q[here, :] = ((mxu(x, w_in[:, :width]) + bias[0:1, :]) * 0.125).astype(bf16)
        k[here, :] = mxu(x, w_in[:, width : 2 * width]).astype(bf16)
        v[here, :] = (mxu(x, w_in[:, 2 * width :]) + bias[1:2, :]).astype(bf16)


def middle_kernel(*refs):
    ctxs, ws = refs[:TP], refs[TP : 2 * TP]
    residual, bias, gain, shift, mixed, second, upper, lower = refs[-8:]
    total = residual[...].astype(f32) + bias[...]
    for r in range(TP):
        total = total + mxu(ctxs[r][...], ws[r][...], NT)
    mixed[...] = total
    unit, _ = normed(total)
    second[...] = (unit * gain[...] + shift[...]).astype(bf16)
    half = upper.shape[0]
    upper[...] = second[:half, :]
    lower[...] = second[half:, :]


def turn_kernel(*refs):
    ws = refs[:TP]
    own, other, mixed, cot, gain = refs[TP : TP + 5]
    back, low, sums = refs[TP + 5 : TP + 8]
    outs = refs[TP + 8 :]
    unit, inverse = normed(mixed[...])
    second_back = own[...].astype(f32) + other[...].astype(f32)
    total = cot[...].astype(f32) + norm_back(second_back, unit, inverse, gain[...])
    back[...] = total
    low[...] = total.astype(bf16)

    @pl.when(pl.program_id(0) == 0)
    def _():
        sums[...] = jnp.zeros_like(sums)

    sums[...] += jnp.concatenate(
        [
            jnp.sum(second_back * unit, axis=0, keepdims=True),
            jnp.sum(second_back, axis=0, keepdims=True),
            jnp.sum(total, axis=0, keepdims=True),
            jnp.zeros((5, total.shape[1]), f32),
        ],
        axis=0,
    )
    for r in range(TP):
        outs[r][...] = mxu(low[...], ws[r][...]).astype(bf16)


def output_weight_kernel(*refs):
    ctxs, low, kept, away = refs[:TP], refs[TP], refs[TP + 1], refs[TP + 2]
    size = low.shape[1]
    for r in range(TP):
        out = away if r & 1 else kept
        to = (r // 2) * size
        out[to : to + size, :] = mxu(low[...], ctxs[r][...], TN).astype(bf16)


def pair_sum_kernel(a, b, here, there):
    size = here.shape[0]
    for at, out in enumerate((here, there)):
        rows = slice(at * size, (at + 1) * size)
        out[...] = (a[rows, :].astype(f32) + b[rows, :].astype(f32)).astype(bf16)


def lane_sums(x):
    total = jnp.sum(x, axis=1, keepdims=True)
    return jnp.broadcast_to(total, (x.shape[0], 128)).T[:8]


def projection_back_kernel(n, rows, place, *refs):
    xs, backs, w_in, sums2 = refs[:TP], refs[TP : TP + 3], refs[TP + 3], refs[TP + 4]
    outs, keep, away, vectors, small, total = refs[TP + 5 : -5], *refs[-5:]
    width = w_in.shape[1] // 3
    block = backs[0].shape[0] // TP
    ones = jnp.ones((8, block), bf16)
    for j in range(3):
        part, column = None, None
        for r in range(TP):
            here = pl.ds(r * block, block)
            back = backs[j][here, :]
            term, ends = mxu(xs[r][:block, :], back, TN), mxu(ones, back)
            part = term if part is None else part + term
            column = ends if column is None else column + ends
        total[:, j * width : (j + 1) * width] = part
        small[8 * j : 8 * j + 8, :] = column
    for r in range(TP):
        here = pl.ds(r * block, block)
        term = None
        for j in range(3):
            product = mxu(backs[j][here, :], w_in[:, j * width : (j + 1) * width], NT)
            term = product if term is None else term + product
        outs[r][...] = term.astype(bf16)
    for turn in range(n):
        base = pl.multiple_of((place[0] ^ turn) * rows, rows)
        dest = away if turn % 2 else keep
        to = turn // 2 * rows
        dest[to : to + rows, :] = total[pl.ds(base, rows), :].astype(bf16)
    w = w_in[...].astype(f32)
    column = jnp.concatenate([small[8 * j : 8 * j + 1, :] for j in range(3)], axis=1)
    lines = [lane_sums(total[...] * w)[:1], lane_sums(w * column)[:1]]
    lines += [sums2[r : r + 1, :] for r in range(3)]
    for r, line in enumerate(lines):
        vectors[r : r + 1, :] = line[:, : 3 * width]
    rests = [line[:, 3 * width :] for line in lines]
    rests += [small[0:1, :], small[16:17, :], jnp.zeros((1, 2 * width), f32)]
    rests = jnp.concatenate(rests, axis=1)
    for r in range(3):
        vectors[5 + r : 6 + r, :] = rests[:, 3 * width * r : 3 * width * (r + 1)]
    away[n // 2 * rows :, :] = two_parts(vectors[...])


def last_kernel(residual, gain, own, other, mixed_back, out):
    unit, inverse = normed(residual[...].astype(f32))
    first_back = own[...].astype(f32) + other[...].astype(f32)
    out[...] = mixed_back[...] + norm_back(first_back, unit, inverse, gain[...])


def half_rows(x, h):
    rows = lax.broadcasted_iota(i32, x.shape, 0)
    keep = (rows < HEAD_DIM) if h == 0 else (rows >= HEAD_DIM)
    return jnp.where(keep, x, jnp.zeros_like(x))


def half_lanes(x, h):
    lanes = lax.broadcasted_iota(i32, x.shape, 1)
    keep = (lanes < HEAD_DIM) if h == 0 else (lanes >= HEAD_DIM)
    return jnp.where(keep, x, jnp.zeros_like(x))


def key_base(kb, block, t):
    per = block // BLOCK_K
    return pl.multiple_of(((kb // per) ^ t) * block + lax.rem(kb, per) * BLOCK_K, BLOCK_K)


def lanes(p):
    return slice(128 * p, 128 * (p + 1))


def attend_kernel(t_ref, q_ref, k_ref, v_ref, a_ref, b_ref, *rest):
    outs, lse_ref, vt = rest[:TP], rest[TP], rest[TP + 1]
    i = pl.program_id(0)
    bq, width = q_ref.shape
    bk = BLOCK_K
    pairs = range(width // 128)
    heads = [(p, h) for p in pairs for h in (0, 1)]

    @pl.when(i == 0)
    def _():
        vt[...] = v_ref[...].T

    qts = [q_ref[:, lanes(p)].T for p in pairs]
    qz = [half_rows(qts[p], h) for p, h in heads]
    a = a_ref[...]
    b = b_ref[...]

    def body(kb, carry):
        base = key_base(kb, bq, t_ref[0])
        here = pl.ds(base, bk)
        j = kb * bk + lax.broadcasted_iota(i32, (bk, bq), 0)
        mask = (j >= a) & (j <= b)
        products = [mxu(k_ref[here, lanes(p)], z) for (p, h), z in zip(heads, qz)]
        ss = [jnp.where(mask, s, MASKED) for s in products]
        tops = [
            jnp.maximum(c[0], jnp.max(s, axis=0, keepdims=True)) for c, s in zip(carry, ss)
        ]
        ps = [jnp.exp(s - top) for s, top in zip(ss, tops)]
        out = []
        for at, (m, l, acc) in enumerate(carry):
            al = jnp.exp(m - tops[at])
            l = al * l + jnp.sum(ps[at], axis=0, keepdims=True)
            part = mxu(vt[pl.ds(HEAD_DIM * at, HEAD_DIM), here], ps[at].astype(bf16))
            out.append((tops[at], l, acc * al + part))
        return tuple(out)

    init = tuple(
        (jnp.full((1, bq), MASKED, f32), jnp.zeros((1, bq), f32), jnp.zeros((HEAD_DIM, bq), f32))
        for _ in heads
    )
    res = lax.fori_loop(jnp.min(a) // bk, jnp.max(b) // bk + 1, body, init)
    o = jnp.concatenate([acc / l for m, l, acc in res], axis=0).T.astype(bf16)
    for r in range(TP):

        @pl.when(i == r)
        def _(r=r):
            outs[r][...] = o

    lse_ref[...] = jnp.concatenate(
        [m + jnp.log(l) for m, l, acc in res] + [jnp.zeros((8 - len(heads), bq), f32)], axis=0
    )


def attention_fwd(q, k, v, a, b, t):
    S, W = q.shape
    bq = S // TP
    whole = pl.BlockSpec((S, W), lambda i, *_: (0, 0))
    row = pl.BlockSpec((1, bq), lambda i, *_: (0, i))
    return pl.pallas_call(
        attend_kernel,
        name="attend",
        grid_spec=pltpu.PrefetchScalarGridSpec(
            num_scalar_prefetch=1,
            grid=(TP,),
            in_specs=[pl.BlockSpec((bq, W), lambda i, *_: (i, 0)), whole, whole, row, row],
            out_specs=[pl.BlockSpec((bq, W), lambda i, *_: (0, 0))] * TP
            + [pl.BlockSpec((8, bq), lambda i, *_: (0, i))],
            scratch_shapes=[pltpu.VMEM((W, S), bf16)],
        ),
        out_shape=[struct((bq, W), bf16)] * TP + [struct((8, S), f32)],
        compiler_params=pltpu.CompilerParams(vmem_limit_bytes=VMEM),
        cost_estimate=cost("attend"),
    )(t, q, k, v, a, b)


def attend_back_kernel(t_ref, q_ref, k_ref, v_ref, *rest):
    dos, os = rest[:TP], rest[TP : 2 * TP]
    lse_ref, a_ref, b_ref, dq_ref, dk_ref, dv_ref, kt, dk_acc, dv_acc, do_s, o_s = rest[2 * TP :]
    i = pl.program_id(0)
    bq, width = q_ref.shape
    bk = BLOCK_K
    pairs = range(width // 128)
    heads = [(p, h) for p in pairs for h in (0, 1)]

    @pl.when(i == 0)
    def _():
        kt[...] = k_ref[...].T
        dk_acc[...] = jnp.zeros_like(dk_acc)
        dv_acc[...] = jnp.zeros_like(dv_acc)

    for r in range(TP):

        @pl.when(i == r)
        def _(r=r):
            do_s[...] = dos[r][...]
            o_s[...] = os[r][...]

    def split(x):
        turned = [x[:, lanes(p)].T for p in pairs]
        rows = [half_rows(turned[p], h) for p, h in heads]
        both = [
            jnp.concatenate([half_lanes(x[:, lanes(p)], h) for h in (0, 1)], axis=0) for p in pairs
        ]
        return rows, both

    qz, qcat = split(q_ref[...])
    dz, dcat = split(do_s[...])
    prod = (do_s[...].astype(f32) * o_s[...].astype(f32)).T
    delta = [
        jnp.sum(prod[HEAD_DIM * at : HEAD_DIM * (at + 1)], axis=0, keepdims=True)
        for at in range(len(heads))
    ]
    lse = [lse_ref[at : at + 1, :] for at in range(len(heads))]
    a = a_ref[...]
    b = b_ref[...]

    def body(kb, carry):
        base = key_base(kb, bq, t_ref[0])
        here = pl.ds(base, bk)
        j = kb * bk + lax.broadcasted_iota(i32, (bk, bq), 0)
        mask = (j >= a) & (j <= b)
        ss = [mxu(k_ref[here, lanes(p)], z) for (p, h), z in zip(heads, qz)]
        dps = [mxu(v_ref[here, lanes(p)], z) for (p, h), z in zip(heads, dz)]
        ps, dss = [], []
        for at in range(len(heads)):
            p = jnp.exp(jnp.where(mask, ss[at] - lse[at], MASKED))
            dss.append((p * (dps[at] - delta[at])).astype(bf16))
            ps.append(p.astype(bf16))
        for p in pairs:
            both = slice(2 * p, 2 * p + 2)
            dv_acc[here, lanes(p)] += mxu(jnp.concatenate(ps[both], axis=1), dcat[p])
            dk_acc[here, lanes(p)] += mxu(jnp.concatenate(dss[both], axis=1), qcat[p])
        return tuple(
            c + mxu(kt[pl.ds(HEAD_DIM * at, HEAD_DIM), here], dss[at])
            for at, c in enumerate(carry)
        )

    init = tuple(jnp.zeros((HEAD_DIM, bq), f32) for _ in heads)
    dqt = lax.fori_loop(jnp.min(a) // bk, jnp.max(b) // bk + 1, body, init)
    dq_ref[...] = (jnp.concatenate(dqt, axis=0).T * 0.125).astype(bf16)

    @pl.when(i == TP - 1)
    def _():
        dk_ref[...] = dk_acc[...].astype(bf16)
        dv_ref[...] = dv_acc[...].astype(bf16)


def attention_bwd(q, k, v, dos, os, lse, a, b, t):
    S, W = q.shape
    bq = S // TP
    block = pl.BlockSpec((bq, W), lambda i, *_: (0, 0))
    rows = pl.BlockSpec((bq, W), lambda i, *_: (i, 0))
    whole = pl.BlockSpec((S, W), lambda i, *_: (0, 0))
    row = pl.BlockSpec((1, bq), lambda i, *_: (0, i))
    return pl.pallas_call(
        attend_back_kernel,
        name="attend_back",
        grid_spec=pltpu.PrefetchScalarGridSpec(
            num_scalar_prefetch=1,
            grid=(TP,),
            in_specs=[rows, whole, whole]
            + [block] * (2 * TP)
            + [pl.BlockSpec((8, bq), lambda i, *_: (0, i)), row, row],
            out_specs=[rows, whole, whole],
            scratch_shapes=[
                pltpu.VMEM((W, S), bf16),
                pltpu.VMEM((S, W), f32),
                pltpu.VMEM((S, W), f32),
                pltpu.VMEM((bq, W), bf16),
                pltpu.VMEM((bq, W), bf16),
            ],
        ),
        out_shape=[struct((S, W), bf16)] * 3,
        compiler_params=pltpu.CompilerParams(vmem_limit_bytes=VMEM),
        cost_estimate=cost("attend_back"),
    )(t, q, k, v, *dos, *os, lse, a, b)


def intervals_kernel(place, starts, *refs):
    first, end = refs[TP:]
    rows = first.shape[1] // TP
    docs = [ref[0:1, :rows].astype(f32) for ref in refs[:TP]]
    bounds = [jnp.zeros((1, 1), f32)]
    for number in range(DOCS):
        here = sum(jnp.sum(jnp.where(d == number, 1.0, 0.0), axis=1, keepdims=True) for d in docs)
        bounds.append(bounds[-1] + here)
    for r in range(TP):
        low = jnp.zeros((1, rows), f32)
        last = jnp.zeros((1, rows), f32)
        for number in range(DOCS):
            here = docs[r] == number
            low = jnp.where(here, bounds[number], low)
            last = jnp.where(here, bounds[number + 1] - 1.0, last)
        spot = (place[1] ^ r) * rows + lax.broadcasted_iota(i32, (1, rows), 1)
        piece_last = jnp.full((1, rows), -1, i32)
        for p in range(2):
            inside = (spot >= starts[0, p]) & (spot < starts[0, p] + PIECE)
            piece_last = jnp.where(inside, starts[0, p] + PIECE - 1, piece_last)
        first[:, r * rows : (r + 1) * rows] = low.astype(i32)
        end[:, r * rows : (r + 1) * rows] = jnp.maximum(
            spot, jnp.minimum(piece_last, last.astype(i32))
        )


def intervals(here, starts, xs, rows):
    tail = pl.BlockSpec((EXTRA, xs[0].shape[1]), lambda i: (rows // EXTRA, 0))
    out = struct((1, TP * rows), i32)
    return pl.pallas_call(
        intervals_kernel,
        name="intervals",
        grid=(1,),
        in_specs=[smem_spec(), smem_spec()] + [tail] * TP,
        out_specs=[whole_spec(out)] * 2,
        out_shape=[out] * 2,
        cost_estimate=cost("intervals"),
    )(here, starts, *xs)


def place_halves_kernel(upper, lower, s, out):
    spots = lax.broadcasted_iota(i32, (out.shape[0], s.shape[1]), 0)
    pick = jnp.where(spots == s[0:1, :], 1.0, 0.0).astype(bf16)
    half = upper.shape[0]
    total = mxu(pick[:, :half], upper[...]) + mxu(pick[:, half:], lower[...])
    out[...] = total.astype(bf16)


def place_kernel(x, s, out):
    spots = lax.broadcasted_iota(i32, (out.shape[0], s.shape[1]), 0)
    pick = jnp.where(spots == s[0:1, :], 1.0, 0.0).astype(bf16)
    out[...] = mxu(pick, x[...]).astype(bf16)


def collect_kernel(s_own, s_other, own_rows, other_rows, own, other):
    slots = lax.broadcasted_iota(i32, (own_rows.shape[0], own.shape[0]), 0)
    for s, rows, out in ((s_own, own_rows, own), (s_other, other_rows, other)):
        pick = jnp.where(slots == s[0:1, :], 1.0, 0.0).astype(bf16)
        out[...] = mxu(pick, rows[...], TN).astype(bf16)


def collect(s_own, s_other, own_rows, other_rows):
    rows, width = s_own.shape[1], own_rows.shape[1]
    return plain_call(
        collect_kernel,
        [s_own, s_other, own_rows, other_rows],
        [struct((rows, width), bf16)] * 2,
    )


def act_back_kernel(lo, near, far, down_a, down_b, out_near, out_far, sums):
    hidden = down_a.shape[0]
    half = pl.num_programs(0) // 2
    for at, (x, out) in enumerate(((near, out_near), (far, out_far))):

        @pl.when(pl.program_id(0) // half == at)
        def _(x=x, out=out):
            act_back_tile(hidden, x, down_a, down_b, out, sums)


def act_back_tile(hidden, x, down_a, down_b, out, sums):
    for j, down in enumerate((down_a, down_b)):
        out[:, j * hidden : (j + 1) * hidden] = mxu(x[...], down[...], NT).astype(bf16)
    total = mxu(jnp.ones((8, x.shape[0]), bf16), x[...])

    @pl.when(pl.program_id(0) == 0)
    def _():
        sums[...] = jnp.zeros_like(sums)

    sums[...] += total


def expert_kernel(lo, x, act_back, up_a, up_b, bias_a, bias_b, act, pre_back, x_back):
    width = up_a.shape[1]
    pres = [mxu(x[...], up[...]) + bias[...] for up, bias in ((up_a, bias_a), (up_b, bias_b))]
    total = None
    for j, (pre, up) in enumerate(zip(pres, (up_a, up_b))):
        here = slice(j * width, (j + 1) * width)
        square = pre * pre
        tan = jnp.tanh(0.7978845608028654 * pre * (1.0 + 0.044715 * square))
        half = 0.5 + 0.5 * tan
        act[:, here] = (pre * half).astype(bf16)
        slope = half + (0.5 * pre) * (1.0 - tan * tan) * (
            0.7978845608028654 + 0.1070322243 * square
        )
        low = (act_back[:, here].astype(f32) * slope).astype(bf16)
        pre_back[:, here] = low
        part = mxu(low, up[...], NT)
        total = part if total is None else total + part
    x_back[...] = total.astype(bf16)


def expert_out_kernel(lo, act_0, act_1, down_a, down_b, out):
    hidden = down_a.shape[0]
    half = pl.num_programs(0) // 2
    for at, act in enumerate((act_0, act_1)):

        @pl.when(pl.program_id(0) // half == at)
        def _(act=act):
            total = mxu(act[:, :hidden], down_a[...]) + mxu(act[:, hidden:], down_b[...])
            out[...] = total.astype(bf16)


def out_sum_kernel(cap, near, far, bias, out):
    half = near.shape[0] // 2
    for at in range(half // cap):
        for core in range(2):
            here = slice(core * half + at * cap, core * half + (at + 1) * cap)
            to = (2 * at + core) * cap
            total = near[here, :].astype(f32) + far[here, :].astype(f32) + bias[...]
            out[to : to + cap, :] = total.astype(bf16)


def collect_both_kernel(cap, s_own, s_other, both, own, other):
    slots = lax.broadcasted_iota(i32, (both.shape[0] // 2, own.shape[0]), 0)
    for core, (s, out) in enumerate(((s_own, own), (s_other, other))):
        pick = jnp.where(slots == s[0:1, :], 1.0, 0.0).astype(bf16)
        rows = jnp.concatenate(
            [both[at : at + cap, :] for at in range(core * cap, both.shape[0], 2 * cap)], axis=0
        )
        out[...] = mxu(pick, rows, TN).astype(bf16)


def up_outer_kernel(count, lo, *refs):
    left = jnp.concatenate([r[...] for r in refs[:count]], axis=0)
    right = jnp.concatenate([r[...] for r in refs[count:-2]], axis=0)
    out, sums = refs[-2:]
    out[...] = mxu(left, right, TN).astype(out.dtype)
    sums[...] = mxu(jnp.ones((8, right.shape[0]), bf16), right)


def down_outer_kernel(count, lo, *refs):
    left = jnp.concatenate([r[...] for r in refs[:count]], axis=0)
    right = jnp.concatenate([r[...] for r in refs[count:-1]], axis=0)
    refs[-1][...] = mxu(left, right, TN).astype(refs[-1].dtype)


def halves_kernel(lo, up, down, out):
    out[0] = up[...]
    out[1] = down[...]


def fill_kernel(lo, up, down, up_other, down_other, up_out, down_out):
    up_out[...] = up_other[...].astype(f32)
    down_out[...] = down_other[...].astype(f32)


class Expert:
    def __init__(self, lo, width, hidden):
        self.lo = jnp.reshape(lo, (1,)).astype(i32)
        self.width, self.hidden = width, hidden
        self.tile = 256

    def hold(self, up, up_bias, up_bias_other, down, other):
        self.up, self.down, self.other = up, down, other
        self.up_bias, self.up_bias_other = up_bias[:, None, :], up_bias_other

    def call(self, kernel, grid, in_specs, out_specs, out_shape, args, alias=None, scratch=(), part=1.0):
        return pl.pallas_call(
            kernel,
            name=kernel_name(kernel),
            grid_spec=pltpu.PrefetchScalarGridSpec(
                num_scalar_prefetch=1,
                grid=grid,
                in_specs=in_specs,
                out_specs=out_specs,
                scratch_shapes=list(scratch),
            ),
            out_shape=out_shape,
            input_output_aliases=alias or {},
            compiler_params=pltpu.CompilerParams(vmem_limit_bytes=VMEM),
            cost_estimate=cost(kernel_name(kernel), part),
        )(self.lo, *args)

    def away(self, at):
        return pl.BlockSpec((None,) + self.other.shape[1:], lambda i, lo: (at, 0, 0))

    def own(self, x):
        return pl.BlockSpec((None,) + x.shape[1:], lambda i, lo: (lo[0], 0, 0))

    def row(self, columns):
        return pl.BlockSpec((self.tile, columns), lambda i, lo: (i, 0))

    def two(self, columns, steps):
        return [
            pl.BlockSpec((self.tile, columns), lambda i, lo: (jnp.minimum(i, steps - 1), 0)),
            pl.BlockSpec((self.tile, columns), lambda i, lo: (jnp.maximum(i - steps, 0), 0)),
        ]

    def act_back(self, near, far):
        rows = near.shape[0]
        steps = rows // self.tile
        return self.call(
            act_back_kernel,
            (2 * steps,),
            self.two(self.width, steps) + [self.own(self.down), self.away(1)],
            self.two(2 * self.hidden, steps)
            + [pl.BlockSpec((8, self.width), lambda i, lo: (0, 0))],
            [struct((rows, 2 * self.hidden), bf16)] * 2 + [struct((8, self.width), f32)],
            [near, far, self.down, self.other],
        )

    def rows(self, x, act_back):
        rows = x.shape[0]
        wide = self.row(2 * self.hidden)
        return self.call(
            expert_kernel,
            (rows // self.tile,),
            [
                self.row(self.width),
                wide,
                self.own(self.up),
                self.away(0),
                self.own(self.up_bias),
                whole_spec(self.up_bias_other),
            ],
            [wide, wide, self.row(self.width)],
            [struct((rows, 2 * self.hidden), bf16)] * 2 + [struct((rows, self.width), bf16)],
            [x, act_back, self.up, self.other, self.up_bias, self.up_bias_other],
        )

    def out(self, act_0, act_1, part=1.0):
        rows = act_0.shape[0]
        steps = rows // self.tile
        return self.call(
            expert_out_kernel,
            (2 * steps,),
            self.two(2 * self.hidden, steps) + [self.own(self.down), self.away(1)],
            self.row(self.width),
            struct((2 * rows, self.width), bf16),
            [act_0, act_1, self.down, self.other],
            part=part,
        )

    def outer_specs(self, own):
        size, tile = self.width, 512
        if own:
            out = pl.BlockSpec((None, tile, size), lambda i, lo: (lo[0], i, 0))
            return out, struct((2, size, size), f32)
        return pl.BlockSpec((tile, size), lambda i, lo: (i, 0)), struct((size, size), bf16)

    def up_outer(self, xs, backs, at, own, part=1.0):
        size, count = self.width, len(xs)
        out, shape = self.outer_specs(own)
        return self.call(
            functools.partial(up_outer_kernel, count),
            (size // 512,),
            [pl.BlockSpec((xs[0].shape[0], 512), lambda i, lo: (0, i))] * count
            + [pl.BlockSpec((backs[0].shape[0], size), lambda i, lo: (0, at))] * len(backs),
            [out, pl.BlockSpec((8, size), lambda i, lo: (0, 0))],
            [shape, struct((8, size), f32)],
            list(xs) + list(backs),
            part=part,
        )

    def down_outer(self, acts, cots, at, own, part=1.0):
        rows, size, count = acts[0].shape[0], self.width, len(acts)
        out, shape = self.outer_specs(own)
        return self.call(
            functools.partial(down_outer_kernel, count),
            (size // 512,),
            [pl.BlockSpec((rows, 512), lambda i, lo: (0, at * (size // 512) + i))] * count
            + [whole_spec(c) for c in cots],
            out,
            shape,
            list(acts) + list(cots),
            part=part,
        )

    def halves(self, up, down):
        size = up.shape[1]
        part = pl.BlockSpec((None, size // 4, size), lambda i, lo: (1 - lo[0], i, 0))
        return self.call(
            halves_kernel,
            (4,),
            [part, part],
            pl.BlockSpec((2, size // 4, size), lambda i, lo: (0, i, 0)),
            struct((2, size, size), bf16),
            [up, down],
        )

    def fill(self, up, down, up_other, down_other):
        size = up_other.shape[0]
        part = pl.BlockSpec((size // 4, size), lambda i, lo: (i, 0))
        out = pl.BlockSpec((None, size // 4, size), lambda i, lo: (1 - lo[0], i, 0))
        return self.call(
            fill_kernel,
            (4,),
            [pl.BlockSpec(memory_space=pl.ANY)] * 2 + [part, part],
            [out, out],
            [struct(up.shape, f32), struct(down.shape, f32)],
            [up, down, up_other, down_other],
            alias={1: 0, 2: 1},
        )


def ordered(lo, own, other):
    return jnp.where(lo == 0, jnp.stack([own, other]), jnp.stack([other, own]))


def local(
    residual_in,
    out_cotangent,
    expert_index,
    document_index,
    piece_starts,
    first_norm_gain,
    first_norm_shift,
    input_weight,
    input_bias,
    output_weight,
    output_bias,
    second_norm_gain,
    second_norm_shift,
    expert_up,
    expert_up_bias,
    expert_down,
    expert_down_bias,
):
    rows, width = residual_in.shape
    n = lax.axis_size("fsdp")
    g = lax.axis_index("fsdp")
    t = lax.axis_index("tp")
    lo = t & 1
    place = jnp.reshape(g, (1,)).astype(i32)
    turn = jnp.reshape(t, (1,)).astype(i32)
    row = lambda v: v.reshape(1, -1)
    head_width = input_weight.shape[2]
    shard = input_weight.shape[0]
    cap = rows * 2 // (2 * n)
    evens = list(range(0, n, 2))

    expert = Expert(lo, width, expert_up.shape[2])

    def exchange(x):
        return lax.all_to_all(x, "fsdp", split_axis=0, concat_axis=0, tiled=True)

    share = jnp.pad(
        jnp.tile(input_bias, (1, 1, n)).reshape(2, head_width), ((0, EXTRA - 2), (0, 0))
    )
    x0, packed, copies = plain_call(
        first_kernel,
        [
            residual_in,
            row(first_norm_gain),
            row(first_norm_shift),
            document_index,
            jnp.transpose(input_weight, (1, 0, 2)),
            output_weight,
            share,
        ],
        [
            struct((rows + EXTRA, width), bf16),
            struct((shard + EXTRA, 3 * head_width), bf16),
            struct((n * shard, head_width), bf16),
        ],
    )
    x2 = send_tp(x0, 2)
    weights = {0: packed}
    for k in evens[1:]:
        weights[k] = send_fsdp(packed, k)
    weights[1] = send_fsdp(packed, 1)
    arrived = [weights[k] for k in evens[1:] + [1]]
    for k in evens[1:]:
        weights[k ^ 1] = send_fsdp(after(weights[k], arrived), 1)
    x1 = send_tp(after(x0, arrived), 1)
    x3 = send_tp(after(x2, arrived), 1)
    xs = [x0, x1, x2, x3]

    here = jnp.concatenate([place, turn])
    length = TP * rows
    first, end = intervals(here, piece_starts, xs, rows)
    s_own, cot_sent = plain_call(
        functools.partial(slots_kernel, cap),
        [after(expert_index, x1), out_cotangent],
        [struct((8, rows), i32), struct((rows + EXTRA, width), bf16)],
        scalars=[here],
    )

    slotted = struct((n * cap, width), bf16)
    cot_sent_own = plain_call(place_kernel, [out_cotangent, s_own], [slotted])[0]
    queries, keys, values, w_in = plain_call(
        functools.partial(project_kernel, n, shard),
        list(after(tuple(xs), cot_sent_own)) + [weights[k] for k in range(n)],
        [struct((length, head_width), bf16)] * 3 + [struct((width, 3 * head_width), bf16)],
        scalars=[place],
    )
    cot_other = send_tp(after(cot_sent, queries), 1)
    s_other, cot_sent_other = plain_call(
        functools.partial(other_slots_kernel, cap),
        [cot_other],
        [struct((8, rows), i32), slotted],
    )
    halves_sent = expert.halves(*after((expert_up, expert_down), queries))
    halves_other = send_tp(halves_sent, 1)
    near_own = exchange(cot_sent_own)
    w_out0 = exchange(after(copies, near_own))
    down_bias = lax.dynamic_index_in_dim(expert_down_bias, lo, keepdims=True)

    *contexts, totals = attention_fwd(
        after(queries, near_own, halves_sent), keys, values, first, end, turn
    )
    w_late = after(w_out0, totals)
    w_out2, w_out1 = send_tp(w_late, 2), send_tp(w_late, 1)
    ctxs = [contexts[0]] + [send_tp(contexts[r], r) for r in range(1, TP)]
    w_outs = [w_out0, w_out1, w_out2, send_tp(after(w_out2, ctxs[1]), 1)]
    near_other = exchange(after(cot_sent_other, w_out0, totals))
    far_own = send_tp(near_own, 2)
    cot_pieces = [near_own, far_own, near_other, send_tp(near_other, 2)]
    expert.hold(expert_up, expert_up_bias, None, expert_down, halves_other)
    act_backs, cot_sums = [None] * 4, [None] * 2
    act_backs[0], act_backs[1], cot_sums[0] = expert.act_back(*cot_pieces[:2])
    mixed, second, upper, lower = plain_call(
        middle_kernel,
        ctxs
        + w_outs
        + [
            after(residual_in, act_backs[0]),
            row(output_bias),
            row(second_norm_gain),
            row(second_norm_shift),
        ],
        [struct((rows, width), f32), struct((rows, width), bf16)]
        + [struct((rows // 2, width), bf16)] * 2,
    )

    bias_sent = lax.dynamic_index_in_dim(after(expert_up_bias, second), 1 - lo, keepdims=True)
    expert.hold(expert_up, expert_up_bias, send_tp(bias_sent, 1), expert_down, halves_other)
    act_backs[2], act_backs[3], cot_sums[1] = expert.act_back(*cot_pieces[2:])
    cot_sum = added(*cot_sums, dtype=f32)[:1]
    sent_own = plain_call(place_kernel, [second, s_own], [slotted])[0]
    sent_other = plain_call(
        place_halves_kernel, [send_tp(upper, 1), send_tp(lower, 1), s_other], [slotted]
    )[0]
    rows_own = exchange(after(sent_own, near_other))
    rows_other = exchange(after(sent_other, rows_own, cot_pieces[3]))
    pieces = [rows_own, send_tp(rows_own, 2), rows_other]
    acts, pre_backs, x_backs = [], [], []
    for at in range(4):
        act, pre_back, x_back = expert.rows(after(pieces[at], x_backs, act_backs[3]), act_backs[at])
        if at == 0:
            pieces.append(send_tp(after(rows_other, x_back), 2))
        acts.append(act)
        pre_backs.append(pre_back)
        x_backs.append(x_back)

    got_own = send_tp(x_backs[1], 2)
    got_other = send_tp(x_backs[3], 2)
    down_own = expert.down_outer(after(tuple(acts), x_backs[3]), cot_pieces, 0, True)
    back_sent_own = added(x_backs[0], after(got_own, down_own))
    back_home_own = exchange(back_sent_own)
    out_far = expert.out(*after((acts[1], acts[3]), back_sent_own))
    up_away, up_sum_away = expert.up_outer(pieces, after(tuple(pre_backs), out_far), 1, False)
    back_sent_other = added(x_backs[2], after(got_other, up_away))
    back_home_other = exchange(after(back_sent_other, back_home_own))
    out_got = send_tp(after(out_far, got_other), 2)
    late = after(tuple(acts), back_sent_other)
    down_away = expert.down_outer(late, cot_pieces, 1, False)
    out_near = expert.out(*after((acts[0], acts[2]), down_away), part=0.5)
    up_got, down_got = send_tp(up_away, 1), send_tp(down_away, 1)
    sent = send_tp(jnp.concatenate([up_sum_away[:1], cot_sum], axis=0), 1)
    back_own, back_away = collect(
        s_own, s_other, back_home_own, after(back_home_other, out_near, out_got, sent)
    )
    back_other = send_tp(back_away, 1)

    mixed_back, mixed_low, sums2, *ctx_backs = plain_call(
        turn_kernel,
        w_outs + [back_own, back_other, mixed, out_cotangent, row(second_norm_gain)],
        [
            struct((rows, width), f32),
            struct((rows, width), bf16),
            struct((8, width), f32),
        ]
        + [struct((rows, head_width), bf16)] * TP,
    )

    wo_kept, wo_away = plain_call(
        output_weight_kernel,
        ctxs + [mixed_low],
        [struct((2 * width, head_width), bf16)] * 2,
    )

    dos = [ctx_backs[0]] + [send_tp(ctx_backs[r], r) for r in range(1, TP)]
    wo_sum, wo_there = plain_call(
        pair_sum_kernel,
        [wo_kept, send_tp(wo_away, 1)],
        [struct((width, head_width), bf16)] * 2,
    )
    wo_got = send_tp(wo_there, 2)
    out_sent = plain_call(
        functools.partial(out_sum_kernel, cap),
        [out_near, after(out_got, dos[0]), down_bias],
        [struct((2 * n * cap, width), bf16)],
    )[0]
    out_home = exchange(out_sent)
    projected_backs = attention_bwd(
        after(queries, wo_sum, out_sent), keys, values, dos, contexts, totals, first, end, turn
    )
    wo = added(wo_sum, after(wo_got, projected_backs))

    part0, part1, part2, part3, keep, away, vector = plain_call(
        functools.partial(projection_back_kernel, n, shard),
        xs + list(projected_backs) + [after(w_in, up_got, down_got, wo), sums2],
        [struct((rows, width), bf16)] * TP
        + [
            struct((n // 2 * shard, 3 * head_width), bf16),
            struct((n // 2 * shard + EXTRA, 3 * head_width), bf16),
            struct((8, 3 * head_width), f32),
        ],
        scratch=[
            pltpu.VMEM((24, head_width), f32),
            pltpu.VMEM((width, 3 * head_width), f32),
        ],
        scalars=[place],
    )
    got = send_fsdp(away, 1)
    sum2 = added(part2, send_tp(part3, 1))
    got2 = send_tp(sum2, 2)
    sum0 = added(part0, send_tp(part1, 1))
    out_own, out_away = plain_call(
        functools.partial(collect_both_kernel, cap),
        [s_own, s_other, after(out_home, sum2)],
        [struct((rows, width), bf16)] * 2,
    )
    out_other = send_tp(out_away, 1)

    kept, vector, *folds = plain_call(
        fold_kernel,
        [keep, vector, after(got, out_own, sum2)],
        [struct((shard, 3 * head_width), f32), struct((8, 3 * head_width), f32)]
        + [struct((shard + EXTRA, 3 * head_width), bf16)] * (n // 2 - 1),
    )
    wi_kept = (kept, folds)
    wo_home = exchange(after(wo, out_own))
    output_weight_back = plain_call(
        turned_sum_kernel, [wo_home], [struct((head_width, shard), f32)]
    )[0]
    wi_total, vector = plain_call(
        last_fold_kernel,
        [kept, vector] + [send_fsdp(fold, k) for fold, k in zip(folds, evens[1:])],
        [struct((3, shard, head_width), f32), struct((8, 3 * head_width), f32)],
    )

    up_own, up_sum = expert.up_outer(pieces, after(tuple(pre_backs), wi_kept), 0, True, part=0.0)
    up_back, down_back = expert.fill(up_own, down_own, up_got, down_got)
    sent = after(sent, folds)
    up_bias_back = ordered(lo, up_sum[0], sent[0])
    down_bias_back = ordered(lo, cot_sum[0], sent[1])
    block_output = added(mixed, after(out_own, up_back), out_other)

    back_residual = row_call(
        last_kernel,
        [residual_in, row(first_norm_gain), sum0, got2, after(mixed_back, folds)],
        [struct((rows, width), f32)],
        rows,
    )[0]

    tails = vector[5:].reshape(-1)
    bias_sum = tails[5 * head_width : 7 * head_width]
    bias_sum = bias_sum.reshape(2, head_width // HEAD_DIM, n, HEAD_DIM // n)
    input_bias_back = lax.dynamic_index_in_dim(bias_sum, g, axis=2, keepdims=False)
    vector = after(vector, up_back, back_residual)
    turned = [send_tp(vector, r) for r in (1, 2, 3)]
    vector = plain_call(
        pairs_sum_kernel,
        [after(vector, block_output, output_weight_back)] + turned,
        [struct(vector.shape, f32)],
    )[0]
    tails = vector[5:].reshape(-1)[: 5 * head_width].reshape(5, head_width)
    vectors = jnp.concatenate([vector[:5], tails], axis=1)
    first_gain_back = (vectors[0] - first_norm_shift * vectors[1]) / first_norm_gain
    return (
        block_output,
        back_residual,
        first_gain_back,
        vectors[1],
        jnp.transpose(wi_total, (1, 0, 2)),
        input_bias_back,
        output_weight_back,
        vectors[4],
        vectors[2],
        vectors[3],
        up_back,
        up_bias_back,
        down_back,
        down_bias_back,
    )


def solution(mesh):
    in_specs = (
        P(("fsdp", "tp"), None),
        P(("fsdp", "tp"), None),
        P(("fsdp", "tp"), None),
        P("fsdp", "tp"),
        P("fsdp", None),
        P(),
        P(),
        P("fsdp", None, "tp"),
        P(None, "tp", "fsdp"),
        P("tp", "fsdp"),
        P(),
        P(),
        P(),
        P("fsdp", None, "tp"),
        P("fsdp", "tp"),
        P("fsdp", "tp", None),
        P("fsdp", None),
    )
    out_specs = (
        P(("fsdp", "tp"), None),
        P(("fsdp", "tp"), None),
        P(),
        P(),
        P("fsdp", None, "tp"),
        P(None, "tp", "fsdp"),
        P("tp", "fsdp"),
        P(),
        P(),
        P(),
        P("fsdp", None, "tp"),
        P("fsdp", "tp"),
        P("fsdp", "tp", None),
        P("fsdp", None),
    )
    return jax.shard_map(local, mesh=mesh, in_specs=in_specs, out_specs=out_specs, check_vma=False)
```

```python
import functools

import jax
import jax.numpy as jnp
from jax import lax
from jax.experimental import pallas as pl
from jax.experimental.pallas import tpu as pltpu
from jax.sharding import PartitionSpec as P

f32 = jnp.float32
bf16 = jnp.bfloat16
i32 = jnp.int32

HEAD_DIM = 64
PIECE = 256
DOCS = 4
TP = 4
BLOCK_K = 256
EXTRA = 16
EPSILON = 1e-05
MASKED = -1e30
VMEM = 60 << 20

NN = (((1,), (0,)), ((), ()))
NT = (((1,), (1,)), ((), ()))
TN = (((0,), (0,)), ((), ()))


def mxu(a, b, dims=NN):
    return lax.dot_general(a, b, dims, preferred_element_type=f32)


TIMES = {
    "attend": 22,
    "middle_kernel": 8,
    "project_kernel": 7,
    "halves_kernel": 5,
    "attend_back": 30,
    "act_back_kernel": 9,
    "expert_kernel": 10,
    "expert_out_kernel": 9,
    "up_outer_kernel": 9,
    "down_outer_kernel": 9,
    "output_weight_kernel": 4,
    "out_sum_kernel": 4,
    "projection_back_kernel": 13,
}


def cost(name, part=1.0):
    flops = int(part * TIMES.get(name, 0) * 1.1e9) + 1
    return pl.CostEstimate(flops=flops, bytes_accessed=1, transcendentals=0)


def whole_spec(x):
    return pl.BlockSpec(x.shape, lambda *_: (0,) * x.ndim)


def smem_spec():
    return pl.BlockSpec(memory_space=pltpu.SMEM)


def kernel_name(kernel):
    return getattr(kernel, "func", kernel).__name__


def plain_call(kernel, ins, outs, scratch=(), scalars=()):
    return pl.pallas_call(
        kernel,
        name=kernel_name(kernel),
        grid=(1,),
        in_specs=[smem_spec() for _ in scalars] + [whole_spec(x) for x in ins],
        out_specs=[whole_spec(x) for x in outs],
        out_shape=list(outs),
        scratch_shapes=list(scratch),
        compiler_params=pltpu.CompilerParams(vmem_limit_bytes=VMEM),
        cost_estimate=cost(kernel_name(kernel)),
    )(*scalars, *ins)


def row_call(kernel, ins, outs, rows, tile=128):
    spec = lambda x: (
        pl.BlockSpec((tile,) + x.shape[1:], lambda i: (i, 0))
        if x.shape[0] == rows
        else whole_spec(x)
    )
    return pl.pallas_call(
        kernel,
        name=kernel_name(kernel),
        grid=(rows // tile,),
        in_specs=[spec(x) for x in ins],
        out_specs=[spec(x) for x in outs],
        out_shape=list(outs),
        compiler_params=pltpu.CompilerParams(vmem_limit_bytes=VMEM),
        cost_estimate=cost(kernel_name(kernel)),
    )(*ins)


def struct(shape, dtype):
    return jax.ShapeDtypeStruct(shape, dtype)


def send_tp(x, turn):
    return lax.ppermute(x, "tp", [(i, i ^ turn) for i in range(TP)])


def send_fsdp(x, turn):
    n = lax.axis_size("fsdp")
    return lax.ppermute(x, "fsdp", [(i, i ^ turn) for i in range(n)])


def after(x, *firsts):
    return lax.optimization_barrier((x, firsts))[0]


def sum_kernel(*refs):
    total = refs[0][...].astype(f32)
    for ref in refs[1:-1]:
        total = total + ref[...].astype(f32)
    refs[-1][...] = total.astype(refs[-1].dtype)


def added(*parts, dtype=bf16):
    return plain_call(sum_kernel, parts, [struct(parts[0].shape, dtype)])[0]


def pairs_sum_kernel(a, b, c, d, gain, shift, out):
    total = (a[...] + b[...]) + (c[...] + d[...])
    size = total.shape[1]
    rest = size // 3
    lines = []
    for r in range(5):
        row, column = 5 + r * rest // size, r * rest % size
        lines.append(
            jnp.concatenate(
                [total[r : r + 1, :], total[row : row + 1, column : column + rest]], axis=1
            )
        )
    lines[0] = (lines[0] - shift[...] * lines[1]) / gain[...]
    out[...] = jnp.concatenate(lines + [jnp.zeros((3, out.shape[1]), f32)], axis=0)


def turned_sum_kernel(blocks, out):
    rows = out.shape[1]
    total = blocks[:rows, :].astype(f32)
    for at in range(rows, blocks.shape[0], rows):
        total = total + blocks[at : at + rows, :].astype(f32)
    out[...] = total.T


def two_parts(x):
    high = x.astype(bf16)
    return jnp.concatenate([high, (x - high.astype(f32)).astype(bf16)], axis=0)


def one_part(x):
    x = x.astype(f32)
    return x[: x.shape[0] // 2] + x[x.shape[0] // 2 :]


def fold_kernel(own, vector, got, kept, vectors, *outs):
    rows = kept.shape[0]
    size = own.shape[0]
    kept[...] = own[:rows, :].astype(f32) + got[:rows, :].astype(f32)
    vectors[...] = one_part(two_parts(vector[...])) + one_part(got[size:, :])
    parts = two_parts(vectors[...])
    for at, out in enumerate(outs):
        here = slice((at + 1) * rows, (at + 2) * rows)
        out[:rows, :] = (own[here, :].astype(f32) + got[here, :].astype(f32)).astype(bf16)
        out[rows:, :] = parts


def last_fold_kernel(kept, vector, *refs):
    out, vectors = refs[-2:]
    rows, width = out.shape[1:]
    total = kept[...]
    sums = [one_part(two_parts(vector[...]))]
    for ref in refs[:-2]:
        total = total + ref[:rows, :].astype(f32)
        sums.append(one_part(ref[rows:, :]))
    while len(sums) > 1:
        sums = [a + b for a, b in zip(sums[0::2], sums[1::2])]
    for j in range(out.shape[0]):
        out[j] = total[:, j * width : (j + 1) * width]
    vectors[...] = sums[0]


def normed(values):
    centered = values - jnp.mean(values, axis=-1, keepdims=True)
    inverse = lax.rsqrt(jnp.mean(centered * centered, axis=-1, keepdims=True) + EPSILON)
    return centered * inverse, inverse


def norm_back(incoming, unit, inverse, gain):
    scaled = incoming * gain
    return inverse * (
        scaled
        - jnp.mean(scaled, axis=-1, keepdims=True)
        - unit * jnp.mean(scaled * unit, axis=-1, keepdims=True)
    )


def first_kernel(x, gain, shift, docs, w_in, w_out, bias, out, packed, copies):
    rows = x.shape[0]
    unit, _ = normed(x[...].astype(f32))
    out[:rows, :] = (unit * gain[...] + shift[...]).astype(bf16)
    out[rows:, :] = jnp.zeros_like(out[rows:, :])
    out[rows : rows + EXTRA, :rows] = jnp.broadcast_to(
        docs[...].astype(f32), (EXTRA, rows)
    ).astype(bf16)
    shard, width = w_in.shape[1:]
    for j in range(3):
        packed[:shard, j * width : (j + 1) * width] = w_in[j]
    turned = w_out[...].T
    for at in range(0, copies.shape[0], shard):
        copies[at : at + shard, :] = turned
    packed[shard:, :] = jnp.zeros_like(packed[shard:, :])
    packed[shard:, :width] = bias[...]


def slots_kernel(cap, place, ids, cot, slots, sent):
    rows = ids.shape[0]
    column = ids[...].astype(f32)
    across = jnp.broadcast_to(column, (rows, 128)).T[:1]
    before = lax.broadcasted_iota(i32, (rows, rows), 0) < lax.broadcasted_iota(i32, (rows, rows), 1)
    rank = jnp.sum(jnp.where(before & (column == across), 1.0, 0.0), axis=0, keepdims=True)
    rank = rank.astype(i32)
    expert = across.astype(i32)
    mine = (expert & 1) == (place[1] & 1)
    own = (expert >> 1) * cap + rank
    slots[...] = jnp.broadcast_to(jnp.where(mine, own, -1), slots.shape)
    sent[:rows, :] = cot[...]
    sent[rows:, :] = jnp.zeros_like(sent[rows:, :])
    meta = [jnp.where(mine, -1, v).astype(f32) for v in (expert >> 1, rank)]
    meta += [jnp.zeros((EXTRA - 2, rows), f32)]
    sent[rows:, :rows] = jnp.concatenate(meta, axis=0).astype(bf16)


def other_slots_kernel(cap, sent, slots, out):
    rows = slots.shape[1]
    meta = sent[rows:, :rows].astype(f32)
    group, rank = meta[0:1].astype(i32), meta[1:2].astype(i32)
    named = group >= 0
    own = jnp.where(named, group * cap + rank, -1)
    slots[...] = jnp.broadcast_to(own, slots.shape)
    spots = lax.broadcasted_iota(i32, (out.shape[0], rows), 0)
    out[...] = mxu(jnp.where(spots == own, 1.0, 0.0).astype(bf16), sent[:rows, :]).astype(bf16)


def project_kernel(n, rows, place, *refs):
    xs, ws = refs[:TP], refs[TP : TP + n]
    q, k, v, w_in = refs[TP + n :]
    width = q.shape[1]
    bias = jnp.zeros((8, width), f32)
    lane = lax.rem(lax.broadcasted_iota(i32, (8, width), 1), HEAD_DIM) // (HEAD_DIM // n)
    for turn in range(n):
        base = pl.multiple_of((place[0] ^ turn) * rows, rows)
        w_in[pl.ds(base, rows), :] = ws[turn][:rows, :]
        part = ws[turn][rows:, :width].astype(f32)[:8]
        bias = jnp.where(lane == (place[0] ^ turn), part, bias)
    block = q.shape[0] // TP
    for r in range(TP):
        x = xs[r][:block, :]
        here = pl.ds(r * block, block)
        q[here, :] = ((mxu(x, w_in[:, :width]) + bias[0:1, :]) * 0.125).astype(bf16)
        k[here, :] = mxu(x, w_in[:, width : 2 * width]).astype(bf16)
        v[here, :] = (mxu(x, w_in[:, 2 * width :]) + bias[1:2, :]).astype(bf16)


def middle_kernel(*refs):
    ctxs, ws = refs[:TP], refs[TP : 2 * TP]
    residual, bias, gain, shift, mixed, second, upper, lower = refs[-8:]
    total = residual[...].astype(f32) + bias[...]
    for r in range(TP):
        total = total + mxu(ctxs[r][...], ws[r][...], NT)
    mixed[...] = total
    unit, _ = normed(total)
    second[...] = (unit * gain[...] + shift[...]).astype(bf16)
    half = upper.shape[0]
    upper[...] = second[:half, :]
    lower[...] = second[half:, :]


def turn_kernel(*refs):
    ws = refs[:TP]
    own, other, mixed, cot, gain = refs[TP : TP + 5]
    back, low, sums = refs[TP + 5 : TP + 8]
    outs = refs[TP + 8 :]
    unit, inverse = normed(mixed[...])
    second_back = own[...].astype(f32) + other[...].astype(f32)
    total = cot[...].astype(f32) + norm_back(second_back, unit, inverse, gain[...])
    back[...] = total
    low[...] = total.astype(bf16)

    @pl.when(pl.program_id(0) == 0)
    def _():
        sums[...] = jnp.zeros_like(sums)

    sums[...] += jnp.concatenate(
        [
            jnp.sum(second_back * unit, axis=0, keepdims=True),
            jnp.sum(second_back, axis=0, keepdims=True),
            jnp.sum(total, axis=0, keepdims=True),
            jnp.zeros((5, total.shape[1]), f32),
        ],
        axis=0,
    )
    for r in range(TP):
        outs[r][...] = mxu(low[...], ws[r][...]).astype(bf16)


def output_weight_kernel(*refs):
    ctxs, low, kept, away = refs[:TP], refs[TP], refs[TP + 1], refs[TP + 2]
    size = low.shape[1]
    for r in range(TP):
        out = away if r & 1 else kept
        to = (r // 2) * size
        out[to : to + size, :] = mxu(low[...], ctxs[r][...], TN).astype(bf16)


def pair_sum_kernel(a, b, here, there):
    size = here.shape[0]
    for at, out in enumerate((here, there)):
        rows = slice(at * size, (at + 1) * size)
        out[...] = (a[rows, :].astype(f32) + b[rows, :].astype(f32)).astype(bf16)


def lane_sums(x):
    total = jnp.sum(x, axis=1, keepdims=True)
    return jnp.broadcast_to(total, (x.shape[0], 128)).T[:8]


def projection_back_kernel(n, rows, place, *refs):
    xs, backs, w_in, sums2 = refs[:TP], refs[TP : TP + 3], refs[TP + 3], refs[TP + 4]
    outs, keep, away, vectors, small, total = refs[TP + 5 : -5], *refs[-5:]
    width = w_in.shape[1] // 3
    block = backs[0].shape[0] // TP
    ones = jnp.ones((8, block), bf16)
    for j in range(3):
        part, column = None, None
        for r in range(TP):
            here = pl.ds(r * block, block)
            back = backs[j][here, :]
            term, ends = mxu(xs[r][:block, :], back, TN), mxu(ones, back)
            part = term if part is None else part + term
            column = ends if column is None else column + ends
        total[:, j * width : (j + 1) * width] = part
        small[8 * j : 8 * j + 8, :] = column
    for r in range(TP):
        here = pl.ds(r * block, block)
        term = None
        for j in range(3):
            product = mxu(backs[j][here, :], w_in[:, j * width : (j + 1) * width], NT)
            term = product if term is None else term + product
        outs[r][...] = term.astype(bf16)
    for turn in range(n):
        base = pl.multiple_of((place[0] ^ turn) * rows, rows)
        dest = away if turn % 2 else keep
        to = turn // 2 * rows
        dest[to : to + rows, :] = total[pl.ds(base, rows), :].astype(bf16)
    w = w_in[...].astype(f32)
    column = jnp.concatenate([small[8 * j : 8 * j + 1, :] for j in range(3)], axis=1)
    lines = [lane_sums(total[...] * w)[:1], lane_sums(w * column)[:1]]
    lines += [sums2[r : r + 1, :] for r in range(3)]
    for r, line in enumerate(lines):
        vectors[r : r + 1, :] = line[:, : 3 * width]
    rests = [line[:, 3 * width :] for line in lines]
    rests += [small[0:1, :], small[16:17, :], jnp.zeros((1, 2 * width), f32)]
    rests = jnp.concatenate(rests, axis=1)
    for r in range(3):
        vectors[5 + r : 6 + r, :] = rests[:, 3 * width * r : 3 * width * (r + 1)]
    away[n // 2 * rows :, :] = two_parts(vectors[...])


def last_kernel(residual, gain, own, other, mixed_back, out):
    unit, inverse = normed(residual[...].astype(f32))
    first_back = own[...].astype(f32) + other[...].astype(f32)
    out[...] = mixed_back[...] + norm_back(first_back, unit, inverse, gain[...])


def half_rows(x, h):
    rows = lax.broadcasted_iota(i32, x.shape, 0)
    keep = (rows < HEAD_DIM) if h == 0 else (rows >= HEAD_DIM)
    return jnp.where(keep, x, jnp.zeros_like(x))


def half_lanes(x, h):
    lanes = lax.broadcasted_iota(i32, x.shape, 1)
    keep = (lanes < HEAD_DIM) if h == 0 else (lanes >= HEAD_DIM)
    return jnp.where(keep, x, jnp.zeros_like(x))


def key_base(kb, block, t):
    per = block // BLOCK_K
    return pl.multiple_of(((kb // per) ^ t) * block + lax.rem(kb, per) * BLOCK_K, BLOCK_K)


def lanes(p):
    return slice(128 * p, 128 * (p + 1))


def attend_kernel(t_ref, q_ref, k_ref, v_ref, a_ref, b_ref, *rest):
    outs, lse_ref, vt = rest[:TP], rest[TP], rest[TP + 1]
    i = pl.program_id(0)
    bq, width = q_ref.shape
    bk = BLOCK_K
    pairs = range(width // 128)
    heads = [(p, h) for p in pairs for h in (0, 1)]

    @pl.when(i == 0)
    def _():
        vt[...] = v_ref[...].T

    qts = [q_ref[:, lanes(p)].T for p in pairs]
    qz = [half_rows(qts[p], h) for p, h in heads]
    a = a_ref[...]
    b = b_ref[...]

    def body(kb, carry):
        base = key_base(kb, bq, t_ref[0])
        here = pl.ds(base, bk)
        j = kb * bk + lax.broadcasted_iota(i32, (bk, bq), 0)
        mask = (j >= a) & (j <= b)
        products = [mxu(k_ref[here, lanes(p)], z) for (p, h), z in zip(heads, qz)]
        ss = [jnp.where(mask, s, MASKED) for s in products]
        tops = [
            jnp.maximum(c[0], jnp.max(s, axis=0, keepdims=True)) for c, s in zip(carry, ss)
        ]
        ps = [jnp.exp(s - top) for s, top in zip(ss, tops)]
        out = []
        for at, (m, l, acc) in enumerate(carry):
            al = jnp.exp(m - tops[at])
            l = al * l + jnp.sum(ps[at], axis=0, keepdims=True)
            part = mxu(vt[pl.ds(HEAD_DIM * at, HEAD_DIM), here], ps[at].astype(bf16))
            out.append((tops[at], l, acc * al + part))
        return tuple(out)

    init = tuple(
        (jnp.full((1, bq), MASKED, f32), jnp.zeros((1, bq), f32), jnp.zeros((HEAD_DIM, bq), f32))
        for _ in heads
    )
    res = lax.fori_loop(jnp.min(a) // bk, jnp.max(b) // bk + 1, body, init)
    o = jnp.concatenate([acc / l for m, l, acc in res], axis=0).T.astype(bf16)
    for r in range(TP):

        @pl.when(i == r)
        def _(r=r):
            outs[r][...] = o

    lse_ref[...] = jnp.concatenate(
        [m + jnp.log(l) for m, l, acc in res] + [jnp.zeros((8 - len(heads), bq), f32)], axis=0
    )


def attention_fwd(q, k, v, a, b, t):
    S, W = q.shape
    bq = S // TP
    whole = pl.BlockSpec((S, W), lambda i, *_: (0, 0))
    row = pl.BlockSpec((1, bq), lambda i, *_: (0, i))
    return pl.pallas_call(
        attend_kernel,
        name="attend",
        grid_spec=pltpu.PrefetchScalarGridSpec(
            num_scalar_prefetch=1,
            grid=(TP,),
            in_specs=[pl.BlockSpec((bq, W), lambda i, *_: (i, 0)), whole, whole, row, row],
            out_specs=[pl.BlockSpec((bq, W), lambda i, *_: (0, 0))] * TP
            + [pl.BlockSpec((8, bq), lambda i, *_: (0, i))],
            scratch_shapes=[pltpu.VMEM((W, S), bf16)],
        ),
        out_shape=[struct((bq, W), bf16)] * TP + [struct((8, S), f32)],
        compiler_params=pltpu.CompilerParams(vmem_limit_bytes=VMEM),
        cost_estimate=cost("attend"),
    )(t, q, k, v, a, b)


def attend_back_kernel(t_ref, q_ref, k_ref, v_ref, *rest):
    dos, os = rest[:TP], rest[TP : 2 * TP]
    lse_ref, a_ref, b_ref, dq_ref, dk_ref, dv_ref, kt, dk_acc, dv_acc, do_s, o_s = rest[2 * TP :]
    i = pl.program_id(0)
    bq, width = q_ref.shape
    bk = BLOCK_K
    pairs = range(width // 128)
    heads = [(p, h) for p in pairs for h in (0, 1)]

    @pl.when(i == 0)
    def _():
        kt[...] = k_ref[...].T
        dk_acc[...] = jnp.zeros_like(dk_acc)
        dv_acc[...] = jnp.zeros_like(dv_acc)

    for r in range(TP):

        @pl.when(i == r)
        def _(r=r):
            do_s[...] = dos[r][...]
            o_s[...] = os[r][...]

    def split(x):
        turned = [x[:, lanes(p)].T for p in pairs]
        rows = [half_rows(turned[p], h) for p, h in heads]
        both = [
            jnp.concatenate([half_lanes(x[:, lanes(p)], h) for h in (0, 1)], axis=0) for p in pairs
        ]
        return rows, both

    qz, qcat = split(q_ref[...])
    dz, dcat = split(do_s[...])
    prod = (do_s[...].astype(f32) * o_s[...].astype(f32)).T
    delta = [
        jnp.sum(prod[HEAD_DIM * at : HEAD_DIM * (at + 1)], axis=0, keepdims=True)
        for at in range(len(heads))
    ]
    lse = [lse_ref[at : at + 1, :] for at in range(len(heads))]
    a = a_ref[...]
    b = b_ref[...]

    def body(kb, carry):
        base = key_base(kb, bq, t_ref[0])
        here = pl.ds(base, bk)
        j = kb * bk + lax.broadcasted_iota(i32, (bk, bq), 0)
        mask = (j >= a) & (j <= b)
        ss = [mxu(k_ref[here, lanes(p)], z) for (p, h), z in zip(heads, qz)]
        dps = [mxu(v_ref[here, lanes(p)], z) for (p, h), z in zip(heads, dz)]
        ps, dss = [], []
        for at in range(len(heads)):
            p = jnp.exp(jnp.where(mask, ss[at] - lse[at], MASKED))
            dss.append((p * (dps[at] - delta[at])).astype(bf16))
            ps.append(p.astype(bf16))
        for p in pairs:
            both = slice(2 * p, 2 * p + 2)
            dv_acc[here, lanes(p)] += mxu(jnp.concatenate(ps[both], axis=1), dcat[p])
            dk_acc[here, lanes(p)] += mxu(jnp.concatenate(dss[both], axis=1), qcat[p])
        return tuple(
            c + mxu(kt[pl.ds(HEAD_DIM * at, HEAD_DIM), here], dss[at])
            for at, c in enumerate(carry)
        )

    init = tuple(jnp.zeros((HEAD_DIM, bq), f32) for _ in heads)
    dqt = lax.fori_loop(jnp.min(a) // bk, jnp.max(b) // bk + 1, body, init)
    dq_ref[...] = (jnp.concatenate(dqt, axis=0).T * 0.125).astype(bf16)

    @pl.when(i == TP - 1)
    def _():
        dk_ref[...] = dk_acc[...].astype(bf16)
        dv_ref[...] = dv_acc[...].astype(bf16)


def attention_bwd(q, k, v, dos, os, lse, a, b, t):
    S, W = q.shape
    bq = S // TP
    block = pl.BlockSpec((bq, W), lambda i, *_: (0, 0))
    rows = pl.BlockSpec((bq, W), lambda i, *_: (i, 0))
    whole = pl.BlockSpec((S, W), lambda i, *_: (0, 0))
    row = pl.BlockSpec((1, bq), lambda i, *_: (0, i))
    return pl.pallas_call(
        attend_back_kernel,
        name="attend_back",
        grid_spec=pltpu.PrefetchScalarGridSpec(
            num_scalar_prefetch=1,
            grid=(TP,),
            in_specs=[rows, whole, whole]
            + [block] * (2 * TP)
            + [pl.BlockSpec((8, bq), lambda i, *_: (0, i)), row, row],
            out_specs=[rows, whole, whole],
            scratch_shapes=[
                pltpu.VMEM((W, S), bf16),
                pltpu.VMEM((S, W), f32),
                pltpu.VMEM((S, W), f32),
                pltpu.VMEM((bq, W), bf16),
                pltpu.VMEM((bq, W), bf16),
            ],
        ),
        out_shape=[struct((S, W), bf16)] * 3,
        compiler_params=pltpu.CompilerParams(vmem_limit_bytes=VMEM),
        cost_estimate=cost("attend_back"),
    )(t, q, k, v, *dos, *os, lse, a, b)


def intervals_kernel(place, starts, *refs):
    first, end = refs[TP:]
    rows = first.shape[1] // TP
    docs = [ref[0:1, :rows].astype(f32) for ref in refs[:TP]]
    bounds = [jnp.zeros((1, 1), f32)]
    for number in range(DOCS):
        here = sum(jnp.sum(jnp.where(d == number, 1.0, 0.0), axis=1, keepdims=True) for d in docs)
        bounds.append(bounds[-1] + here)
    for r in range(TP):
        low = jnp.zeros((1, rows), f32)
        last = jnp.zeros((1, rows), f32)
        for number in range(DOCS):
            here = docs[r] == number
            low = jnp.where(here, bounds[number], low)
            last = jnp.where(here, bounds[number + 1] - 1.0, last)
        spot = (place[1] ^ r) * rows + lax.broadcasted_iota(i32, (1, rows), 1)
        piece_last = jnp.full((1, rows), -1, i32)
        for p in range(2):
            inside = (spot >= starts[0, p]) & (spot < starts[0, p] + PIECE)
            piece_last = jnp.where(inside, starts[0, p] + PIECE - 1, piece_last)
        first[:, r * rows : (r + 1) * rows] = low.astype(i32)
        end[:, r * rows : (r + 1) * rows] = jnp.maximum(
            spot, jnp.minimum(piece_last, last.astype(i32))
        )


def intervals(here, starts, xs, rows):
    tail = pl.BlockSpec((EXTRA, xs[0].shape[1]), lambda i: (rows // EXTRA, 0))
    out = struct((1, TP * rows), i32)
    return pl.pallas_call(
        intervals_kernel,
        name="intervals",
        grid=(1,),
        in_specs=[smem_spec(), smem_spec()] + [tail] * TP,
        out_specs=[whole_spec(out)] * 2,
        out_shape=[out] * 2,
        cost_estimate=cost("intervals"),
    )(here, starts, *xs)


def place_halves_kernel(upper, lower, s, out):
    spots = lax.broadcasted_iota(i32, (out.shape[0], s.shape[1]), 0)
    pick = jnp.where(spots == s[0:1, :], 1.0, 0.0).astype(bf16)
    half = upper.shape[0]
    total = mxu(pick[:, :half], upper[...]) + mxu(pick[:, half:], lower[...])
    out[...] = total.astype(bf16)


def place_kernel(x, s, out):
    spots = lax.broadcasted_iota(i32, (out.shape[0], s.shape[1]), 0)
    pick = jnp.where(spots == s[0:1, :], 1.0, 0.0).astype(bf16)
    out[...] = mxu(pick, x[...]).astype(bf16)


def collect_kernel(s_own, s_other, own_rows, other_rows, own, other):
    slots = lax.broadcasted_iota(i32, (own_rows.shape[0], own.shape[0]), 0)
    for s, rows, out in ((s_own, own_rows, own), (s_other, other_rows, other)):
        pick = jnp.where(slots == s[0:1, :], 1.0, 0.0).astype(bf16)
        out[...] = mxu(pick, rows[...], TN).astype(bf16)


def collect(s_own, s_other, own_rows, other_rows):
    rows, width = s_own.shape[1], own_rows.shape[1]
    return plain_call(
        collect_kernel,
        [s_own, s_other, own_rows, other_rows],
        [struct((rows, width), bf16)] * 2,
    )


def act_back_kernel(lo, near, far, down_a, down_b, out_near, out_far, sums):
    hidden = down_a.shape[0]
    half = pl.num_programs(0) // 2
    for at, (x, out) in enumerate(((near, out_near), (far, out_far))):

        @pl.when(pl.program_id(0) // half == at)
        def _(x=x, out=out):
            act_back_tile(hidden, x, down_a, down_b, out, sums)


def act_back_tile(hidden, x, down_a, down_b, out, sums):
    for j, down in enumerate((down_a, down_b)):
        out[:, j * hidden : (j + 1) * hidden] = mxu(x[...], down[...], NT).astype(bf16)
    total = mxu(jnp.ones((8, x.shape[0]), bf16), x[...])

    @pl.when(pl.program_id(0) == 0)
    def _():
        sums[...] = jnp.zeros_like(sums)

    sums[...] += total


def expert_kernel(lo, x, act_back, up_a, up_b, bias_a, bias_b, act, pre_back, x_back):
    width = up_a.shape[1]
    pres = [mxu(x[...], up[...]) + bias[...] for up, bias in ((up_a, bias_a), (up_b, bias_b))]
    total = None
    for j, (pre, up) in enumerate(zip(pres, (up_a, up_b))):
        here = slice(j * width, (j + 1) * width)
        square = pre * pre
        tan = jnp.tanh(0.7978845608028654 * pre * (1.0 + 0.044715 * square))
        half = 0.5 + 0.5 * tan
        act[:, here] = (pre * half).astype(bf16)
        slope = half + (0.5 * pre) * (1.0 - tan * tan) * (
            0.7978845608028654 + 0.1070322243 * square
        )
        low = (act_back[:, here].astype(f32) * slope).astype(bf16)
        pre_back[:, here] = low
        part = mxu(low, up[...], NT)
        total = part if total is None else total + part
    x_back[...] = total.astype(bf16)


def expert_out_kernel(lo, act_0, act_1, down_a, down_b, out):
    hidden = down_a.shape[0]
    half = pl.num_programs(0) // 2
    for at, act in enumerate((act_0, act_1)):

        @pl.when(pl.program_id(0) // half == at)
        def _(act=act):
            total = mxu(act[:, :hidden], down_a[...]) + mxu(act[:, hidden:], down_b[...])
            out[...] = total.astype(bf16)


def out_sum_kernel(cap, near, far, bias, out):
    half = near.shape[0] // 2
    for at in range(half // cap):
        for core in range(2):
            here = slice(core * half + at * cap, core * half + (at + 1) * cap)
            to = (2 * at + core) * cap
            total = near[here, :].astype(f32) + far[here, :].astype(f32) + bias[...]
            out[to : to + cap, :] = total.astype(bf16)


def collect_both_kernel(cap, s_own, s_other, both, own, other):
    slots = lax.broadcasted_iota(i32, (both.shape[0] // 2, own.shape[0]), 0)
    for core, (s, out) in enumerate(((s_own, own), (s_other, other))):
        pick = jnp.where(slots == s[0:1, :], 1.0, 0.0).astype(bf16)
        rows = jnp.concatenate(
            [both[at : at + cap, :] for at in range(core * cap, both.shape[0], 2 * cap)], axis=0
        )
        out[...] = mxu(pick, rows, TN).astype(bf16)


def up_outer_kernel(count, lo, *refs):
    left = jnp.concatenate([r[...] for r in refs[:count]], axis=0)
    right = jnp.concatenate([r[...] for r in refs[count:-2]], axis=0)
    out, sums = refs[-2:]
    out[...] = mxu(left, right, TN).astype(out.dtype)
    sums[...] = mxu(jnp.ones((8, right.shape[0]), bf16), right)


def down_outer_kernel(count, lo, *refs):
    left = jnp.concatenate([r[...] for r in refs[:count]], axis=0)
    right = jnp.concatenate([r[...] for r in refs[count:-1]], axis=0)
    refs[-1][...] = mxu(left, right, TN).astype(refs[-1].dtype)


def halves_kernel(lo, up, down, out):
    out[0] = up[...]
    out[1] = down[...]


def fill_kernel(lo, up, down, up_other, down_other, up_out, down_out):
    up_out[...] = up_other[...].astype(f32)
    down_out[...] = down_other[...].astype(f32)


class Expert:
    def __init__(self, lo, width, hidden):
        self.lo = jnp.reshape(lo, (1,)).astype(i32)
        self.width, self.hidden = width, hidden
        self.tile = 256

    def hold(self, up, up_bias, up_bias_other, down, other):
        self.up, self.down, self.other = up, down, other
        self.up_bias, self.up_bias_other = up_bias[:, None, :], up_bias_other

    def call(self, kernel, grid, in_specs, out_specs, out_shape, args, alias=None, scratch=(), part=1.0):
        return pl.pallas_call(
            kernel,
            name=kernel_name(kernel),
            grid_spec=pltpu.PrefetchScalarGridSpec(
                num_scalar_prefetch=1,
                grid=grid,
                in_specs=in_specs,
                out_specs=out_specs,
                scratch_shapes=list(scratch),
            ),
            out_shape=out_shape,
            input_output_aliases=alias or {},
            compiler_params=pltpu.CompilerParams(vmem_limit_bytes=VMEM),
            cost_estimate=cost(kernel_name(kernel), part),
        )(self.lo, *args)

    def away(self, at):
        return pl.BlockSpec((None,) + self.other.shape[1:], lambda i, lo: (at, 0, 0))

    def own(self, x):
        return pl.BlockSpec((None,) + x.shape[1:], lambda i, lo: (lo[0], 0, 0))

    def row(self, columns):
        return pl.BlockSpec((self.tile, columns), lambda i, lo: (i, 0))

    def two(self, columns, steps):
        return [
            pl.BlockSpec((self.tile, columns), lambda i, lo: (jnp.minimum(i, steps - 1), 0)),
            pl.BlockSpec((self.tile, columns), lambda i, lo: (jnp.maximum(i - steps, 0), 0)),
        ]

    def act_back(self, near, far):
        rows = near.shape[0]
        steps = rows // self.tile
        return self.call(
            act_back_kernel,
            (2 * steps,),
            self.two(self.width, steps) + [self.own(self.down), self.away(1)],
            self.two(2 * self.hidden, steps)
            + [pl.BlockSpec((8, self.width), lambda i, lo: (0, 0))],
            [struct((rows, 2 * self.hidden), bf16)] * 2 + [struct((8, self.width), f32)],
            [near, far, self.down, self.other],
        )

    def rows(self, x, act_back):
        rows = x.shape[0]
        wide = self.row(2 * self.hidden)
        return self.call(
            expert_kernel,
            (rows // self.tile,),
            [
                self.row(self.width),
                wide,
                self.own(self.up),
                self.away(0),
                self.own(self.up_bias),
                whole_spec(self.up_bias_other),
            ],
            [wide, wide, self.row(self.width)],
            [struct((rows, 2 * self.hidden), bf16)] * 2 + [struct((rows, self.width), bf16)],
            [x, act_back, self.up, self.other, self.up_bias, self.up_bias_other],
        )

    def out(self, act_0, act_1, part=1.0):
        rows = act_0.shape[0]
        steps = rows // self.tile
        return self.call(
            expert_out_kernel,
            (2 * steps,),
            self.two(2 * self.hidden, steps) + [self.own(self.down), self.away(1)],
            self.row(self.width),
            struct((2 * rows, self.width), bf16),
            [act_0, act_1, self.down, self.other],
            part=part,
        )

    def outer_specs(self, own):
        size, tile = self.width, 512
        if own:
            out = pl.BlockSpec((None, tile, size), lambda i, lo: (lo[0], i, 0))
            return out, struct((2, size, size), f32)
        return pl.BlockSpec((tile, size), lambda i, lo: (i, 0)), struct((size, size), bf16)

    def up_outer(self, xs, backs, at, own, part=1.0):
        size, count = self.width, len(xs)
        out, shape = self.outer_specs(own)
        return self.call(
            functools.partial(up_outer_kernel, count),
            (size // 512,),
            [pl.BlockSpec((xs[0].shape[0], 512), lambda i, lo: (0, i))] * count
            + [pl.BlockSpec((backs[0].shape[0], size), lambda i, lo: (0, at))] * len(backs),
            [out, pl.BlockSpec((8, size), lambda i, lo: (0, 0))],
            [shape, struct((8, size), f32)],
            list(xs) + list(backs),
            part=part,
        )

    def down_outer(self, acts, cots, at, own, part=1.0):
        rows, size, count = acts[0].shape[0], self.width, len(acts)
        out, shape = self.outer_specs(own)
        return self.call(
            functools.partial(down_outer_kernel, count),
            (size // 512,),
            [pl.BlockSpec((rows, 512), lambda i, lo: (0, at * (size // 512) + i))] * count
            + [whole_spec(c) for c in cots],
            out,
            shape,
            list(acts) + list(cots),
            part=part,
        )

    def halves(self, up, down):
        size = up.shape[1]
        part = pl.BlockSpec((None, size // 4, size), lambda i, lo: (1 - lo[0], i, 0))
        return self.call(
            halves_kernel,
            (4,),
            [part, part],
            pl.BlockSpec((2, size // 4, size), lambda i, lo: (0, i, 0)),
            struct((2, size, size), bf16),
            [up, down],
        )

    def fill(self, up, down, up_other, down_other):
        size = up_other.shape[0]
        part = pl.BlockSpec((size // 4, size), lambda i, lo: (i, 0))
        out = pl.BlockSpec((None, size // 4, size), lambda i, lo: (1 - lo[0], i, 0))
        return self.call(
            fill_kernel,
            (4,),
            [pl.BlockSpec(memory_space=pl.ANY)] * 2 + [part, part],
            [out, out],
            [struct(up.shape, f32), struct(down.shape, f32)],
            [up, down, up_other, down_other],
            alias={1: 0, 2: 1},
        )


def ordered(lo, own, other):
    return jnp.where(lo == 0, jnp.stack([own, other]), jnp.stack([other, own]))


def local(
    residual_in,
    out_cotangent,
    expert_index,
    document_index,
    piece_starts,
    first_norm_gain,
    first_norm_shift,
    input_weight,
    input_bias,
    output_weight,
    output_bias,
    second_norm_gain,
    second_norm_shift,
    expert_up,
    expert_up_bias,
    expert_down,
    expert_down_bias,
):
    rows, width = residual_in.shape
    n = lax.axis_size("fsdp")
    g = lax.axis_index("fsdp")
    t = lax.axis_index("tp")
    lo = t & 1
    place = jnp.reshape(g, (1,)).astype(i32)
    turn = jnp.reshape(t, (1,)).astype(i32)
    row = lambda v: v.reshape(1, -1)
    head_width = input_weight.shape[2]
    shard = input_weight.shape[0]
    cap = rows * 2 // (2 * n)
    evens = list(range(0, n, 2))

    expert = Expert(lo, width, expert_up.shape[2])

    def exchange(x):
        return lax.all_to_all(x, "fsdp", split_axis=0, concat_axis=0, tiled=True)

    share = jnp.pad(
        jnp.tile(input_bias, (1, 1, n)).reshape(2, head_width), ((0, EXTRA - 2), (0, 0))
    )
    x0, packed, copies = plain_call(
        first_kernel,
        [
            residual_in,
            row(first_norm_gain),
            row(first_norm_shift),
            document_index,
            jnp.transpose(input_weight, (1, 0, 2)),
            output_weight,
            share,
        ],
        [
            struct((rows + EXTRA, width), bf16),
            struct((shard + EXTRA, 3 * head_width), bf16),
            struct((n * shard, head_width), bf16),
        ],
    )
    x2 = send_tp(x0, 2)
    weights = {0: packed}
    for k in evens[1:]:
        weights[k] = send_fsdp(packed, k)
    weights[1] = send_fsdp(packed, 1)
    arrived = [weights[k] for k in evens[1:] + [1]]
    for k in evens[1:]:
        weights[k ^ 1] = send_fsdp(after(weights[k], arrived), 1)
    x1 = send_tp(after(x0, arrived), 1)
    x3 = send_tp(after(x2, arrived), 1)
    xs = [x0, x1, x2, x3]

    here = jnp.concatenate([place, turn])
    length = TP * rows
    first, end = intervals(here, piece_starts, xs, rows)
    s_own, cot_sent = plain_call(
        functools.partial(slots_kernel, cap),
        [after(expert_index, x1), out_cotangent],
        [struct((8, rows), i32), struct((rows + EXTRA, width), bf16)],
        scalars=[here],
    )

    slotted = struct((n * cap, width), bf16)
    cot_sent_own = plain_call(place_kernel, [out_cotangent, s_own], [slotted])[0]
    queries, keys, values, w_in = plain_call(
        functools.partial(project_kernel, n, shard),
        list(after(tuple(xs), cot_sent_own)) + [weights[k] for k in range(n)],
        [struct((length, head_width), bf16)] * 3 + [struct((width, 3 * head_width), bf16)],
        scalars=[place],
    )
    cot_other = send_tp(after(cot_sent, queries), 1)
    s_other, cot_sent_other = plain_call(
        functools.partial(other_slots_kernel, cap),
        [cot_other],
        [struct((8, rows), i32), slotted],
    )
    halves_sent = expert.halves(*after((expert_up, expert_down), queries))
    halves_other = send_tp(halves_sent, 1)
    near_own = exchange(cot_sent_own)
    w_out0 = exchange(after(copies, near_own))
    down_bias = lax.dynamic_index_in_dim(expert_down_bias, lo, keepdims=True)

    *contexts, totals = attention_fwd(
        after(queries, near_own, halves_sent), keys, values, first, end, turn
    )
    w_late = after(w_out0, totals)
    w_out2, w_out1 = send_tp(w_late, 2), send_tp(w_late, 1)
    ctxs = [contexts[0]] + [send_tp(contexts[r], r) for r in range(1, TP)]
    w_outs = [w_out0, w_out1, w_out2, send_tp(after(w_out2, ctxs[1]), 1)]
    near_other = exchange(after(cot_sent_other, w_out0, totals))
    far_own = send_tp(near_own, 2)
    cot_pieces = [near_own, far_own, near_other, send_tp(near_other, 2)]
    expert.hold(expert_up, expert_up_bias, None, expert_down, halves_other)
    act_backs, cot_sums = [None] * 4, [None] * 2
    act_backs[0], act_backs[1], cot_sums[0] = expert.act_back(*cot_pieces[:2])
    mixed, second, upper, lower = plain_call(
        middle_kernel,
        ctxs
        + w_outs
        + [
            after(residual_in, act_backs[0]),
            row(output_bias),
            row(second_norm_gain),
            row(second_norm_shift),
        ],
        [struct((rows, width), f32), struct((rows, width), bf16)]
        + [struct((rows // 2, width), bf16)] * 2,
    )

    bias_sent = lax.dynamic_index_in_dim(after(expert_up_bias, second), 1 - lo, keepdims=True)
    expert.hold(expert_up, expert_up_bias, send_tp(bias_sent, 1), expert_down, halves_other)
    act_backs[2], act_backs[3], cot_sums[1] = expert.act_back(*cot_pieces[2:])
    cot_sum = added(*cot_sums, dtype=f32)[:1]
    sent_own = plain_call(place_kernel, [second, s_own], [slotted])[0]
    sent_other = plain_call(
        place_halves_kernel, [send_tp(upper, 1), send_tp(lower, 1), s_other], [slotted]
    )[0]
    rows_own = exchange(after(sent_own, near_other))
    rows_other = exchange(after(sent_other, rows_own, cot_pieces[3]))
    pieces = [rows_own, send_tp(rows_own, 2), rows_other]
    acts, pre_backs, x_backs = [], [], []
    for at in range(4):
        act, pre_back, x_back = expert.rows(after(pieces[at], x_backs, act_backs[3]), act_backs[at])
        if at == 0:
            pieces.append(send_tp(after(rows_other, x_back), 2))
        acts.append(act)
        pre_backs.append(pre_back)
        x_backs.append(x_back)

    got_own = send_tp(x_backs[1], 2)
    got_other = send_tp(x_backs[3], 2)
    down_own = expert.down_outer(after(tuple(acts), x_backs[3]), cot_pieces, 0, True)
    back_sent_own = added(x_backs[0], after(got_own, down_own))
    back_home_own = exchange(back_sent_own)
    out_far = expert.out(*after((acts[1], acts[3]), back_sent_own))
    up_away, up_sum_away = expert.up_outer(pieces, after(tuple(pre_backs), out_far), 1, False)
    back_sent_other = added(x_backs[2], after(got_other, up_away))
    back_home_other = exchange(after(back_sent_other, back_home_own))
    out_got = send_tp(after(out_far, got_other), 2)
    late = after(tuple(acts), back_sent_other)
    down_away = expert.down_outer(late, cot_pieces, 1, False)
    out_near = expert.out(*after((acts[0], acts[2]), down_away), part=0.5)
    up_got, down_got = send_tp(up_away, 1), send_tp(down_away, 1)
    sent = send_tp(jnp.concatenate([up_sum_away[:1], cot_sum], axis=0), 1)
    back_own, back_away = collect(
        s_own, s_other, back_home_own, after(back_home_other, out_near, out_got, sent)
    )
    back_other = send_tp(back_away, 1)

    mixed_back, mixed_low, sums2, *ctx_backs = plain_call(
        turn_kernel,
        w_outs + [back_own, back_other, mixed, out_cotangent, row(second_norm_gain)],
        [
            struct((rows, width), f32),
            struct((rows, width), bf16),
            struct((8, width), f32),
        ]
        + [struct((rows, head_width), bf16)] * TP,
    )

    wo_kept, wo_away = plain_call(
        output_weight_kernel,
        ctxs + [mixed_low],
        [struct((2 * width, head_width), bf16)] * 2,
    )

    dos = [ctx_backs[0]] + [send_tp(ctx_backs[r], r) for r in range(1, TP)]
    wo_sum, wo_there = plain_call(
        pair_sum_kernel,
        [wo_kept, send_tp(wo_away, 1)],
        [struct((width, head_width), bf16)] * 2,
    )
    wo_got = send_tp(wo_there, 2)
    out_sent = plain_call(
        functools.partial(out_sum_kernel, cap),
        [out_near, after(out_got, dos[0]), down_bias],
        [struct((2 * n * cap, width), bf16)],
    )[0]
    out_home = exchange(out_sent)
    projected_backs = attention_bwd(
        after(queries, wo_sum, out_sent), keys, values, dos, contexts, totals, first, end, turn
    )
    wo = added(wo_sum, after(wo_got, projected_backs))

    part0, part1, part2, part3, keep, away, vector = plain_call(
        functools.partial(projection_back_kernel, n, shard),
        xs + list(projected_backs) + [after(w_in, up_got, down_got, wo), sums2],
        [struct((rows, width), bf16)] * TP
        + [
            struct((n // 2 * shard, 3 * head_width), bf16),
            struct((n // 2 * shard + EXTRA, 3 * head_width), bf16),
            struct((8, 3 * head_width), f32),
        ],
        scratch=[
            pltpu.VMEM((24, head_width), f32),
            pltpu.VMEM((width, 3 * head_width), f32),
        ],
        scalars=[place],
    )
    got = send_fsdp(away, 1)
    sum2 = added(part2, send_tp(part3, 1))
    got2 = send_tp(sum2, 2)
    sum0 = added(part0, send_tp(part1, 1))
    out_own, out_away = plain_call(
        functools.partial(collect_both_kernel, cap),
        [s_own, s_other, after(out_home, sum2)],
        [struct((rows, width), bf16)] * 2,
    )
    out_other = send_tp(out_away, 1)

    kept, vector, *folds = plain_call(
        fold_kernel,
        [keep, vector, after(got, out_own, sum2)],
        [struct((shard, 3 * head_width), f32), struct((8, 3 * head_width), f32)]
        + [struct((shard + EXTRA, 3 * head_width), bf16)] * (n // 2 - 1),
    )
    wi_kept = (kept, folds)
    wo_home = exchange(after(wo, out_own))
    output_weight_back = plain_call(
        turned_sum_kernel, [wo_home], [struct((head_width, shard), f32)]
    )[0]
    wi_total, vector = plain_call(
        last_fold_kernel,
        [kept, vector] + [send_fsdp(fold, k) for fold, k in zip(folds, evens[1:])],
        [struct((3, shard, head_width), f32), struct((8, 3 * head_width), f32)],
    )

    up_own, up_sum = expert.up_outer(pieces, after(tuple(pre_backs), wi_kept), 0, True, part=0.0)
    up_back, down_back = expert.fill(up_own, down_own, up_got, down_got)
    sent = after(sent, folds)
    up_bias_back = ordered(lo, up_sum[0], sent[0])
    down_bias_back = ordered(lo, cot_sum[0], sent[1])
    block_output = added(mixed, after(out_own, up_back), out_other)

    back_residual = row_call(
        last_kernel,
        [residual_in, row(first_norm_gain), sum0, got2, after(mixed_back, folds)],
        [struct((rows, width), f32)],
        rows,
    )[0]

    tails = vector[5:].reshape(-1)
    bias_sum = tails[5 * head_width : 7 * head_width]
    bias_sum = bias_sum.reshape(2, head_width // HEAD_DIM, n, HEAD_DIM // n)
    input_bias_back = lax.dynamic_index_in_dim(bias_sum, g, axis=2, keepdims=False)
    vector = after(vector, up_back, back_residual)
    turned = [send_tp(vector, r) for r in (1, 2, 3)]
    vectors = plain_call(
        pairs_sum_kernel,
        [after(vector, block_output, output_weight_back)]
        + turned
        + [row(first_norm_gain), row(first_norm_shift)],
        [struct((8, width), f32)],
    )[0]
    return (
        block_output,
        back_residual,
        vectors[0],
        vectors[1],
        jnp.transpose(wi_total, (1, 0, 2)),
        input_bias_back,
        output_weight_back,
        vectors[4],
        vectors[2],
        vectors[3],
        up_back,
        up_bias_back,
        down_back,
        down_bias_back,
    )


def solution(mesh):
    in_specs = (
        P(("fsdp", "tp"), None),
        P(("fsdp", "tp"), None),
        P(("fsdp", "tp"), None),
        P("fsdp", "tp"),
        P("fsdp", None),
        P(),
        P(),
        P("fsdp", None, "tp"),
        P(None, "tp", "fsdp"),
        P("tp", "fsdp"),
        P(),
        P(),
        P(),
        P("fsdp", None, "tp"),
        P("fsdp", "tp"),
        P("fsdp", "tp", None),
        P("fsdp", None),
    )
    out_specs = (
        P(("fsdp", "tp"), None),
        P(("fsdp", "tp"), None),
        P(),
        P(),
        P("fsdp", None, "tp"),
        P(None, "tp", "fsdp"),
        P("tp", "fsdp"),
        P(),
        P(),
        P(),
        P("fsdp", None, "tp"),
        P("fsdp", "tp"),
        P("fsdp", "tp", None),
        P("fsdp", None),
    )
    return jax.shard_map(local, mesh=mesh, in_specs=in_specs, out_specs=out_specs, check_vma=False)
```
